32 devices in a mesh: seq: 4 (over y, x), dp: 8 (over z, core).
Axes of the slice: x: 2, y: 2, z: 4, core: 2. Of those that a mesh axis runs over, the one named last changes fastest.
Arguments:
- tokens: bfloat16 [16, 512, 768], P('dp', 'seq'), may hold values from -6 to 6
- doc_starts: int32 [16, 8], P('dp'), may hold values from 0 to 511, as said below
- decay: float32 [2, 768], replicated, may hold values from -9 to -3.2
- first: float32 [2, 768], replicated, may hold values from -1 to 1
- mix: float32 [2, 5, 768], replicated, may hold values from 0 to 1
- ln_gain: float32 [2, 2, 768], replicated, may hold values from 0.5 to 1.5
- ln_bias: float32 [2, 2, 768], replicated, may hold values from -2 to 2
- att_kvr: bfloat16 [2, 768, 2304], P(None, 'dp'), may hold values from -0.21875 to 0.21875
- att_out: bfloat16 [2, 768, 768], P(None, 'dp'), may hold values from -1.75 to 1.75
- ffn_key: bfloat16 [2, 768, 3072], P(None, 'dp'), may hold values from -0.21875 to 0.21875
- ffn_recept: bfloat16 [2, 768, 768], P(None, 'dp'), may hold values from -0.21875 to 0.21875
- ffn_value: bfloat16 [2, 3072, 768], P(None, 'dp'), may hold values from -0.109375 to 0.109375
- cotangent: bfloat16 [16, 512, 768], P('dp', 'seq'), may hold values from -6 to 6
Outputs:
- output: bfloat16 [16, 512, 768], P('dp', 'seq')
- grad_tokens: bfloat16 [16, 512, 768], P('dp', 'seq')
- grad_decay: float32 [2, 768], P(None, 'dp')
- grad_first: float32 [2, 768], P(None, 'dp')
- grad_mix: float32 [2, 5, 768], P(None, None, 'dp')
- grad_gain: float32 [2, 2, 768], P(None, None, 'dp')
- grad_bias: float32 [2, 2, 768], P(None, None, 'dp')
- grad_kvr: float32 [2, 768, 2304], P(None, 'dp')
- grad_att_out: float32 [2, 768, 768], P(None, 'dp')
- grad_ffn_key: float32 [2, 768, 3072], P(None, 'dp')
- grad_ffn_recept: float32 [2, 768, 768], P(None, 'dp')
- grad_ffn_value: float32 [2, 3072, 768], P(None, 'dp')
The draws below stay inside these ranges and needn't reach their ends.
Inputs may be any that keep to these rules, and one draw needn't show every extreme that they name: `doc_starts`: column 0 of every row is 0 and entries may repeat; in each aligned block of 2 rows at least one row lists only 0, so that its single document covers the whole row.
All inputs are finite; a program needn't handle non-finite values.
Results may differ from the reference program's by a relative error of at most 0.015.
Values may be sent and summed in bfloat16 or wider, within the bound.
A program may use at most 256 MiB of HBM per device.

```python
import math
import jax
import jax.numpy as jnp
from jax import lax

D = 768
FF = 3072
LAYERS = 2
NDOC = 8
ROWS_DEV = 2
LEN = 512
ROWS = 16


def draw_decay(key, part):
    key = jax.random.fold_in(key, 11)
    return jax.random.uniform(key, (LAYERS, D), jnp.float32, -9.0, -3.2)


def draw_doc_starts(key, part):
    key = jax.random.fold_in(key, 23)
    key_spots, key_chosen = jax.random.split(key)
    start_spots = jax.random.randint(key_spots, (ROWS, NDOC - 1), 1, LEN)
    chosen = jax.random.randint(key_chosen, (ROWS // ROWS_DEV,), 0, ROWS_DEV)
    single_row = jnp.arange(ROWS) % ROWS_DEV == jnp.repeat(chosen, ROWS_DEV, total_repeat_length=ROWS)
    start_spots = jnp.where(single_row[:, None], 0, start_spots)
    return jnp.concatenate([jnp.zeros((ROWS, 1), jnp.int32), start_spots], axis=1).astype(jnp.int32)


def levels(own_key, shape, pieces, low, largest):
    gain, own = 1.0, jax.random.fold_in(own_key, 6)
    for position, blocks in pieces:
        steps = jnp.exp(jax.random.uniform(jax.random.fold_in(own, position), (blocks,), jnp.float32, low / len(pieces), largest / len(pieces)))
        gain = gain * jnp.repeat(steps, shape[position] // blocks).reshape([-1 if axis == position else 1 for axis in range(len(shape))])
    return gain


def noise(own_key, dims, deviation, bound, shards=(), kind=jnp.bfloat16):
    level = levels(own_key, dims, shards, -0.22, 0.18) if shards else 1.0
    result = jax.random.normal(own_key, dims, jnp.float32) * deviation * level
    return jnp.minimum(jnp.maximum(result, -bound), bound).astype(kind)


def setup_inputs(seed: int = 0) -> dict:
    streams_of = jax.random.split(jax.random.key(seed), 14)
    return {
        "tokens": noise(streams_of[0], (ROWS, LEN, D), 1.0, 6.0, ((0, 8), (1, 4))),
        "doc_starts": draw_doc_starts(jax.random.fold_in(streams_of[13], 71), 0),
        "decay": draw_decay(jax.random.fold_in(streams_of[13], 71), 0),
        "first": jnp.clip(jax.random.uniform(streams_of[3], (LAYERS, D), jnp.float32, -1.0, 1.0), -1.0, 1.0),
        "mix": jnp.clip(jax.random.uniform(streams_of[4], (LAYERS, 5, D), jnp.float32, 0.0, 1.0), 0.0, 1.0),
        "ln_gain": jnp.clip(1.0 + 0.1 * jax.random.normal(streams_of[5], (LAYERS, 2, D), jnp.float32), 0.5, 1.5),
        "ln_bias": noise(streams_of[6], (LAYERS, 2, D), 0.3, 2.0, (), jnp.float32),
        "att_kvr": noise(streams_of[7], (LAYERS, D, 3 * D), D ** -0.5, 0.21875, ((1, 8),)),
        "att_out": noise(streams_of[8], (LAYERS, D, D), (D // 64) ** -0.5, 1.75, ((1, 8),)),
        "ffn_key": noise(streams_of[9], (LAYERS, D, FF), D ** -0.5, 0.21875, ((1, 8),)),
        "ffn_recept": noise(streams_of[10], (LAYERS, D, D), D ** -0.5, 0.21875, ((1, 8),)),
        "ffn_value": noise(streams_of[11], (LAYERS, FF, D), FF ** -0.5, 0.109375, ((1, 8),)),
        "cotangent": noise(streams_of[12], (ROWS, LEN, D), 1.0, 6.0, ((0, 8), (1, 4))),
    }


@jax.custom_vjp
def low(v):
    return lax.optimization_barrier(v.astype(jnp.bfloat16)).astype(jnp.float32)

@jax.custom_vjp
def low_back(v):
    return v

def low_keep(v):
    return (low(v), None)

def low_pass(kept, grad):
    return (grad,)

def back_keep(v):
    return (v, None)

def back_low(kept, grad):
    return (low(grad),)
low.defvjp(low_keep, low_pass)
low_back.defvjp(back_keep, back_low)
EPSILON = 1e-05

def normalize(stream, gain_row, bias_row):
    center = stream - lax.optimization_barrier(jnp.mean(stream, -1, keepdims=True))
    spread = lax.optimization_barrier(jnp.mean(center * center, -1, keepdims=True))
    return center * lax.rsqrt(spread + EPSILON) * gain_row + bias_row

def shift_later(hidden, starts):
    earlier = jnp.concatenate([jnp.zeros_like(hidden[:, :1]), hidden[:, :-1]], axis=1)
    return earlier * (1.0 - starts)[:, :, None]

def project(inputs, matrix):
    return jnp.einsum('gtd,de->gte', inputs, matrix, precision=lax.Precision.HIGHEST)

def wkv_scan(key_proj, value_proj, decay_row, foremost_line_entry, starts):
    keep_rate = jnp.exp(-jnp.exp(decay_row))

    def step(carry, inputs):
        accrued_dividend_total, accrued_divisor_total = carry
        present_lookup_entry, present_payload_entry, start_now = inputs
        live = (1.0 - start_now)[:, None]
        accrued_dividend_total = accrued_dividend_total * live
        accrued_divisor_total = accrued_divisor_total * live
        key_exp = jnp.exp(present_lookup_entry)
        present_reward_term = jnp.exp(foremost_line_entry + present_lookup_entry)
        recurrence_result = (accrued_dividend_total + present_reward_term * present_payload_entry) / (accrued_divisor_total + present_reward_term)
        return ((keep_rate * accrued_dividend_total + key_exp * present_payload_entry, keep_rate * accrued_divisor_total + key_exp), recurrence_result)
    zeros = jnp.zeros((key_proj.shape[0], key_proj.shape[2]), jnp.float32)
    inputs = (jnp.swapaxes(key_proj, 0, 1), jnp.swapaxes(value_proj, 0, 1), jnp.swapaxes(starts, 0, 1))
    carry_end, results = lax.scan(jax.checkpoint(step), (zeros, zeros), inputs)
    return jnp.swapaxes(results, 0, 1)

def forward(stream, starts, decay, first, mix, ln_gain, ln_bias, att_kvr, att_out, ffn_key, ffn_recept, ffn_value):
    for level in range(LAYERS):
        hidden = normalize(stream, ln_gain[level, 0], ln_bias[level, 0])
        earlier = shift_later(hidden, starts)
        blends = [low(hidden * mix[level, j] + earlier * (1.0 - mix[level, j])) for j in range(3)]
        key_proj = low_back(project(blends[0], att_kvr[level][:, :D]))
        value_proj = low_back(project(blends[1], att_kvr[level][:, D:2 * D]))
        logit = low_back(project(blends[2], att_kvr[level][:, 2 * D:]))
        mixed = wkv_scan(key_proj, value_proj, decay[level], first[level], starts)
        gated = low(jax.nn.sigmoid(logit) * mixed)
        stream = stream + low_back(project(gated, att_out[level]))
        hidden_two = normalize(stream, ln_gain[level, 1], ln_bias[level, 1])
        earlier_two = shift_later(hidden_two, starts)
        key_in = low(hidden_two * mix[level, 3] + earlier_two * (1.0 - mix[level, 3]))
        recept_in = low(hidden_two * mix[level, 4] + earlier_two * (1.0 - mix[level, 4]))
        key_two = low_back(project(key_in, ffn_key[level]))
        squared = low(jnp.square(jax.nn.relu(key_two)))
        value_two = low_back(project(squared, ffn_value[level]))
        recept = low_back(project(recept_in, ffn_recept[level]))
        stream = stream + jax.nn.sigmoid(recept) * value_two
    return stream

def reference(tokens, doc_starts, decay, first, mix, ln_gain, ln_bias, att_kvr, att_out, ffn_key, ffn_recept, ffn_value, cotangent):
    row_total = tokens.shape[0]
    group_size = math.gcd(row_total, 4)
    positions = jnp.arange(LEN, dtype=jnp.int32)
    starts = jnp.any(doc_starts[:, :, None] == positions[None, None, :], axis=1).astype(jnp.float32)
    weights_f32 = tuple((p.astype(jnp.float32) for p in (decay, first, mix, ln_gain, ln_bias, att_kvr, att_out, ffn_key, ffn_recept, ffn_value)))
    grouped = tokens.reshape(row_total // group_size, group_size, LEN, D)
    grouped_cot = cotangent.reshape(row_total // group_size, group_size, LEN, D)
    grouped_starts = starts.reshape(row_total // group_size, group_size, LEN)

    def one_group(totals, inputs):
        stream, start_rows, cot_rows = inputs

        def run(stream_in, *params):
            return forward(stream_in, start_rows, *params)
        recurrence_result, pullback = jax.vjp(run, stream.astype(jnp.float32), *weights_f32)
        grads = pullback(cot_rows.astype(jnp.float32))
        totals = tuple((t + g for t, g in zip(totals, grads[1:])))
        return (totals, (recurrence_result.astype(jnp.bfloat16), grads[0].astype(jnp.bfloat16)))
    init = tuple((jnp.zeros_like(p) for p in weights_f32))
    totals, (outputs, grad_rows) = lax.scan(one_group, init, (grouped, grouped_starts, grouped_cot))
    output = outputs.reshape(row_total, LEN, D)
    grad_tokens = grad_rows.reshape(row_total, LEN, D)
    return (output, grad_tokens, totals[0], totals[1], totals[2], totals[3], totals[4], totals[5], totals[6], totals[7], totals[8], totals[9])
```

```python
import functools
import math

import jax
import jax.numpy as jnp
from jax import lax
from jax.experimental import pallas as pl
from jax.experimental.pallas import tpu as pltpu
from jax.sharding import PartitionSpec as P

EPSILON = 1e-05
MESH = pl.DeviceIdType.MESH

class Place:
    def __init__(self, lines):
        self.lines = lines
        s = lax.axis_index("seq"); d = lax.axis_index("dp")
        self.s, self.d = s, d
        self.c, self.z = lax.rem(d, 2), d // 2
        x, y = lax.rem(s, 2), s // 2
        c = self.c
        self.f = x * (1 - c) + y * c
        self.g = y * (1 - c) + x * c
        flip_x, flip_y = s + 1 - 2 * x, s + 2 - 4 * y
        self.first = (flip_x * (1 - c) + flip_y * c, d)
        self.second = (flip_y * (1 - c) + flip_x * c, d)
        self.partner = (s, d + 1 - 2 * c)
    def line(self, k):
        return lax.rem(self.z + k + self.lines, self.lines)
    def along(self, k):
        return (self.s, self.line(k) * 2 + self.c)

def remote(src, dst, ssem, rsem, dev):
    return pltpu.make_async_remote_copy(src_ref=src, dst_ref=dst, send_sem=ssem, recv_sem=rsem, device_id=dev, device_id_type=MESH)


def gather_ops(pos, w, box, u, send, recv, lines):
    r0, rows, c0, cols = box
    gh = pl.ds(pl.multiple_of(r0 + pos.g * (rows // 2), 16), rows // 2)
    fh = pl.ds(pl.multiple_of(c0 + pos.f * (cols // 2), 128), cols // 2)
    ar, ac = pl.ds(r0, rows), pl.ds(c0, cols)
    stages = [[], [], [], []]
    for k in range(1, lines):
        own, far = (pos.z, pos.c, gh, fh), pos.line(-k)
        stages[0].append(remote(w.at[own], w.at[own], send.at[u, k - 1], recv.at[u, k - 1], pos.along(k)))
        j = lines - 1 + k - 1
        at = (far, pos.c, gh, fh)
        stages[1].append(remote(w.at[at], w.at[at], send.at[u, j], recv.at[u, j], pos.second))
        j = 2 * (lines - 1) + k - 1
        at = (far, pos.c, ar, fh)
        stages[2].append(remote(w.at[at], w.at[at], send.at[u, j], recv.at[u, j], pos.first))
    j = 3 * (lines - 1)
    half = w.at[:, pos.c, ar, ac]
    stages[3].append(remote(half, half, send.at[u, j], recv.at[u, j], pos.partner))
    return stages


def boxes(shapes, pieces):
    units = []
    for i, (rows, cols) in enumerate(shapes):
        if rows % (32 * pieces) == 0:
            step = rows // pieces
            units += [(i, (j, step, 0, cols)) for j in range(0, rows, step)]
        elif cols % (256 * pieces) == 0:
            step = cols // pieces
            units += [(i, (0, rows, j, step)) for j in range(0, cols, step)]
        else:
            units.append((i, (0, rows, 0, cols)))
    return units


def gather_kernel(lines, ahead, units, n, *refs):
    shards, wholes, slots = refs[:n], refs[n : 2 * n], refs[2 * n : 3 * n]
    send, recv, local, out = refs[3 * n :]
    pos = Place(lines)
    barrier = pltpu.get_barrier_semaphore()
    peers = [pos.along(k) for k in range(1, lines)] + [pos.first, pos.second, pos.partner]
    for peer in peers:
        pl.semaphore_signal(barrier, inc=1, device_id=peer, device_id_type=MESH)
    locals_ = [
        pltpu.make_async_copy(shards[i], slots[i].at[pos.z, pos.c], local.at[i]) for i in range(n)
    ]
    for copy in locals_:
        copy.start()
    pl.semaphore_wait(barrier, len(peers))
    for copy in locals_:
        copy.wait()
    stages = [gather_ops(pos, slots[i], box, u, send, recv, lines) for u, (i, box) in enumerate(units)]
    count = len(units)
    for u in range(min(ahead, count)):
        for copy in stages[u][0]:
            copy.start()
    for turn in range(count + 3):
        if turn + ahead < count:
            for copy in stages[turn + ahead][0]:
                copy.start()
        for stage in range(4):
            u = turn - stage
            if 0 <= u < count:
                for i, copy in enumerate(stages[u][stage]):
                    copy.wait_recv()
                    if stage < 2:
                        stages[u][stage + 1][i].start()
                    if stage == 2 and i == lines - 2:
                        stages[u][3][0].start()
    for u in range(count):
        for stage in range(4):
            for copy in stages[u][stage]:
                copy.wait_send()
    outs = [pltpu.make_async_copy(slots[i], wholes[i], out.at[i]) for i in range(n)]
    for copy in outs:
        copy.start()
    for copy in outs:
        copy.wait()


def gather_weights(shards, lines):
    n = len(shards)
    units = boxes([w.shape for w in shards], 3)
    copies = 3 * (lines - 1) + 1
    return pl.pallas_call(
        functools.partial(gather_kernel, lines, 2, units, n),
        out_shape=[jax.ShapeDtypeStruct((lines, 2) + w.shape, w.dtype) for w in shards],
        in_specs=[pl.BlockSpec(memory_space=pl.ANY)] * n,
        out_specs=[pl.BlockSpec(memory_space=pl.ANY)] * n,
        scratch_shapes=[pltpu.VMEM((lines, 2) + w.shape, w.dtype) for w in shards]
        + [
            pltpu.SemaphoreType.DMA((len(units), copies)),
            pltpu.SemaphoreType.DMA((len(units), copies)),
            pltpu.SemaphoreType.DMA((n,)),
            pltpu.SemaphoreType.DMA((n,)),
        ],
        compiler_params=pltpu.CompilerParams(
            collective_id=0, has_side_effects=True, vmem_limit_bytes=60 * 2**20
        ),
    )(*shards)


def kernel_fits(shards):
    pairs = lax.axis_size("dp")
    return (
        lax.axis_size("seq") == 4
        and pairs == 8
        and all(w.shape[0] % 32 == 0 and w.shape[1] % 256 == 0 for w in shards)
    )


def from_behind(block, axis, distance):
    devices = range(lax.axis_size(axis))
    route = [(i - distance, i) for i in devices if i - distance in devices]
    return lax.ppermute(block, axis, route)


def normalize(stream, gain_row, bias_row):
    center = stream - jnp.mean(stream, -1, keepdims=True)
    spread = jnp.mean(center * center, -1, keepdims=True)
    return center * lax.rsqrt(spread + EPSILON) * gain_row + bias_row


def blend(hidden, edge_row, rates, starts):
    earlier = (
        jnp.concatenate([edge_row[:, None, :], hidden[:, :-1, :]], axis=1)
        * (1.0 - starts)[:, :, None]
    )
    return tuple((hidden * rates[j] + earlier * (1.0 - rates[j]) for j in range(rates.shape[0])))


def product(inputs, matrix):
    return jnp.einsum("rcd,de->rce", inputs, matrix, preferred_element_type=jnp.float32)


def product_back(grads, matrix):
    return jnp.einsum("rce,de->rcd", grads, matrix, preferred_element_type=jnp.float32)


def outer_sum(inputs, grads):
    return jnp.einsum("rcd,rce->de", inputs, grads, preferred_element_type=jnp.float32)


def wkv_tokens(key_proj, value_proj, decay_row, foremost_line_entry, numer_in, denom_in, starts):
    rows, length, width = key_proj.shape
    block = math.gcd(length, 64)
    count = length // block
    rate = jnp.exp(decay_row)
    local = jnp.arange(block, dtype=jnp.float32)
    lower = (local[:, None] > local[None, :]).astype(jnp.float32)
    grow = jnp.exp(local[:, None] * rate[None, :])
    shrink = jnp.exp(-(local[:, None] - 1.0) * rate[None, :])
    fade = jnp.exp(-local[:, None] * rate[None, :])
    keep_rate = jnp.exp(-rate)

    def one_block(carry, inputs):
        accrued_dividend_total, accrued_divisor_total = carry
        present_lookup_entry, present_payload_entry, start_now = inputs
        counted = jnp.cumsum(start_now, axis=1)
        same = lower[None] * (counted[:, :, None] == counted[:, None, :]).astype(jnp.float32)
        alive = (counted == 0.0).astype(jnp.float32)[:, :, None]
        key_exp = jnp.exp(present_lookup_entry)
        lifted = grow[None] * key_exp
        numer_sum = jnp.einsum(
            "rji,ric->rjc", same, lifted * present_payload_entry, precision=lax.Precision.HIGHEST
        )
        denom_sum = jnp.einsum("rji,ric->rjc", same, lifted, precision=lax.Precision.HIGHEST)
        present_dividend_term = (
            shrink[None] * numer_sum + fade[None] * alive * accrued_dividend_total[:, None, :]
        )
        present_divisor_term = (
            shrink[None] * denom_sum + fade[None] * alive * accrued_divisor_total[:, None, :]
        )
        present_reward_term = jnp.exp(foremost_line_entry + present_lookup_entry)
        recurrence_result = (
            present_dividend_term + present_reward_term * present_payload_entry
        ) / (present_divisor_term + present_reward_term)
        numer_end = (
            keep_rate * present_dividend_term[:, -1] + key_exp[:, -1] * present_payload_entry[:, -1]
        )
        denom_end = keep_rate * present_divisor_term[:, -1] + key_exp[:, -1]
        return ((numer_end, denom_end), recurrence_result)

    def split(values):
        return jnp.swapaxes(values.reshape((rows, count, block) + values.shape[2:]), 0, 1)

    carry_end, results = lax.scan(
        one_block, (numer_in, denom_in), (split(key_proj), split(value_proj), split(starts))
    )
    return jnp.swapaxes(results, 0, 1).reshape(rows, length, width)


def span_transform(key_proj, value_proj, decay_row, starts):
    length = key_proj.shape[1]
    rate = jnp.exp(decay_row)
    steps = jnp.arange(length, dtype=jnp.float32)
    last_start = jnp.max(steps[None, :] * starts, axis=1)
    after = (steps[None, :] >= last_start[:, None]).astype(jnp.float32)
    weight = jnp.exp(key_proj - (length - 1.0 - steps)[None, :, None] * rate) * after[:, :, None]
    carry_numer = jnp.sum(weight * value_proj, axis=1)
    carry_denom = jnp.sum(weight, axis=1)
    through = jnp.prod(1.0 - starts, axis=1)[:, None] * jnp.exp(-length * rate)[None, :]
    return (through, carry_numer, carry_denom)


def body(
    tokens,
    doc_starts,
    decay,
    first,
    mix,
    ln_gain,
    ln_bias,
    att_kvr,
    att_out,
    ffn_key,
    ffn_recept,
    ffn_value,
    cotangent,
):
    row_total, token_total, width = tokens.shape
    layer_total = decay.shape[0]
    batches = 1
    per_batch = row_total // batches
    positions = lax.axis_index("seq") * token_total + jnp.arange(token_total, dtype=jnp.int32)
    starts_all = jnp.any(doc_starts[:, :, None] == positions[None, None, :], axis=1).astype(
        jnp.float32
    )
    empty = jnp.zeros((per_batch, width), jnp.float32)

    def edge_of(hidden):
        return from_behind(hidden[:, -1, :], "seq", 1)

    def edge_back(grad_edge):
        return from_behind(grad_edge, "seq", -1)

    def chain_forward(through, carry_numer, carry_denom):
        incoming = (empty, empty)
        sent_numer, sent_denom = (carry_numer, carry_denom)
        for relay_turn in range(lax.axis_size("seq") - 1):
            incoming = from_behind((sent_numer, sent_denom), "seq", 1)
            sent_numer = through * incoming[0] + carry_numer
            sent_denom = through * incoming[1] + carry_denom
        return incoming

    def forward_layer(stream, level, matrices, starts):
        w_kvr, w_out, w_fkey, w_frec, w_fval = matrices
        hidden, norm_one = jax.vjp(normalize, stream, ln_gain[level, 0], ln_bias[level, 0])
        edge_row = edge_of(hidden)
        blends, blend_one = jax.vjp(
            lambda h_in, e_in, r_in: blend(h_in, e_in, r_in, starts),
            hidden,
            edge_row,
            mix[level, :3],
        )
        xk_low, xv_low, xr_low = [b.astype(jnp.bfloat16) for b in blends]
        key_proj = product(xk_low, w_kvr[:, :width])
        value_proj = product(xv_low, w_kvr[:, width : 2 * width])
        logit = product(xr_low, w_kvr[:, 2 * width :])
        transform, transform_one = jax.vjp(
            lambda k_in, v_in, d_in: span_transform(k_in, v_in, d_in, starts),
            key_proj,
            value_proj,
            decay[level],
        )
        numer_in, denom_in = chain_forward(transform[0], transform[1], transform[2])
        mixed, tokens_one = jax.vjp(
            lambda k_in, v_in, d_in, f_in, n_in, z_in: wkv_tokens(
                k_in, v_in, d_in, f_in, n_in, z_in, starts
            ),
            key_proj,
            value_proj,
            decay[level],
            first[level],
            numer_in,
            denom_in,
        )
        gated, gate_one = jax.vjp(lambda g_in, m_in: jax.nn.sigmoid(g_in) * m_in, logit, mixed)
        gated_low = gated.astype(jnp.bfloat16)
        middle = stream + product(gated_low, w_out)
        hidden_two, norm_two = jax.vjp(normalize, middle, ln_gain[level, 1], ln_bias[level, 1])
        edge_two = edge_of(hidden_two)
        blends_two, blend_two = jax.vjp(
            lambda h_in, e_in, r_in: blend(h_in, e_in, r_in, starts),
            hidden_two,
            edge_two,
            mix[level, 3:],
        )
        xk2_low, xr2_low = [b.astype(jnp.bfloat16) for b in blends_two]
        key_two = product(xk2_low, w_fkey)
        squared, square_one = jax.vjp(lambda k_in: jnp.square(jax.nn.relu(k_in)), key_two)
        squared_low = squared.astype(jnp.bfloat16)
        value_two = product(squared_low, w_fval)
        recept = product(xr2_low, w_frec)
        branch, branch_one = jax.vjp(
            lambda r_in, v_in: jax.nn.sigmoid(r_in) * v_in, recept, value_two
        )
        record = (
            norm_one,
            blend_one,
            xk_low,
            xv_low,
            xr_low,
            transform[0],
            numer_in,
            denom_in,
            transform_one,
            tokens_one,
            gate_one,
            gated_low,
            norm_two,
            blend_two,
            xk2_low,
            xr2_low,
            square_one,
            squared_low,
            branch_one,
        )
        return (middle + branch, record)

    names = (att_kvr, att_out, ffn_key, ffn_recept, ffn_value)
    shards = [w[level] for level in range(layer_total) for w in names]
    if kernel_fits(shards):
        wholes = gather_weights(shards, lax.axis_size("dp") // 2)
        wholes = [w.reshape(-1, w.shape[-1]) for w in wholes]
    else:
        wholes = [lax.all_gather(w, "dp", axis=0, tiled=True) for w in shards]
    count = len(names)
    gathered = [tuple(wholes[level * count : (level + 1) * count]) for level in range(layer_total)]
    pair_lists = [[] for level in range(layer_total)]
    vector_sums = [None] * layer_total
    outputs = []
    grad_parts = []
    for batch in range(batches):
        low_row = batch * per_batch
        starts = starts_all[low_row : low_row + per_batch]
        stream = tokens[low_row : low_row + per_batch].astype(jnp.float32)
        records = []
        for level in range(layer_total):
            stream, record = forward_layer(stream, level, gathered[level], starts)
            records.append(record)
        outputs.append(stream.astype(jnp.bfloat16))
        gradient = cotangent[low_row : low_row + per_batch].astype(jnp.float32)
        for level in reversed(range(layer_total)):
            backward_w_kvr, backward_w_out, backward_w_fkey, backward_w_frec, backward_w_fval = (
                gathered[level]
            )
            (
                backward_norm_one,
                backward_blend_one,
                backward_xk_low,
                backward_xv_low,
                backward_xr_low,
                backward_through,
                backward_numer_in,
                backward_denom_in,
                backward_transform_one,
                backward_tokens_one,
                backward_gate_one,
                backward_gated_low,
                backward_norm_two,
                backward_blend_two,
                backward_xk2_low,
                backward_xr2_low,
                backward_square_one,
                backward_squared_low,
                backward_branch_one,
            ) = records[level]
            d_recept, d_value_two = backward_branch_one(gradient)
            g_value_two = d_value_two.astype(jnp.bfloat16)
            g_recept = d_recept.astype(jnp.bfloat16)
            (d_key_two,) = backward_square_one(product_back(g_value_two, backward_w_fval))
            g_key_two = d_key_two.astype(jnp.bfloat16)
            d_hidden_two, d_edge_two, d_rates_two = backward_blend_two(
                (product_back(g_key_two, backward_w_fkey), product_back(g_recept, backward_w_frec))
            )
            d_hidden_two = d_hidden_two.at[:, -1, :].add(edge_back(d_edge_two))
            d_middle_norm, d_gain_two, d_bias_two = backward_norm_two(d_hidden_two)
            d_middle = gradient + d_middle_norm
            g_att = d_middle.astype(jnp.bfloat16)
            d_logit, d_mixed = backward_gate_one(product_back(g_att, backward_w_out))
            g_logit = d_logit.astype(jnp.bfloat16)
            (
                d_key_one,
                d_value_one,
                d_decay_one,
                d_first,
                backward_direct_numer,
                backward_direct_denom,
            ) = backward_tokens_one(d_mixed)
            chain_incoming = (empty, empty)
            chain_sent_numer = backward_direct_numer
            chain_sent_denom = backward_direct_denom
            for chain_relay_turn in range(lax.axis_size("seq") - 1):
                chain_incoming = from_behind((chain_sent_numer, chain_sent_denom), "seq", -1)
                chain_sent_numer = backward_through * chain_incoming[0] + backward_direct_numer
                chain_sent_denom = backward_through * chain_incoming[1] + backward_direct_denom
            g_numer_out, g_denom_out = chain_incoming
            d_key_two_part, d_value_two_part, d_decay_two = backward_transform_one(
                (
                    g_numer_out * backward_numer_in + g_denom_out * backward_denom_in,
                    g_numer_out,
                    g_denom_out,
                )
            )
            g_key = (d_key_one + d_key_two_part).astype(jnp.bfloat16)
            g_value = (d_value_one + d_value_two_part).astype(jnp.bfloat16)
            d_blends = (
                product_back(g_key, backward_w_kvr[:, :width]),
                product_back(g_value, backward_w_kvr[:, width : 2 * width]),
                product_back(g_logit, backward_w_kvr[:, 2 * width :]),
            )
            d_hidden, d_edge, d_rates = backward_blend_one(d_blends)
            d_hidden = d_hidden.at[:, -1, :].add(edge_back(d_edge))
            d_stream_norm, d_gain_one, d_bias_one = backward_norm_one(d_hidden)
            pairs = (
                (backward_xk2_low, g_key_two),
                (backward_xr2_low, g_recept),
                (backward_squared_low, g_value_two),
                (backward_xk_low, g_key),
                (backward_xv_low, g_value),
                (backward_xr_low, g_logit),
                (backward_gated_low, g_att),
            )
            columns = (
                [d_decay_one + d_decay_two, d_first]
                + [d_rates[j] for j in range(3)]
                + [d_rates_two[j] for j in range(2)]
                + [d_gain_one, d_gain_two, d_bias_one, d_bias_two]
            )
            backward_vectors = jnp.stack(columns, axis=1)
            gradient, pairs, vectors = (d_middle + d_stream_norm, pairs, backward_vectors)
            pair_lists[level].append(pairs)
            vector_sums[level] = (
                vectors if vector_sums[level] is None else vector_sums[level] + vectors
            )
        grad_parts.append(gradient.astype(jnp.bfloat16))
    results = [None] * layer_total
    for level in reversed(range(layer_total)):
        pair_list = pair_lists[level]

        def summed(index):
            inputs = jnp.concatenate([p[index][0] for p in pair_list], axis=0)
            grads = jnp.concatenate([p[index][1] for p in pair_list], axis=0)
            return outer_sum(inputs, grads)

        ffn_part = (summed(0), summed(1), summed(2))
        finish_grad_kvr = jnp.concatenate([summed(3), summed(4), summed(5)], axis=1)
        totals = (
            lax.psum(
                lax.psum_scatter(ffn_part[0].astype(jnp.bfloat16), "dp", scatter_dimension=0, tiled=True),
                "seq",
            ).astype(jnp.float32),
            lax.psum(
                lax.psum_scatter(ffn_part[1].astype(jnp.bfloat16), "dp", scatter_dimension=0, tiled=True),
                "seq",
            ).astype(jnp.float32),
            lax.psum(
                lax.psum_scatter(ffn_part[2].astype(jnp.bfloat16), "dp", scatter_dimension=0, tiled=True),
                "seq",
            ).astype(jnp.float32),
            lax.psum(
                lax.psum_scatter(finish_grad_kvr.astype(jnp.bfloat16), "dp", scatter_dimension=0, tiled=True),
                "seq",
            ).astype(jnp.float32),
            lax.psum(
                lax.psum_scatter(summed(6).astype(jnp.bfloat16), "dp", scatter_dimension=0, tiled=True),
                "seq",
            ).astype(jnp.float32),
            lax.psum(
                lax.psum_scatter(vector_sums[level], "dp", scatter_dimension=0, tiled=True),
                "seq",
            ).astype(jnp.float32),
        )
        ffn_part = (totals[0], totals[1], totals[2])
        att_part = (totals[3], totals[4], totals[5])
        results[level] = (ffn_part, att_part)
    output = jnp.concatenate(outputs, axis=0)
    grad_tokens = jnp.concatenate(grad_parts, axis=0)
    grad_ffn_key = jnp.stack([r[0][0] for r in results])
    grad_ffn_recept = jnp.stack([r[0][1] for r in results])
    grad_ffn_value = jnp.stack([r[0][2] for r in results])
    grad_kvr = jnp.stack([r[1][0] for r in results])
    grad_att_out = jnp.stack([r[1][1] for r in results])
    vector_rows = jnp.stack([r[1][2] for r in results])
    grad_decay = vector_rows[:, :, 0]
    grad_first = vector_rows[:, :, 1]
    grad_mix = jnp.swapaxes(vector_rows[:, :, 2:7], 1, 2)
    grad_gain = jnp.swapaxes(vector_rows[:, :, 7:9], 1, 2)
    grad_bias = jnp.swapaxes(vector_rows[:, :, 9:11], 1, 2)
    return (
        output,
        grad_tokens,
        grad_decay,
        grad_first,
        grad_mix,
        grad_gain,
        grad_bias,
        grad_kvr,
        grad_att_out,
        grad_ffn_key,
        grad_ffn_recept,
        grad_ffn_value,
    )


def solution(mesh):
    in_specs = (
        P("dp", "seq", None),
        P("dp", None),
        P(),
        P(),
        P(),
        P(),
        P(),
        P(None, "dp", None),
        P(None, "dp", None),
        P(None, "dp", None),
        P(None, "dp", None),
        P(None, "dp", None),
        P("dp", "seq", None),
    )
    out_specs = (
        P("dp", "seq", None),
        P("dp", "seq", None),
        P(None, "dp"),
        P(None, "dp"),
        P(None, None, "dp"),
        P(None, None, "dp"),
        P(None, None, "dp"),
        P(None, "dp", None),
        P(None, "dp", None),
        P(None, "dp", None),
        P(None, "dp", None),
        P(None, "dp", None),
    )
    return jax.shard_map(body, mesh=mesh, in_specs=in_specs, out_specs=out_specs, check_vma=False)
```

```python
import functools
import math

import jax
import jax.numpy as jnp
from jax import lax
from jax.experimental import pallas as pl
from jax.experimental.pallas import tpu as pltpu
from jax.sharding import PartitionSpec as P

EPSILON = 1e-05
MESH = pl.DeviceIdType.MESH
F32, LOW = jnp.float32, jnp.bfloat16


class Place:
    def __init__(self, lines):
        self.lines = lines
        s, d = lax.axis_index("seq"), lax.axis_index("dp")
        self.s, self.d = s, d
        self.c, self.z = lax.rem(d, 2), d // 2
        x, y, c = lax.rem(s, 2), s // 2, self.c
        self.f = x * (1 - c) + y * c
        self.g = y * (1 - c) + x * c
        flip_x, flip_y = s + 1 - 2 * x, s + 2 - 4 * y
        self.first = (flip_x * (1 - c) + flip_y * c, d)
        self.second = (flip_y * (1 - c) + flip_x * c, d)
        self.across = (3 - s, d)
        self.partner = (s, d + 1 - 2 * c)

    def line(self, k):
        return lax.rem(self.z + k + self.lines, self.lines)

    def along(self, k):
        return (self.s, self.line(k) * 2 + self.c)

    def later(self, k):
        return (self.s + k, self.d)


def remote(src, dst, send, recv, device):
    return pltpu.make_async_remote_copy(
        src_ref=src, dst_ref=dst, send_sem=send, recv_sem=recv, device_id=device, device_id_type=MESH
    )


def signal(semaphore, device):
    pl.semaphore_signal(semaphore, inc=1, device_id=device, device_id_type=MESH)


def half(start, size, which, align):
    return pl.ds(pl.multiple_of(start + which * (size // 2), align), size // 2)


class Gather:
    def __init__(self, pos, units, send, recv, ahead):
        self.pos, self.units, self.ahead = pos, units, ahead
        self.turns = 0
        lines = pos.lines
        self.stages = []
        for u, (w, (r0, rows, c0, cols)) in enumerate(units):
            gh, fh = half(r0, rows, pos.g, 16), half(c0, cols, pos.f, 128)
            ar, ac = pl.ds(r0, rows), pl.ds(c0, cols)
            stages = [[], [], [], []]
            for k in range(1, lines):
                far = pos.line(-k)
                own = w.at[pos.z, pos.c, gh, fh]
                stages[0].append(remote(own, own, send.at[u, k - 1], recv.at[u, k - 1], pos.along(k)))
                j = lines - 1 + k - 1
                block = w.at[far, pos.c, gh, fh]
                stages[1].append(remote(block, block, send.at[u, j], recv.at[u, j], pos.second))
                j = 2 * (lines - 1) + k - 1
                block = w.at[far, pos.c, ar, fh]
                stages[2].append(remote(block, block, send.at[u, j], recv.at[u, j], pos.first))
            j = 3 * (lines - 1)
            block = w.at[:, pos.c, ar, ac]
            stages[3].append(remote(block, block, send.at[u, j], recv.at[u, j], pos.partner))
            self.stages.append(stages)

    def begin(self, u):
        if u < len(self.units):
            for copy in self.stages[u][0]:
                copy.start()

    def turn(self):
        turn, count = self.turns, len(self.units)
        self.turns += 1
        self.begin(turn + self.ahead)
        for stage in range(4):
            u = turn - stage
            if 0 <= u < count:
                for i, copy in enumerate(self.stages[u][stage]):
                    copy.wait_recv()
                    if stage < 2:
                        self.stages[u][stage + 1][i].start()
                if stage == 2:
                    self.stages[u][3][0].start()

    def need(self, u):
        while self.turns < u + 4:
            self.turn()

    def finish(self):
        for stages in self.stages:
            for stage in stages:
                for copy in stage:
                    copy.wait_send()


class Reduce:
    def __init__(self, pos, units, shared, send, recv, free, credit, local):
        self.pos, self.units, self.shared = pos, units, shared
        self.send, self.recv, self.free, self.credit, self.local = send, recv, free, credit, local
        self.turns = 0
        self.copies = {}

    def copy(self, u, j, src, dst, device):
        made = remote(src, dst, self.send.at[u, j], self.recv.at[u, j], device)
        self.copies[u, j] = made
        made.start()

    def views(self, u):
        w, landing, out, (r0, rows, c0, cols) = self.units[u]
        pos = self.pos
        v = {
            "ar": pl.ds(r0, rows),
            "ac": pl.ds(c0, cols),
            "gh": half(r0, rows, pos.g, 16),
            "go": half(r0, rows, 1 - pos.g, 16),
            "fh": half(c0, cols, pos.f, 128),
            "fo": half(c0, cols, 1 - pos.f, 128),
            "r0": pl.ds(r0, rows // 2),
            "r1": pl.ds(r0 + rows // 2, rows // 2),
            "c0": pl.ds(c0, cols // 2),
            "c1": pl.ds(c0 + cols // 2, cols // 2),
        }
        return w, landing, out, v

    def emit(self, u):
        w, landing, _, v = self.views(u)
        pos = self.pos
        if u >= self.shared:
            pl.semaphore_wait(self.credit.at[u - self.shared], 1)
        self.copy(
            u, 0, w.at[:, 1 - pos.c, v["ar"], v["ac"]], landing.at[:, v["ar"], v["ac"]], pos.partner
        )

    def pair(self, u):
        w, landing, _, v = self.views(u)
        pos, c = self.pos, self.pos.c
        self.copies[u, 0].wait_recv()

        @pl.loop(0, pos.lines)
        def _(z):
            w[z, c, v["ar"], v["ac"]] += landing[z, v["ar"], v["ac"]]

        if u < self.shared:
            signal(self.credit.at[u], pos.partner)
        self.copies[u, 0].wait_send()
        signal(self.free.at[u, 0], pos.first)
        signal(self.free.at[u, 1], pos.second)
        for k in range(1, pos.lines):
            signal(self.free.at[u, 1 + k], pos.along(-k))
        pl.semaphore_wait(self.free.at[u, 0], 1)
        self.copy(u, 1, w.at[:, c, v["ar"], v["fo"]], w.at[:, 1 - c, v["ar"], v["c0"]], pos.first)

    def one(self, u):
        w, _, _, v = self.views(u)
        pos, c = self.pos, self.pos.c
        self.copies[u, 1].wait_recv()

        @pl.loop(0, pos.lines)
        def _(z):
            w[z, c, v["ar"], v["fh"]] += w[z, 1 - c, v["ar"], v["c0"]]

        pl.semaphore_wait(self.free.at[u, 1], 1)
        self.copy(u, 2, w.at[:, c, v["go"], v["fh"]], w.at[:, 1 - c, v["r0"], v["c1"]], pos.second)

    def two(self, u):
        w, _, _, v = self.views(u)
        pos, c = self.pos, self.pos.c
        self.copies[u, 2].wait_recv()

        @pl.loop(0, pos.lines)
        def _(z):
            w[z, c, v["gh"], v["fh"]] += w[z, 1 - c, v["r0"], v["c1"]]

        for k in range(1, pos.lines):
            pl.semaphore_wait(self.free.at[u, 1 + k], 1)
            self.copy(
                u,
                2 + k,
                w.at[pos.line(k), c, v["gh"], v["fh"]],
                w.at[k - 1, 1 - c, v["r1"], v["c1"]],
                pos.along(k),
            )

    def line(self, u):
        w, _, out, v = self.views(u)
        pos, c, lines = self.pos, self.pos.c, self.pos.lines
        for k in range(1, lines):
            self.copies[u, 2 + k].wait_recv()
        total = w[pos.z, c, v["gh"], v["fh"]].astype(F32)
        for k in range(1, lines):
            total = total + w[k - 1, 1 - c, v["r1"], v["c1"]].astype(F32)
        w[pos.z, c, v["gh"], v["fh"]] = total.astype(LOW)
        mine, there = w.at[pos.z, c, v["gh"], v["fh"]], out.at[v["gh"], v["fh"]]
        pltpu.make_async_copy(mine, there, self.local.at[u]).start()
        for j, device in enumerate((pos.first, pos.second, pos.across)):
            self.copy(u, 2 + lines + j, mine, there, device)

    def turn(self):
        turn = self.turns
        self.turns += 1
        for stage, step in enumerate((self.pair, self.one, self.two, self.line)):
            if 0 <= turn - stage < len(self.units):
                step(turn - stage)

    def finish(self):
        lines = self.pos.lines
        for u in range(len(self.units)):
            w, _, out, v = self.views(u)
            for j in range(1, 5 + lines):
                self.copies[u, j].wait_send()
            for j in range(2 + lines, 5 + lines):
                self.copies[u, j].wait_recv()
            mine, there = w.at[self.pos.z, self.pos.c, v["gh"], v["fh"]], out.at[v["gh"], v["fh"]]
            pltpu.make_async_copy(mine, there, self.local.at[u]).wait()


def dot(a, b):
    return jnp.dot(a, b, preferred_element_type=F32)


def dot_across(a, b):
    return lax.dot_general(a, b, (((1,), (1,)), ((), ())), preferred_element_type=F32)


SAVED = ("x", "x1", "key", "value", "logit", "numer", "denom", "value2", "recept")
SAVED_LOW = ("xk", "xv", "xr", "gated", "xk2", "xr2")
WIDE = 256
BLOCK = 32
VMEM_BYTES = 63 * 2**20


def train_kernel(dims, *refs):
    layers, lines, rows, length, width, hidden = dims
    refs = list(refs)

    def take(count):
        got = refs[:count]
        del refs[:count]
        return got

    matrices = 5
    tokens, doc_starts, decay, first, mix, ln_gain, ln_bias = take(7)
    shards = take(matrices)
    (cotangent,) = take(1)
    output, grad_tokens, vector_out = take(3)
    grad_out = take(matrices)
    names = SAVED + SAVED_LOW + ("squared",)
    store = dict(zip(names, take(len(names))))
    weights = [take(matrices) for _ in range(layers)]
    landing = take(matrices)
    act = dict(zip(names, take(len(names))))
    (live, padded, grad, main, d_one, d_two, d_three, g_low, g_low2, g_low3, g_key2, turned) = take(12)
    vectors, small, vec, v_buf = take(4)
    (g_send, g_recv, own_sem, r_send, r_recv, r_free, r_credit, r_local, save_sem, load_sem, s_send, s_recv, v_send, v_recv) = take(14)
    tokens_total = rows * length
    blocks = length // BLOCK
    chunk = length // 8
    pos = Place(lines)
    s, last = pos.s, 3

    small[...] = jnp.zeros_like(small)
    vectors[...] = jnp.zeros_like(vectors)
    own = []
    for l in range(layers):
        for m in range(matrices):
            own.append(
                pltpu.make_async_copy(
                    shards[m].at[l], weights[l][m].at[pos.z, pos.c], own_sem.at[l, m]
                )
            )
    for copy in own:
        copy.start()
    barrier = pltpu.get_barrier_semaphore()
    peers = [pos.along(k) for k in range(1, lines)]
    peers += [pos.first, pos.second, pos.across, pos.partner]
    for peer in peers:
        signal(barrier, peer)
    pl.semaphore_wait(barrier, len(peers))
    for copy in own:
        copy.wait()

    def pieces(m, count):
        _, _, r, c = weights[0][m].shape
        if m == 4:
            return [(m, (j * (r // count), r // count, 0, c)) for j in range(count)]
        return [(m, (0, r, j * (c // count), c // count)) for j in range(count)]

    layout = pieces(0, 3) + pieces(1, 1) + pieces(2, 3) + pieces(3, 1) + pieces(4, 3)
    per_layer = len(layout)
    gather = Gather(
        pos,
        [(weights[l][m], box) for l in range(layers) for m, box in layout],
        g_send,
        g_recv,
        2,
    )
    for u in range(gather.ahead):
        gather.begin(u)

    kvr = pieces(0, 3)
    back = pieces(4, 3) + pieces(3, 1) + pieces(2, 3) + pieces(1, 1) + [kvr[2], kvr[0], kvr[1]]
    reduce = Reduce(
        pos,
        [
            (weights[l][m], landing[m], grad_out[m].at[l], box)
            for l in reversed(range(layers))
            for m, box in back
        ],
        len(back),
        r_send,
        r_recv,
        r_free,
        r_credit,
        r_local,
    )

    sub = lax.broadcasted_iota(jnp.int32, (8, width), 0)
    place = lax.broadcasted_iota(jnp.int32, (length, 128), 0)
    at_token = (place % 8) * chunk + place // 8 + s * length
    for r in range(rows):
        start = jnp.zeros((length, 128), F32)
        for j in range(doc_starts.shape[1]):
            start = jnp.where(at_token == doc_starts[r, j], 1.0, start)
        live[r] = 1.0 - start
    p_row = lax.broadcasted_iota(jnp.int32, (length, length), 0)
    p_col = lax.broadcasted_iota(jnp.int32, (length, length), 1)
    order = jnp.where((p_row % 8) * chunk + p_row // 8 == p_col, 1.0, 0.0).astype(LOW)
    order_back = jnp.where((p_col % 8) * chunk + p_col // 8 == p_row, 1.0, 0.0).astype(LOW)

    def spread(tile):
        return jnp.concatenate([tile] * (width // 128), axis=-1)

    def span(i):
        return pl.ds(pl.multiple_of(i * BLOCK, BLOCK), BLOCK)

    def span_on(i):
        return pl.ds(pl.multiple_of(i * BLOCK + 8, 8), BLOCK)

    def tile(i):
        return pl.ds(pl.multiple_of(i * 8, 8), 8)

    def flat(ref):
        return ref[...].reshape(tokens_total, ref.shape[-1])

    def wide(j, base=0, size=WIDE):
        return pl.ds(pl.multiple_of(base + j * size, 128), size)

    def fold(block):
        return jnp.sum(block.reshape(rows * BLOCK // 8, 8, width), axis=0)

    def add_vector(level, row, block):
        vectors[level, row] += fold(block)

    def saving(name, level):
        if level == 0:
            pltpu.make_async_copy(act[name], store[name], save_sem.at[names.index(name)]).start()

    def saved(name, level):
        if level == 1:
            pltpu.make_async_copy(act[name], store[name], save_sem.at[names.index(name)]).wait()

    def loading(some):
        for name in some:
            pltpu.make_async_copy(store[name], act[name], load_sem.at[names.index(name)]).start()

    def loaded(name, level):
        if level == 0:
            pltpu.make_async_copy(store[name], act[name], load_sem.at[names.index(name)]).wait()

    def hop(index, device):
        return remote(small.at[0, index], small.at[1, index], s_send.at[index], s_recv.at[index], device)

    edge_count = 4 * layers

    def edge_start(index, step, there):
        @pl.when(there)
        def _():
            hop(index, pos.later(step)).start()

    def edge_wait(index, step, there):
        @pl.when(there)
        def _():
            hop(index, pos.later(step)).wait_recv()

    def edge_sent(index, step, there):
        @pl.when(there)
        def _():
            hop(index, pos.later(step)).wait_send()

    def chain_hop(level, direction, k):
        slot = edge_count + (level * 2 + direction) * 3
        return remote(
            small.at[0, slot],
            small.at[1, slot + k - 1],
            s_send.at[slot + k - 1],
            s_recv.at[slot + k - 1],
            pos.later(k if direction == 0 else -k),
        )

    def chain_do(level, direction, what):
        for k in range(1, 4):
            inside = s + k <= last if direction == 0 else s - k >= 0
            from_inside = s - k >= 0 if direction == 0 else s + k <= last

            @pl.when(from_inside if what == "wait_recv" else inside)
            def _():
                getattr(chain_hop(level, direction, k), what)()

    def chain_total(level, direction, r):
        slot = edge_count + (level * 2 + direction) * 3
        numer = jnp.zeros((1, width), F32)
        denom = jnp.zeros((1, width), F32)
        for k in (3, 2, 1):
            through = small[1, slot + k - 1, 3 * r : 3 * r + 1, :]
            numer = through * numer + small[1, slot + k - 1, 3 * r + 1 : 3 * r + 2, :]
            denom = through * denom + small[1, slot + k - 1, 3 * r + 2 : 3 * r + 3, :]
        return numer, denom

    def centred(x):
        center = x - jnp.mean(x, -1, keepdims=True)
        spread_ = jnp.mean(center * center, -1, keepdims=True)
        scale = lax.rsqrt(spread_ + EPSILON)
        return center * scale, scale

    def normalize_into(x_ref, level, which):
        gain, bias = ln_gain[level, which : which + 1, :], ln_bias[level, which : which + 1, :]

        @pl.loop(0, blocks)
        def _(i):
            n, _ = centred(x_ref[:, span(i), :])
            padded[:, span_on(i), :] = n * gain + bias

    def wrap_in(index):
        for r in range(rows):
            moved = pltpu.roll(padded[r, length : length + 8, :], 1, 0)
            padded[r, 0:8, :] = jnp.where(sub == 0, small[1, index, r : r + 1, :], moved)

    def normalize_shift(x_ref, level, which, outs, rates):
        index = level * 2 + which
        normalize_into(x_ref, level, which)
        for r in range(rows):
            small[0, index, r : r + 1, :] = padded[r, length + 7 : length + 8, :]
        edge_start(index, 1, s < last)
        edge_wait(index, 1, s > 0)
        wrap_in(index)

        @pl.loop(0, blocks)
        def _(i):
            h = padded[:, span_on(i), :]
            before = padded[:, span(i), :] * spread(live[:, span(i), :])
            for out, j in zip(outs, rates):
                rate = mix[level, j : j + 1, :]
                out[:, span(i), :] = (h * rate + before * (1.0 - rate)).astype(LOW)

    def project(x_ref, w, base, count, put):
        @pl.loop(0, count // WIDE)
        def _(j):
            block = w[:, :, :, wide(j, base)].reshape(-1, WIDE)
            put(j, dot(flat(x_ref), block).reshape(rows, length, WIDE))

    def put_in(ref):
        def put(j, block):
            ref[:, :, wide(j)] = block

        return put

    def back_project(g_ref, w, base, count, out_ref):
        size = min(width, count)
        for j in range(count // size):
            block = w[:, :, :, base + j * size : base + (j + 1) * size].reshape(-1, size)
            got = dot_across(g_ref[:, :, j * size : (j + 1) * size].reshape(tokens_total, size), block)
            got = got.reshape(rows, length, width)
            if j == 0:
                out_ref[...] = got
            else:
                out_ref[...] += got

    def outer(x_ref, g_ref, w, base, count, g_base=0):
        turned[...] = flat(x_ref).T

        @pl.loop(0, count // WIDE)
        def _(j):
            g = g_ref[:, :, wide(j, g_base)].reshape(tokens_total, WIDE)
            got = dot(turned[...], g).astype(LOW)
            w[:, :, :, wide(j, base)] = got.reshape(lines, 2, width // (2 * lines), WIDE)

    def keep_rows(level):
        rate = jnp.exp(decay[level : level + 1, :])
        return jnp.broadcast_to(jnp.exp(-rate), (8, width)), rate

    def scan_local(level):
        keep, _ = keep_rows(level)

        def step(i, carry):
            out = []
            for r in range(rows):
                numer, denom, alive = carry[3 * r : 3 * r + 3]
                l128 = live[r, tile(i), :]
                l_now = spread(l128)
                lifted = jnp.exp(act["key"][r, tile(i), :])
                numer = keep * (numer * l_now) + lifted * act["value"][r, tile(i), :]
                denom = keep * (denom * l_now) + lifted
                out += [numer, denom, alive * l128]
            return tuple(out)

        zero = jnp.zeros((8, width), F32)
        carry = lax.fori_loop(0, chunk, step, (zero, zero, jnp.ones((8, 128), F32)) * rows, unroll=2)
        faded = keep
        for _ in range(chunk.bit_length() - 1):
            faded = faded * faded
        slot = edge_count + (level * 2) * 3
        before = []
        for r in range(rows):
            numer, denom, alive = carry[3 * r : 3 * r + 3]
            through = spread(alive) * faded
            vec[level, r] = through
            for shift in (1, 2, 4):
                inside = sub >= shift
                n_b, d_b, t_b = (pltpu.roll(a, shift, 0) for a in (numer, denom, through))
                numer = jnp.where(inside, through * n_b + numer, numer)
                denom = jnp.where(inside, through * d_b + denom, denom)
                through = jnp.where(inside, through * t_b, through)
            for j, a in enumerate((through, numer, denom)):
                small[0, slot, 3 * r + j : 3 * r + j + 1, :] = a[7:8, :]
            at_start = sub == 0
            n_b, d_b, t_b = (pltpu.roll(a, 1, 0) for a in (numer, denom, through))
            before.append(
                (jnp.where(at_start, 0.0, n_b), jnp.where(at_start, 0.0, d_b), jnp.where(at_start, 1.0, t_b))
            )
        chain_do(level, 0, "start")
        return before

    def scan_final(level, before):
        chain_do(level, 0, "wait_recv")
        keep, _ = keep_rows(level)
        bonus = jnp.broadcast_to(jnp.exp(first[level : level + 1, :]), (8, width))
        carry = []
        for r in range(rows):
            n_in, d_in = chain_total(level, 0, r)
            n_b, d_b, t_b = before[r]
            carry += [t_b * n_in + n_b, t_b * d_in + d_b]

        def step(i, carry):
            out = []
            for r in range(rows):
                numer, denom = carry[2 * r : 2 * r + 2]
                l_now = spread(live[r, tile(i), :])
                numer, denom = numer * l_now, denom * l_now
                act["numer"][r, tile(i), :] = numer
                act["denom"][r, tile(i), :] = denom
                value = act["value"][r, tile(i), :]
                lifted = jnp.exp(act["key"][r, tile(i), :])
                now = bonus * lifted
                main[r, tile(i), :] = (numer + now * value) / (denom + now)
                out += [keep * numer + lifted * value, keep * denom + lifted]
            return tuple(out)

        lax.fori_loop(0, chunk, step, tuple(carry), unroll=2)

    for r in range(rows):
        act["x"][r] = dot(order, tokens[r])

    def forward_layer(level):
        w_kvr, w_out, w_fkey, w_frec, w_fval = weights[level]
        base = level * per_layer
        for name in ("xk", "xv", "xr"):
            saved(name, level)
        normalize_shift(act["x"], level, 0, [act["xk"], act["xv"], act["xr"]], (0, 1, 2))
        saving("x", level)
        for j, (low, name) in enumerate((("xk", "key"), ("xv", "value"), ("xr", "logit"))):
            saving(low, level)
            saved(name, level)
            gather.need(base + j)
            project(act[low], w_kvr, j * width, width, put_in(act[name]))
            saving(name, level)
            if j == 1:
                before = scan_local(level)
        saved("numer", level)
        saved("denom", level)
        scan_final(level, before)
        saving("numer", level)
        saving("denom", level)
        saved("gated", level)

        @pl.loop(0, blocks)
        def _(i):
            act["gated"][:, span(i), :] = (
                jax.nn.sigmoid(act["logit"][:, span(i), :]) * main[:, span(i), :]
            ).astype(LOW)

        saving("gated", level)
        gather.need(base + 3)
        saved("x1", level)

        def put_x1(j, block):
            act["x1"][:, :, wide(j)] = act["x"][:, :, wide(j)] + block

        project(act["gated"], w_out, 0, width, put_x1)
        saving("x1", level)
        saved("xk2", level)
        saved("xr2", level)
        normalize_shift(act["x1"], level, 1, [act["xk2"], act["xr2"]], (3, 4))
        saving("xk2", level)
        saving("xr2", level)
        saved("squared", level)
        third = hidden // 3
        for j in range(3):
            gather.need(base + 4 + j)

            def put_squared(i, block, j=j):
                up = jnp.maximum(block, 0.0)
                act["squared"][:, :, wide(i, j * third)] = (up * up).astype(LOW)

            project(act["xk2"], w_fkey, j * third, third, put_squared)
        saving("squared", level)
        gather.need(base + 7)
        saved("recept", level)
        project(act["xr2"], w_frec, 0, width, put_in(act["recept"]))
        saving("recept", level)
        gather.need(base + 10)
        saved("value2", level)
        share = hidden // lines
        for j in range(width // WIDE):
            total = None
            for z in range(lines):
                got = dot(
                    act["squared"][:, :, z * share : (z + 1) * share].reshape(tokens_total, share),
                    w_fval[z, :, :, j * WIDE : (j + 1) * WIDE].reshape(share, WIDE),
                )
                total = got if total is None else total + got
            act["value2"][:, :, j * WIDE : (j + 1) * WIDE] = total.reshape(rows, length, WIDE)
        saving("value2", level)
        saved("x", level + 1)

        @pl.loop(0, blocks)
        def _(i):
            up = jax.nn.sigmoid(act["recept"][:, span(i), :]) * act["value2"][:, span(i), :]
            after = act["x1"][:, span(i), :] + up
            if level + 1 < layers:
                act["x"][:, span(i), :] = after
            else:
                g_low[:, span(i), :] = after.astype(LOW)

    for level in range(layers):
        forward_layer(level)
    for r in range(rows):
        output[r] = dot(order_back, g_low[r]).astype(LOW)
        grad[r] = dot(order, cotangent[r])
    gather.finish()

    def blend_back(level, which, d_refs, rates):
        index = level * 2 + which
        wrap_in(index)

        @pl.loop(0, blocks)
        def _(i):
            l_now = spread(live[:, span(i), :])
            change = padded[:, span_on(i), :] - padded[:, span(i), :] * l_now
            direct, shifted = None, None
            for ref, j in zip(d_refs, rates):
                d = ref[:, span(i), :]
                rate = mix[level, j : j + 1, :]
                add_vector(level, 2 + j, d * change)
                direct = d * rate if direct is None else direct + d * rate
                shifted = d * (1.0 - rate) if shifted is None else shifted + d * (1.0 - rate)
            main[:, span(i), :] = direct
            d_refs[0][:, span(i), :] = shifted * l_now

        back_index = 2 * layers + index
        for r in range(rows):
            small[0, back_index, r : r + 1, :] = d_refs[0][r, 0:1, :]
        edge_start(back_index, -1, s > 0)

    def normalize_back(level, which, x_ref, q_ref, write):
        index = level * 2 + which
        back_index = 2 * layers + index
        edge_wait(back_index, -1, s < last)
        for r in range(rows):
            moved = pltpu.roll(q_ref[r, 0:8, :], 7, 0)
            padded[r, length : length + 8, :] = jnp.where(
                sub == 7, small[1, back_index, r : r + 1, :], moved
            )
            padded[r, 8:length, :] = q_ref[r, 8:length, :]
        gain = ln_gain[level, which : which + 1, :]

        @pl.loop(0, blocks)
        def _(i):
            d_h = main[:, span(i), :] + padded[:, span_on(i), :]
            n, scale = centred(x_ref[:, span(i), :])
            add_vector(level, 7 + which, d_h * n)
            add_vector(level, 9 + which, d_h)
            e = d_h * gain
            inner = e - jnp.mean(e, -1, keepdims=True) - n * jnp.mean(e * n, -1, keepdims=True)
            after = grad[:, span(i), :] + scale * inner
            grad[:, span(i), :] = after
            write(i, after)

    def wkv_terms(r, i, bonus):
        value = act["value"][r, tile(i), :]
        lifted = jnp.exp(act["key"][r, tile(i), :])
        now = bonus * lifted
        numer, denom = act["numer"][r, tile(i), :], act["denom"][r, tile(i), :]
        part = 1.0 / (denom + now)
        result = (numer + now * value) * part
        return value, lifted, now, numer, denom, part, result

    def scan_back_local(level):
        keep, _ = keep_rows(level)
        bonus = jnp.broadcast_to(jnp.exp(first[level : level + 1, :]), (8, width))

        def step(j, carry):
            i = chunk - 1 - j
            out = []
            for r in range(rows):
                h_n, h_d = carry[2 * r : 2 * r + 2]
                value, lifted, now, numer, denom, part, result = wkv_terms(r, i, bonus)
                gate = jax.nn.sigmoid(act["logit"][r, tile(i), :])
                d_gated = main[r, tile(i), :]
                d_wkv = d_gated * gate
                d_two[r, tile(i), :] = d_gated * result * gate * (1.0 - gate)
                main[r, tile(i), :] = d_wkv
                l_now = spread(live[r, tile(i), :])
                a = d_wkv * part
                out += [l_now * (a + keep * h_n), l_now * (keep * h_d - a * result)]
            return tuple(out)

        zero = jnp.zeros((8, width), F32)
        carry = lax.fori_loop(0, chunk, step, (zero, zero) * rows)
        slot = edge_count + (level * 2 + 1) * 3
        after = []
        for r in range(rows):
            h_n, h_d = carry[2 * r : 2 * r + 2]
            through = vec[level, r]
            for shift in (1, 2, 4):
                inside = sub < 8 - shift
                n_a, d_a, t_a = (pltpu.roll(a, 8 - shift, 0) for a in (h_n, h_d, through))
                h_n = jnp.where(inside, through * n_a + h_n, h_n)
                h_d = jnp.where(inside, through * d_a + h_d, h_d)
                through = jnp.where(inside, through * t_a, through)
            for j, a in enumerate((through, h_n, h_d)):
                small[0, slot, 3 * r + j : 3 * r + j + 1, :] = a[0:1, :]
            at_end = sub == 7
            n_a, d_a, t_a = (pltpu.roll(a, 7, 0) for a in (h_n, h_d, through))
            after.append(
                (jnp.where(at_end, 0.0, n_a), jnp.where(at_end, 0.0, d_a), jnp.where(at_end, 1.0, t_a))
            )
        chain_do(level, 1, "start")
        return after

    def scan_back_final(level, after):
        chain_do(level, 1, "wait_recv")
        keep, rate = keep_rows(level)
        bonus = jnp.broadcast_to(jnp.exp(first[level : level + 1, :]), (8, width))
        zero = jnp.zeros((8, width), F32)
        carry = [zero, zero]
        for r in range(rows):
            n_in, d_in = chain_total(level, 1, r)
            n_a, d_a, t_a = after[r]
            carry += [t_a * n_in + n_a, t_a * d_in + d_a]

        def step(j, carry):
            i = chunk - 1 - j
            d_keep, d_first = carry[:2]
            out = []
            for r in range(rows):
                h_n, h_d = carry[2 + 2 * r : 4 + 2 * r]
                value, lifted, now, numer, denom, part, result = wkv_terms(r, i, bonus)
                a = main[r, tile(i), :] * part
                d_now = a * (value - result) * now
                d_keep = d_keep + numer * h_n + denom * h_d
                d_first = d_first + d_now
                d_one[r, tile(i), :] = d_now + lifted * (value * h_n + h_d)
                d_two[r, tile(i), :] = a * now + lifted * h_n
                l_now = spread(live[r, tile(i), :])
                out += [l_now * (a + keep * h_n), l_now * (keep * h_d - a * result)]
            return (d_keep, d_first, *out)

        carry = lax.fori_loop(0, chunk, step, tuple(carry))
        vectors[level, 0] += carry[0] * (-rate * keep)
        vectors[level, 1] += carry[1]

    def to_low(src, dst):
        @pl.loop(0, blocks)
        def _(i):
            dst[:, span(i), :] = src[:, span(i), :].astype(LOW)

    ffn_names = ("value2", "recept", "squared", "xk2", "xr2", "x1")
    att_names = tuple(n for n in names if n not in ffn_names)

    def backward_layer(level):
        w_kvr, w_out, w_fkey, w_frec, w_fval = weights[level]
        base = (layers - 1 - level) * per_layer
        third = hidden // 3
        share = hidden // lines
        loaded("value2", level)
        loaded("recept", level)

        @pl.loop(0, blocks)
        def _(i):
            gate = jax.nn.sigmoid(act["recept"][:, span(i), :])
            g = grad[:, span(i), :]
            g_low[:, span(i), :] = (g * gate).astype(LOW)
            g_low2[:, span(i), :] = (g * act["value2"][:, span(i), :] * gate * (1.0 - gate)).astype(LOW)

        loaded("squared", level)

        @pl.loop(0, lines)
        def _(z):
            got = dot_across(flat(g_low), w_fval[z].reshape(share, width)).reshape(rows, length, share)
            root = jnp.sqrt(act["squared"][:, :, wide(z, 0, share)].astype(F32))
            g_key2[:, :, wide(z, 0, share)] = (got * (2.0 * root)).astype(LOW)

        @pl.loop(0, lines)
        def _(z):
            turned[...] = act["squared"][:, :, wide(z, 0, share)].reshape(tokens_total, share).T
            for j in range(width // WIDE):
                g = g_low[:, :, j * WIDE : (j + 1) * WIDE].reshape(tokens_total, WIDE)
                got = dot(turned[...], g).astype(LOW)
                w_fval[z, :, :, j * WIDE : (j + 1) * WIDE] = got.reshape(2, share // 2, WIDE)

        for j in range(3):
            reduce.emit(base + j)
        loaded("xr2", level)
        back_project(g_low2, w_frec, 0, width, d_two)
        outer(act["xr2"], g_low2, w_frec, 0, width)
        reduce.emit(base + 3)
        reduce.turn()
        back_project(g_key2, w_fkey, 0, hidden, d_one)
        reduce.turn()
        loaded("xk2", level)
        for j in range(3):
            outer(act["xk2"], g_key2, w_fkey, j * third, third, j * third)
            reduce.emit(base + 4 + j)
        loaded("x1", level)
        normalize_into(act["x1"], level, 1)
        blend_back(level, 1, [d_one, d_two], (3, 4))
        reduce.turn()

        def write_att(i, after):
            g_low3[:, span(i), :] = after.astype(LOW)

        normalize_back(level, 1, act["x1"], d_one, write_att)
        if level == 1:
            loading(ffn_names)
        back_project(g_low3, w_out, 0, width, main)
        loaded("gated", level)
        outer(act["gated"], g_low3, w_out, 0, width)
        reduce.emit(base + 7)
        reduce.turn()
        for name in ("logit", "key", "value", "numer", "denom"):
            loaded(name, level)
        after = scan_back_local(level)
        to_low(d_two, g_low)
        reduce.turn()
        loaded("xr", level)
        back_project(g_low, w_kvr, 2 * width, width, d_three)
        outer(act["xr"], g_low, w_kvr, 2 * width, width)
        reduce.emit(base + 8)
        scan_back_final(level, after)
        to_low(d_one, g_low2)
        to_low(d_two, g_low3)
        reduce.turn()
        loaded("xk", level)
        loaded("xv", level)
        back_project(g_low2, w_kvr, 0, width, d_one)
        outer(act["xk"], g_low2, w_kvr, 0, width)
        reduce.emit(base + 9)
        back_project(g_low3, w_kvr, width, width, d_two)
        outer(act["xv"], g_low3, w_kvr, width, width)
        reduce.emit(base + 10)
        reduce.turn()
        loaded("x", level)
        normalize_into(act["x"], level, 0)
        blend_back(level, 0, [d_one, d_two, d_three], (0, 1, 2))

        def write_none(i, after):
            g_low[:, span(i), :] = after.astype(LOW)

        normalize_back(level, 0, act["x"], d_one, write_none)
        if level == 1:
            loading(att_names)

    for level in reversed(range(layers)):
        backward_layer(level)
    for r in range(rows):
        grad_tokens[r] = dot(order_back, g_low[r]).astype(LOW)

    count = vectors.shape[1]

    def vector_hop(j, device):
        source = min(j, 3)
        return remote(v_buf.at[0, source], v_buf.at[1, j], v_send.at[j], v_recv.at[j], device)

    def vector_stage(stage):
        if stage == 0:
            for level in range(layers):
                for row in range(count):
                    j = level * count + row
                    v_buf[0, 0, j : j + 1, :] = jnp.sum(vectors[level, row], axis=0, keepdims=True)
        elif stage < 4:
            vector_hop(stage - 1, pos.partner).wait_recv()
            v_buf[0, stage] = v_buf[0, stage - 1] + v_buf[1, stage - 1]
        if stage < 3:
            vector_hop(stage, (pos.partner, pos.first, pos.second)[stage]).start()
        elif stage == 3:
            for k in range(1, lines):
                vector_hop(2 + k, pos.along(k)).start()
        else:
            total = v_buf[0, 3]
            for k in range(1, lines):
                vector_hop(2 + k, pos.along(k)).wait_recv()
                total = total + v_buf[1, 2 + k]
            vector_out[...] = total

    for stage in range(5):
        vector_stage(stage)
        if reduce.turns < len(reduce.units) + 3:
            reduce.turn()
    while reduce.turns < len(reduce.units) + 3:
        reduce.turn()
    reduce.finish()
    for j, device in enumerate((pos.partner, pos.first, pos.second)):
        vector_hop(j, device).wait_send()
    for k in range(1, lines):
        vector_hop(2 + k, pos.along(k)).wait_send()
    for level in range(layers):
        for which in range(2):
            index = level * 2 + which
            edge_sent(index, 1, s < last)
            edge_sent(2 * layers + index, -1, s > 0)
        for direction in range(2):
            chain_do(level, direction, "wait_send")


def fast_body(
    tokens, doc_starts, decay, first, mix, ln_gain, ln_bias,
    att_kvr, att_out, ffn_key, ffn_recept, ffn_value, cotangent,
):
    rows, length, width = tokens.shape
    layers, hidden = decay.shape[0], ffn_key.shape[2]
    lines = lax.axis_size("dp") // 2
    shards = (att_kvr, att_out, ffn_key, ffn_recept, ffn_value)
    plain, low = (rows, length, width), LOW
    saved = [jax.ShapeDtypeStruct(plain, F32)] * len(SAVED)
    saved += [jax.ShapeDtypeStruct(plain, low)] * len(SAVED_LOW)
    saved += [jax.ShapeDtypeStruct((rows, length, hidden), low)]
    vector_rows = -(-layers * 11 // 8) * 8
    outs = [
        jax.ShapeDtypeStruct(plain, low),
        jax.ShapeDtypeStruct(plain, low),
        jax.ShapeDtypeStruct((vector_rows, width), F32),
    ]
    outs += [jax.ShapeDtypeStruct(w.shape, low) for w in shards]
    outs += saved
    vmem, anywhere = pl.BlockSpec(memory_space=pltpu.VMEM), pl.BlockSpec(memory_space=pl.ANY)
    units = 11 * layers
    hops = 4 * layers + 6 * layers
    dma, plain_f32, plain_low = pltpu.SemaphoreType.DMA, pltpu.VMEM(plain, F32), pltpu.VMEM(plain, low)
    scratch = [pltpu.VMEM((lines, 2) + w.shape[1:], low) for _ in range(layers) for w in shards]
    scratch += [pltpu.VMEM((lines,) + w.shape[1:], low) for w in shards]
    scratch += [pltpu.VMEM(a.shape, a.dtype) for a in saved]
    scratch += [
        pltpu.VMEM((rows, length, 128), F32),
        pltpu.VMEM((rows, length + 8, width), F32),
        plain_f32,
        plain_f32,
        plain_f32,
        plain_f32,
        plain_f32,
        plain_low,
        plain_low,
        plain_low,
        pltpu.VMEM((rows, length, hidden), low),
        pltpu.VMEM((width, rows * length), low),
        pltpu.VMEM((layers, 11, 8, width), F32),
        pltpu.VMEM((2, hops, 8, width), F32),
        pltpu.VMEM((layers, rows, 8, width), F32),
        pltpu.VMEM((2, 6, vector_rows, width), F32),
        dma((units, 3 * lines - 2)),
        dma((units, 3 * lines - 2)),
        dma((layers, len(shards))),
        dma((units, 5 + lines)),
        dma((units, 5 + lines)),
        pltpu.SemaphoreType.REGULAR((units, 1 + lines)),
        pltpu.SemaphoreType.REGULAR((units // layers,)),
        dma((units,)),
        dma((len(saved),)),
        dma((len(saved),)),
        dma((hops,)),
        dma((hops,)),
        dma((6,)),
        dma((6,)),
    ]
    smem = pl.BlockSpec(memory_space=pltpu.SMEM)
    got = pl.pallas_call(
        functools.partial(train_kernel, (layers, lines, rows, length, width, hidden)),
        out_shape=outs,
        in_specs=[vmem, smem] + [vmem] * 5 + [anywhere] * len(shards) + [vmem],
        out_specs=[vmem] * 3 + [anywhere] * (len(outs) - 3),
        scratch_shapes=scratch,
        compiler_params=pltpu.CompilerParams(
            collective_id=0, has_side_effects=True, vmem_limit_bytes=VMEM_BYTES
        ),
    )(tokens, doc_starts, decay, first, mix, ln_gain, ln_bias, *shards, cotangent)
    output, grad_tokens, sums = got[:3]
    share = width // lax.axis_size("dp")
    sums = lax.dynamic_slice_in_dim(sums, lax.axis_index("dp") * share, share, axis=1)
    sums = sums[: layers * 11].reshape(layers, 11, share)
    return (
        output,
        grad_tokens,
        sums[:, 0],
        sums[:, 1],
        sums[:, 2:7],
        sums[:, 7:9],
        sums[:, 9:11],
        *[g.astype(F32) for g in got[3 : 3 + len(shards)]],
    )


def kernel_fits(tokens, decay, ffn_key, shards):
    rows, length, width = tokens.shape
    lines = lax.axis_size("dp") // 2
    return (
        lax.axis_size("seq") == 4
        and lax.axis_size("dp") == 2 * lines
        and lines > 1
        and decay.shape[0] == 2
        and rows == 2
        and length % BLOCK == 0
        and length & (length - 1) == 0
        and width % WIDE == 0
        and ffn_key.shape[2] == width * lines
        and all(w.shape[1] % 32 == 0 and w.shape[2] % WIDE == 0 for w in shards)
    )


def from_behind(block, axis, distance):
    devices = range(lax.axis_size(axis))
    route = [(i - distance, i) for i in devices if i - distance in devices]
    return lax.ppermute(block, axis, route)


def normalize(stream, gain_row, bias_row):
    center = stream - jnp.mean(stream, -1, keepdims=True)
    spread = jnp.mean(center * center, -1, keepdims=True)
    return center * lax.rsqrt(spread + EPSILON) * gain_row + bias_row


def blend(hidden, edge_row, rates, starts):
    earlier = (
        jnp.concatenate([edge_row[:, None, :], hidden[:, :-1, :]], axis=1)
        * (1.0 - starts)[:, :, None]
    )
    return tuple((hidden * rates[j] + earlier * (1.0 - rates[j]) for j in range(rates.shape[0])))


def product(inputs, matrix):
    return jnp.einsum("rcd,de->rce", inputs, matrix, preferred_element_type=jnp.float32)


def product_back(grads, matrix):
    return jnp.einsum("rce,de->rcd", grads, matrix, preferred_element_type=jnp.float32)


def outer_sum(inputs, grads):
    return jnp.einsum("rcd,rce->de", inputs, grads, preferred_element_type=jnp.float32)


def wkv_tokens(key_proj, value_proj, decay_row, foremost_line_entry, numer_in, denom_in, starts):
    rows, length, width = key_proj.shape
    block = math.gcd(length, 64)
    count = length // block
    rate = jnp.exp(decay_row)
    local = jnp.arange(block, dtype=jnp.float32)
    lower = (local[:, None] > local[None, :]).astype(jnp.float32)
    grow = jnp.exp(local[:, None] * rate[None, :])
    shrink = jnp.exp(-(local[:, None] - 1.0) * rate[None, :])
    fade = jnp.exp(-local[:, None] * rate[None, :])
    keep_rate = jnp.exp(-rate)

    def one_block(carry, inputs):
        accrued_dividend_total, accrued_divisor_total = carry
        present_lookup_entry, present_payload_entry, start_now = inputs
        counted = jnp.cumsum(start_now, axis=1)
        same = lower[None] * (counted[:, :, None] == counted[:, None, :]).astype(jnp.float32)
        alive = (counted == 0.0).astype(jnp.float32)[:, :, None]
        key_exp = jnp.exp(present_lookup_entry)
        lifted = grow[None] * key_exp
        numer_sum = jnp.einsum(
            "rji,ric->rjc", same, lifted * present_payload_entry, precision=lax.Precision.HIGHEST
        )
        denom_sum = jnp.einsum("rji,ric->rjc", same, lifted, precision=lax.Precision.HIGHEST)
        present_dividend_term = (
            shrink[None] * numer_sum + fade[None] * alive * accrued_dividend_total[:, None, :]
        )
        present_divisor_term = (
            shrink[None] * denom_sum + fade[None] * alive * accrued_divisor_total[:, None, :]
        )
        present_reward_term = jnp.exp(foremost_line_entry + present_lookup_entry)
        recurrence_result = (
            present_dividend_term + present_reward_term * present_payload_entry
        ) / (present_divisor_term + present_reward_term)
        numer_end = (
            keep_rate * present_dividend_term[:, -1] + key_exp[:, -1] * present_payload_entry[:, -1]
        )
        denom_end = keep_rate * present_divisor_term[:, -1] + key_exp[:, -1]
        return ((numer_end, denom_end), recurrence_result)

    def split(values):
        return jnp.swapaxes(values.reshape((rows, count, block) + values.shape[2:]), 0, 1)

    carry_end, results = lax.scan(
        one_block, (numer_in, denom_in), (split(key_proj), split(value_proj), split(starts))
    )
    return jnp.swapaxes(results, 0, 1).reshape(rows, length, width)


def span_transform(key_proj, value_proj, decay_row, starts):
    length = key_proj.shape[1]
    rate = jnp.exp(decay_row)
    steps = jnp.arange(length, dtype=jnp.float32)
    last_start = jnp.max(steps[None, :] * starts, axis=1)
    after = (steps[None, :] >= last_start[:, None]).astype(jnp.float32)
    weight = jnp.exp(key_proj - (length - 1.0 - steps)[None, :, None] * rate) * after[:, :, None]
    carry_numer = jnp.sum(weight * value_proj, axis=1)
    carry_denom = jnp.sum(weight, axis=1)
    through = jnp.prod(1.0 - starts, axis=1)[:, None] * jnp.exp(-length * rate)[None, :]
    return (through, carry_numer, carry_denom)


def body(
    tokens,
    doc_starts,
    decay,
    first,
    mix,
    ln_gain,
    ln_bias,
    att_kvr,
    att_out,
    ffn_key,
    ffn_recept,
    ffn_value,
    cotangent,
):
    shards = (att_kvr, att_out, ffn_key, ffn_recept, ffn_value)
    if kernel_fits(tokens, decay, ffn_key, shards):
        return fast_body(
            tokens, doc_starts, decay, first, mix, ln_gain, ln_bias, *shards, cotangent
        )
    row_total, token_total, width = tokens.shape
    layer_total = decay.shape[0]
    batches = 2
    per_batch = row_total // batches
    positions = lax.axis_index("seq") * token_total + jnp.arange(token_total, dtype=jnp.int32)
    starts_all = jnp.any(doc_starts[:, :, None] == positions[None, None, :], axis=1).astype(
        jnp.float32
    )
    empty = jnp.zeros((per_batch, width), jnp.float32)

    def edge_of(hidden):
        return from_behind(hidden[:, -1, :], "seq", 1)

    def edge_back(grad_edge):
        return from_behind(grad_edge, "seq", -1)

    def chain_forward(through, carry_numer, carry_denom):
        incoming = (empty, empty)
        sent_numer, sent_denom = (carry_numer, carry_denom)
        for relay_turn in range(lax.axis_size("seq") - 1):
            incoming = from_behind((sent_numer, sent_denom), "seq", 1)
            sent_numer = through * incoming[0] + carry_numer
            sent_denom = through * incoming[1] + carry_denom
        return incoming

    def forward_layer(stream, level, matrices, starts):
        w_kvr, w_out, w_fkey, w_frec, w_fval = matrices
        hidden, norm_one = jax.vjp(normalize, stream, ln_gain[level, 0], ln_bias[level, 0])
        edge_row = edge_of(hidden)
        blends, blend_one = jax.vjp(
            lambda h_in, e_in, r_in: blend(h_in, e_in, r_in, starts),
            hidden,
            edge_row,
            mix[level, :3],
        )
        xk_low, xv_low, xr_low = [b.astype(jnp.bfloat16) for b in blends]
        key_proj = product(xk_low, w_kvr[:, :width])
        value_proj = product(xv_low, w_kvr[:, width : 2 * width])
        logit = product(xr_low, w_kvr[:, 2 * width :])
        transform, transform_one = jax.vjp(
            lambda k_in, v_in, d_in: span_transform(k_in, v_in, d_in, starts),
            key_proj,
            value_proj,
            decay[level],
        )
        numer_in, denom_in = chain_forward(transform[0], transform[1], transform[2])
        mixed, tokens_one = jax.vjp(
            lambda k_in, v_in, d_in, f_in, n_in, z_in: wkv_tokens(
                k_in, v_in, d_in, f_in, n_in, z_in, starts
            ),
            key_proj,
            value_proj,
            decay[level],
            first[level],
            numer_in,
            denom_in,
        )
        gated, gate_one = jax.vjp(lambda g_in, m_in: jax.nn.sigmoid(g_in) * m_in, logit, mixed)
        gated_low = gated.astype(jnp.bfloat16)
        middle = stream + product(gated_low, w_out)
        hidden_two, norm_two = jax.vjp(normalize, middle, ln_gain[level, 1], ln_bias[level, 1])
        edge_two = edge_of(hidden_two)
        blends_two, blend_two = jax.vjp(
            lambda h_in, e_in, r_in: blend(h_in, e_in, r_in, starts),
            hidden_two,
            edge_two,
            mix[level, 3:],
        )
        xk2_low, xr2_low = [b.astype(jnp.bfloat16) for b in blends_two]
        key_two = product(xk2_low, w_fkey)
        squared, square_one = jax.vjp(lambda k_in: jnp.square(jax.nn.relu(k_in)), key_two)
        squared_low = squared.astype(jnp.bfloat16)
        value_two = product(squared_low, w_fval)
        recept = product(xr2_low, w_frec)
        branch, branch_one = jax.vjp(
            lambda r_in, v_in: jax.nn.sigmoid(r_in) * v_in, recept, value_two
        )
        record = (
            norm_one,
            blend_one,
            xk_low,
            xv_low,
            xr_low,
            transform[0],
            numer_in,
            denom_in,
            transform_one,
            tokens_one,
            gate_one,
            gated_low,
            norm_two,
            blend_two,
            xk2_low,
            xr2_low,
            square_one,
            squared_low,
            branch_one,
        )
        return (middle + branch, record)

    gathered = []
    for level in range(layer_total):
        gathered.append(
            (
                lax.all_gather(att_kvr[level], "dp", axis=0, tiled=True),
                lax.all_gather(att_out[level], "dp", axis=0, tiled=True),
                lax.all_gather(ffn_key[level], "dp", axis=0, tiled=True),
                lax.all_gather(ffn_recept[level], "dp", axis=0, tiled=True),
                lax.all_gather(ffn_value[level], "dp", axis=0, tiled=True),
            )
        )
    pair_lists = [[] for level in range(layer_total)]
    vector_sums = [None] * layer_total
    outputs = []
    grad_parts = []
    for batch in range(batches):
        low_row = batch * per_batch
        starts = starts_all[low_row : low_row + per_batch]
        stream = tokens[low_row : low_row + per_batch].astype(jnp.float32)
        records = []
        for level in range(layer_total):
            stream, record = forward_layer(stream, level, gathered[level], starts)
            records.append(record)
        outputs.append(stream.astype(jnp.bfloat16))
        gradient = cotangent[low_row : low_row + per_batch].astype(jnp.float32)
        for level in reversed(range(layer_total)):
            backward_w_kvr, backward_w_out, backward_w_fkey, backward_w_frec, backward_w_fval = (
                gathered[level]
            )
            (
                backward_norm_one,
                backward_blend_one,
                backward_xk_low,
                backward_xv_low,
                backward_xr_low,
                backward_through,
                backward_numer_in,
                backward_denom_in,
                backward_transform_one,
                backward_tokens_one,
                backward_gate_one,
                backward_gated_low,
                backward_norm_two,
                backward_blend_two,
                backward_xk2_low,
                backward_xr2_low,
                backward_square_one,
                backward_squared_low,
                backward_branch_one,
            ) = records[level]
            d_recept, d_value_two = backward_branch_one(gradient)
            g_value_two = d_value_two.astype(jnp.bfloat16)
            g_recept = d_recept.astype(jnp.bfloat16)
            (d_key_two,) = backward_square_one(product_back(g_value_two, backward_w_fval))
            g_key_two = d_key_two.astype(jnp.bfloat16)
            d_hidden_two, d_edge_two, d_rates_two = backward_blend_two(
                (product_back(g_key_two, backward_w_fkey), product_back(g_recept, backward_w_frec))
            )
            d_hidden_two = d_hidden_two.at[:, -1, :].add(edge_back(d_edge_two))
            d_middle_norm, d_gain_two, d_bias_two = backward_norm_two(d_hidden_two)
            d_middle = gradient + d_middle_norm
            g_att = d_middle.astype(jnp.bfloat16)
            d_logit, d_mixed = backward_gate_one(product_back(g_att, backward_w_out))
            g_logit = d_logit.astype(jnp.bfloat16)
            (
                d_key_one,
                d_value_one,
                d_decay_one,
                d_first,
                backward_direct_numer,
                backward_direct_denom,
            ) = backward_tokens_one(d_mixed)
            chain_incoming = (empty, empty)
            chain_sent_numer = backward_direct_numer
            chain_sent_denom = backward_direct_denom
            for chain_relay_turn in range(lax.axis_size("seq") - 1):
                chain_incoming = from_behind((chain_sent_numer, chain_sent_denom), "seq", -1)
                chain_sent_numer = backward_through * chain_incoming[0] + backward_direct_numer
                chain_sent_denom = backward_through * chain_incoming[1] + backward_direct_denom
            g_numer_out, g_denom_out = chain_incoming
            d_key_two_part, d_value_two_part, d_decay_two = backward_transform_one(
                (
                    g_numer_out * backward_numer_in + g_denom_out * backward_denom_in,
                    g_numer_out,
                    g_denom_out,
                )
            )
            g_key = (d_key_one + d_key_two_part).astype(jnp.bfloat16)
            g_value = (d_value_one + d_value_two_part).astype(jnp.bfloat16)
            d_blends = (
                product_back(g_key, backward_w_kvr[:, :width]),
                product_back(g_value, backward_w_kvr[:, width : 2 * width]),
                product_back(g_logit, backward_w_kvr[:, 2 * width :]),
            )
            d_hidden, d_edge, d_rates = backward_blend_one(d_blends)
            d_hidden = d_hidden.at[:, -1, :].add(edge_back(d_edge))
            d_stream_norm, d_gain_one, d_bias_one = backward_norm_one(d_hidden)
            pairs = (
                (backward_xk2_low, g_key_two),
                (backward_xr2_low, g_recept),
                (backward_squared_low, g_value_two),
                (backward_xk_low, g_key),
                (backward_xv_low, g_value),
                (backward_xr_low, g_logit),
                (backward_gated_low, g_att),
            )
            columns = (
                [d_decay_one + d_decay_two, d_first]
                + [d_rates[j] for j in range(3)]
                + [d_rates_two[j] for j in range(2)]
                + [d_gain_one, d_gain_two, d_bias_one, d_bias_two]
            )
            backward_vectors = jnp.stack(columns, axis=1)
            gradient, pairs, vectors = (d_middle + d_stream_norm, pairs, backward_vectors)
            pair_lists[level].append(pairs)
            vector_sums[level] = (
                vectors if vector_sums[level] is None else vector_sums[level] + vectors
            )
        grad_parts.append(gradient.astype(jnp.bfloat16))
    results = [None] * layer_total
    for level in reversed(range(layer_total)):
        pair_list = pair_lists[level]

        def summed(index):
            inputs = jnp.concatenate([p[index][0] for p in pair_list], axis=0)
            grads = jnp.concatenate([p[index][1] for p in pair_list], axis=0)
            return outer_sum(inputs, grads)

        ffn_part = (summed(0), summed(1), summed(2))
        finish_grad_kvr = jnp.concatenate([summed(3), summed(4), summed(5)], axis=1)
        totals = (
            lax.psum(
                lax.psum_scatter(ffn_part[0], "dp", scatter_dimension=0, tiled=True).astype(
                    jnp.bfloat16
                ),
                "seq",
            ).astype(jnp.float32),
            lax.psum(
                lax.psum_scatter(ffn_part[1], "dp", scatter_dimension=0, tiled=True).astype(
                    jnp.bfloat16
                ),
                "seq",
            ).astype(jnp.float32),
            lax.psum(
                lax.psum_scatter(ffn_part[2], "dp", scatter_dimension=0, tiled=True).astype(
                    jnp.bfloat16
                ),
                "seq",
            ).astype(jnp.float32),
            lax.psum(
                lax.psum_scatter(finish_grad_kvr, "dp", scatter_dimension=0, tiled=True).astype(
                    jnp.bfloat16
                ),
                "seq",
            ).astype(jnp.float32),
            lax.psum(
                lax.psum_scatter(summed(6), "dp", scatter_dimension=0, tiled=True).astype(
                    jnp.bfloat16
                ),
                "seq",
            ).astype(jnp.float32),
            lax.psum(
                lax.psum_scatter(vector_sums[level], "dp", scatter_dimension=0, tiled=True).astype(
                    jnp.bfloat16
                ),
                "seq",
            ).astype(jnp.float32),
        )
        ffn_part = (totals[0], totals[1], totals[2])
        att_part = (totals[3], totals[4], totals[5])
        results[level] = (ffn_part, att_part)
    output = jnp.concatenate(outputs, axis=0)
    grad_tokens = jnp.concatenate(grad_parts, axis=0)
    grad_ffn_key = jnp.stack([r[0][0] for r in results])
    grad_ffn_recept = jnp.stack([r[0][1] for r in results])
    grad_ffn_value = jnp.stack([r[0][2] for r in results])
    grad_kvr = jnp.stack([r[1][0] for r in results])
    grad_att_out = jnp.stack([r[1][1] for r in results])
    vector_rows = jnp.stack([r[1][2] for r in results])
    grad_decay = vector_rows[:, :, 0]
    grad_first = vector_rows[:, :, 1]
    grad_mix = jnp.swapaxes(vector_rows[:, :, 2:7], 1, 2)
    grad_gain = jnp.swapaxes(vector_rows[:, :, 7:9], 1, 2)
    grad_bias = jnp.swapaxes(vector_rows[:, :, 9:11], 1, 2)
    return (
        output,
        grad_tokens,
        grad_decay,
        grad_first,
        grad_mix,
        grad_gain,
        grad_bias,
        grad_kvr,
        grad_att_out,
        grad_ffn_key,
        grad_ffn_recept,
        grad_ffn_value,
    )


def solution(mesh):
    in_specs = (
        P("dp", "seq", None),
        P("dp", None),
        P(),
        P(),
        P(),
        P(),
        P(),
        P(None, "dp", None),
        P(None, "dp", None),
        P(None, "dp", None),
        P(None, "dp", None),
        P(None, "dp", None),
        P("dp", "seq", None),
    )
    out_specs = (
        P("dp", "seq", None),
        P("dp", "seq", None),
        P(None, "dp"),
        P(None, "dp"),
        P(None, None, "dp"),
        P(None, None, "dp"),
        P(None, None, "dp"),
        P(None, "dp", None),
        P(None, "dp", None),
        P(None, "dp", None),
        P(None, "dp", None),
        P(None, "dp", None),
    )
    return jax.shard_map(body, mesh=mesh, in_specs=in_specs, out_specs=out_specs, check_vma=False)
```

```python
import functools
import math

import jax
import jax.numpy as jnp
from jax import lax
from jax.experimental import pallas as pl
from jax.experimental.pallas import tpu as pltpu
from jax.sharding import PartitionSpec as P

EPSILON = 1e-05
MESH = pl.DeviceIdType.MESH
F32, LOW = jnp.float32, jnp.bfloat16


class Place:
    def __init__(self, lines):
        self.lines = lines
        s, d = lax.axis_index("seq"), lax.axis_index("dp")
        self.s, self.d = s, d
        self.c, self.z = lax.rem(d, 2), d // 2
        x, y, c = lax.rem(s, 2), s // 2, self.c
        self.f = x * (1 - c) + y * c
        self.g = y * (1 - c) + x * c
        flip_x, flip_y = s + 1 - 2 * x, s + 2 - 4 * y
        self.first = (flip_x * (1 - c) + flip_y * c, d)
        self.second = (flip_y * (1 - c) + flip_x * c, d)
        self.across = (3 - s, d)
        self.partner = (s, d + 1 - 2 * c)

    def line(self, k):
        return lax.rem(self.z + k + self.lines, self.lines)

    def along(self, k):
        return (self.s, self.line(k) * 2 + self.c)

    def later(self, k):
        return (self.s + k, self.d)


def remote(src, dst, send, recv, device):
    return pltpu.make_async_remote_copy(
        src_ref=src, dst_ref=dst, send_sem=send, recv_sem=recv, device_id=device, device_id_type=MESH
    )


def signal(semaphore, device):
    pl.semaphore_signal(semaphore, inc=1, device_id=device, device_id_type=MESH)


def half(start, size, which, align):
    return pl.ds(pl.multiple_of(start + which * (size // 2), align), size // 2)


class Gather:
    def __init__(self, pos, units, send, recv, ahead):
        self.pos, self.units, self.ahead = pos, units, ahead
        self.turns = 0
        lines = pos.lines
        self.stages = []
        for u, (w, (r0, rows, c0, cols)) in enumerate(units):
            gh, fh = half(r0, rows, pos.g, 16), half(c0, cols, pos.f, 128)
            ar, ac = pl.ds(r0, rows), pl.ds(c0, cols)
            stages = [[], [], [], []]
            for k in range(1, lines):
                far = pos.line(-k)
                own = w.at[pos.z, pos.c, gh, fh]
                stages[0].append(remote(own, own, send.at[u, k - 1], recv.at[u, k - 1], pos.along(k)))
                j = lines - 1 + k - 1
                block = w.at[far, pos.c, gh, fh]
                stages[1].append(remote(block, block, send.at[u, j], recv.at[u, j], pos.second))
                j = 2 * (lines - 1) + k - 1
                block = w.at[far, pos.c, ar, fh]
                stages[2].append(remote(block, block, send.at[u, j], recv.at[u, j], pos.first))
            j = 3 * (lines - 1)
            block = w.at[:, pos.c, ar, ac]
            stages[3].append(remote(block, block, send.at[u, j], recv.at[u, j], pos.partner))
            self.stages.append(stages)

    def begin(self, u):
        if u < len(self.units):
            for copy in self.stages[u][0]:
                copy.start()

    def turn(self):
        turn, count = self.turns, len(self.units)
        self.turns += 1
        self.begin(turn + self.ahead)
        for stage in range(4):
            u = turn - stage
            if 0 <= u < count:
                for i, copy in enumerate(self.stages[u][stage]):
                    copy.wait_recv()
                    if stage < 2:
                        self.stages[u][stage + 1][i].start()
                if stage == 2:
                    self.stages[u][3][0].start()

    def need(self, u):
        while self.turns < u + 4:
            self.turn()

    def finish(self):
        for stages in self.stages:
            for stage in stages:
                for copy in stage:
                    copy.wait_send()


class Reduce:
    def __init__(self, pos, units, shared, send, recv, free, credit, local):
        self.pos, self.units, self.shared = pos, units, shared
        self.send, self.recv, self.free, self.credit, self.local = send, recv, free, credit, local
        self.turns = self.emitted = self.cleared = self.paired = self.mark = 0
        self.copies = {}
        self.steps = self.plan()
        self.site = 0

    def copy(self, u, j, src, dst, device):
        made = remote(src, dst, self.send.at[u, j], self.recv.at[u, j], device)
        self.copies[u, j] = made
        made.start()

    def views(self, u):
        w, landing, out, (r0, rows, c0, cols), _ = self.units[u]
        pos = self.pos
        v = {
            "ar": pl.ds(r0, rows),
            "ac": pl.ds(c0, cols),
            "gh": half(r0, rows, pos.g, 16),
            "go": half(r0, rows, 1 - pos.g, 16),
            "fh": half(c0, cols, pos.f, 128),
            "fo": half(c0, cols, 1 - pos.f, 128),
            "r0": pl.ds(r0, rows // 2),
            "r1": pl.ds(r0 + rows // 2, rows // 2),
            "c0": pl.ds(c0, cols // 2),
            "c1": pl.ds(c0 + cols // 2, cols // 2),
        }
        return w, landing, out, v

    def emit(self, u):
        w, landing, _, v = self.views(u)
        pos = self.pos
        assert u == self.emitted
        self.emitted += 1
        if u >= self.shared:
            pl.semaphore_wait(self.credit.at[u - self.shared], 1)
        self.copy(
            u, 0, w.at[:, 1 - pos.c, v["ar"], v["ac"]], landing.at[:, v["ar"], v["ac"]], pos.partner
        )

    def clear(self, u):
        pos = self.pos
        self.copies[u, 0].wait_send()
        signal(self.free.at[u, 0], pos.first)
        signal(self.free.at[u, 1], pos.second)
        for k in range(1, pos.lines):
            signal(self.free.at[u, 1 + k], pos.along(-k))

    def pair(self, u):
        w, landing, _, v = self.views(u)
        pos, c = self.pos, self.pos.c
        self.copies[u, 0].wait_recv()

        @pl.loop(0, pos.lines)
        def _(z):
            w[z, c, v["ar"], v["ac"]] += landing[z, v["ar"], v["ac"]]

        if u < self.shared:
            signal(self.credit.at[u], pos.partner)
        if self.units[u][4]:
            for k in range(1, pos.lines):
                pl.semaphore_wait(self.free.at[u, 1 + k], 1)
                self.copy(
                    u,
                    2 + k,
                    w.at[pos.line(k), c, v["ar"], v["ac"]],
                    w.at[k - 1, 1 - c, v["ar"], v["ac"]],
                    pos.along(k),
                )
            return
        pl.semaphore_wait(self.free.at[u, 0], 1)
        self.copy(u, 1, w.at[:, c, v["ar"], v["fo"]], w.at[:, 1 - c, v["ar"], v["c0"]], pos.first)

    def one(self, u):
        w, _, _, v = self.views(u)
        pos, c = self.pos, self.pos.c
        self.copies[u, 1].wait_recv()

        @pl.loop(0, pos.lines)
        def _(z):
            w[z, c, v["ar"], v["fh"]] += w[z, 1 - c, v["ar"], v["c0"]]

        pl.semaphore_wait(self.free.at[u, 1], 1)
        self.copy(u, 2, w.at[:, c, v["go"], v["fh"]], w.at[:, 1 - c, v["r0"], v["c1"]], pos.second)

    def two(self, u):
        w, _, _, v = self.views(u)
        pos, c = self.pos, self.pos.c
        self.copies[u, 2].wait_recv()

        @pl.loop(0, pos.lines)
        def _(z):
            w[z, c, v["gh"], v["fh"]] += w[z, 1 - c, v["r0"], v["c1"]]

        for k in range(1, pos.lines):
            pl.semaphore_wait(self.free.at[u, 1 + k], 1)
            self.copy(
                u,
                2 + k,
                w.at[pos.line(k), c, v["gh"], v["fh"]],
                w.at[k - 1, 1 - c, v["r1"], v["c1"]],
                pos.along(k),
            )

    def line(self, u):
        w, _, out, v = self.views(u)
        pos, c, lines = self.pos, self.pos.c, self.pos.lines
        for k in range(1, lines):
            self.copies[u, 2 + k].wait_recv()
        total = w[pos.z, c, v["gh"], v["fh"]].astype(F32)
        for k in range(1, lines):
            total = total + w[k - 1, 1 - c, v["r1"], v["c1"]].astype(F32)
        w[pos.z, c, v["gh"], v["fh"]] = total.astype(LOW)
        self.spread(u)

    def spread(self, u):
        w, _, out, v = self.views(u)
        pos, c, lines = self.pos, self.pos.c, self.pos.lines
        mine, there = w.at[pos.z, c, v["gh"], v["fh"]], out.at[v["gh"], v["fh"]]
        pltpu.make_async_copy(mine, there, self.local.at[u]).start()
        for j, device in enumerate((pos.first, pos.second, pos.across)):
            self.copy(u, 2 + lines + j, mine, there, device)

    def line_whole(self, u):
        w, _, _, v = self.views(u)
        pos, c, lines = self.pos, self.pos.c, self.pos.lines
        for k in range(1, lines):
            self.copies[u, 2 + k].wait_recv()
        total = w[pos.z, c, v["ar"], v["ac"]].astype(F32)
        for k in range(1, lines):
            total = total + w[k - 1, 1 - c, v["ar"], v["ac"]].astype(F32)
        w[pos.z, c, v["ar"], v["ac"]] = total.astype(LOW)
        pl.semaphore_wait(self.free.at[u, 0], 1)
        self.copy(
            u,
            1,
            w.at[pos.z, c, v["ar"], v["fo"]],
            w.at[lines - 1, 1 - c, v["ar"], v["c0"]],
            pos.first,
        )

    def one_share(self, u):
        w, _, _, v = self.views(u)
        pos, c, lines = self.pos, self.pos.c, self.pos.lines
        self.copies[u, 1].wait_recv()
        w[pos.z, c, v["ar"], v["fh"]] += w[lines - 1, 1 - c, v["ar"], v["c0"]]
        pl.semaphore_wait(self.free.at[u, 1], 1)
        self.copy(
            u,
            2,
            w.at[pos.z, c, v["go"], v["fh"]],
            w.at[lines - 1, 1 - c, v["r0"], v["c1"]],
            pos.second,
        )

    def two_share(self, u):
        w, _, _, v = self.views(u)
        pos, c, lines = self.pos, self.pos.c, self.pos.lines
        self.copies[u, 2].wait_recv()
        w[pos.z, c, v["gh"], v["fh"]] += w[lines - 1, 1 - c, v["r0"], v["c1"]]
        self.spread(u)

    def clears(self, count):
        while self.cleared < count:
            self.clear(self.cleared)
            self.cleared += 1

    def pairs(self, count):
        self.clears(count)
        while self.paired < count:
            self.pair(self.paired)
            self.paired += 1

    def serve(self, turns):
        self.pairs(min(self.cleared, self.turns + LEAD))
        self.clears(self.mark)
        self.mark = self.emitted
        for _ in range(turns):
            if all(u < self.paired for _, u in self.steps.get(self.turns, ())):
                self.turn()

    def plan(self):
        plan = {}
        for u in reversed(range(len(self.units))):
            whole = self.units[u][4]
            steps = (self.line_whole, self.one_share, self.two_share) if whole else (self.one, self.two, self.line)
            lags = (WHOLE_LAG, LAGS[0], LAGS[1]) if whole else LAGS
            at = u
            for step, lag in zip(steps, lags):
                at += lag
                plan.setdefault(at, []).append((step, u))
        return plan

    def done(self):
        return self.turns > max(self.steps)

    def turn(self):
        if not self.done():
            steps = self.steps.get(self.turns, ())
            self.turns += 1
            self.pairs(max([u + 1 for _, u in steps] + [self.paired]))
            for step, u in steps:
                step(u)

    def finish(self):
        lines = self.pos.lines
        for u in range(len(self.units)):
            w, _, out, v = self.views(u)
            for j in range(1, 5 + lines):
                self.copies[u, j].wait_send()
            for j in range(2 + lines, 5 + lines):
                self.copies[u, j].wait_recv()
            mine, there = w.at[self.pos.z, self.pos.c, v["gh"], v["fh"]], out.at[v["gh"], v["fh"]]
            pltpu.make_async_copy(mine, there, self.local.at[u]).wait()


def dot(a, b):
    return jnp.dot(a, b, preferred_element_type=F32)


def dot_across(a, b):
    return lax.dot_general(a, b, (((1,), (1,)), ((), ())), preferred_element_type=F32)


SAVED = ("x", "x1", "key", "value", "logit", "numer", "denom", "value2", "recept")
SAVED_LOW = ("xk", "xv", "xr", "gated", "xk2", "xr2")
WIDE = 256
BLOCK = 32
LEAD = 12
LINE_FIRST = (2, 5)
LAGS = (3,3,4)
WHOLE_LAG = 7
SITES = (0,)*8+(1,)*24
VMEM_BYTES = 63 * 2**20


def train_kernel(dims, *refs):
    layers, lines, rows, length, width, hidden = dims
    refs = list(refs)

    def take(count):
        got = refs[:count]
        del refs[:count]
        return got

    matrices = 5
    tokens, doc_starts, decay, first, mix, ln_gain, ln_bias = take(7)
    shards = take(matrices)
    (cotangent,) = take(1)
    output, grad_tokens, vector_out = take(3)
    grad_out = take(matrices)
    names = SAVED + SAVED_LOW + ("squared",)
    store = dict(zip(names, take(len(names))))
    weights = [take(matrices) for _ in range(layers)]
    landing = take(matrices)
    act = dict(zip(names, take(len(names))))
    (live, padded, grad, main, d_one, d_two, d_three, g_low, g_low2, g_low3, g_key2, turned) = take(12)
    vectors, small, vec, v_buf = take(4)
    (g_send, g_recv, own_sem, r_send, r_recv, r_free, r_credit, r_local, save_sem, load_sem, s_send, s_recv, v_send, v_recv) = take(14)
    tokens_total = rows * length
    blocks = length // BLOCK
    chunk = length // 8
    pos = Place(lines)
    s, last = pos.s, 3

    small[...] = jnp.zeros_like(small)
    vectors[...] = jnp.zeros_like(vectors)
    own = []
    for l in range(layers):
        for m in range(matrices):
            own.append(
                pltpu.make_async_copy(
                    shards[m].at[l], weights[l][m].at[pos.z, pos.c], own_sem.at[l, m]
                )
            )
    for copy in own:
        copy.start()
    barrier = pltpu.get_barrier_semaphore()
    peers = [pos.along(k) for k in range(1, lines)]
    peers += [pos.first, pos.second, pos.across, pos.partner]
    for peer in peers:
        signal(barrier, peer)
    pl.semaphore_wait(barrier, len(peers))
    for copy in own:
        copy.wait()

    def pieces(m, count):
        _, _, r, c = weights[0][m].shape
        if m == 4:
            return [(m, (j * (r // count), r // count, 0, c)) for j in range(count)]
        return [(m, (0, r, j * (c // count), c // count)) for j in range(count)]

    def columns(m, count):
        _, _, r, c = weights[0][m].shape
        return [(m, (0, r, j * (c // count), c // count)) for j in range(count)]

    layout = pieces(0, 3) + pieces(1, 1) + pieces(2, 3) + pieces(3, 1) + columns(4, 3)
    per_layer = len(layout)
    gather = Gather(
        pos,
        [(weights[l][m], box) for l in range(layers) for m, box in layout],
        g_send,
        g_recv,
        2,
    )
    for u in range(gather.ahead):
        gather.begin(u)

    kvr = pieces(0, 3)
    back = pieces(3, 1) + pieces(4, 3) + pieces(2, 3) + pieces(1, 1) + [kvr[2], kvr[0], kvr[1]]
    line_first = LINE_FIRST
    reduce = Reduce(
        pos,
        [
            (weights[l][m], landing[m], grad_out[m].at[l], box, j in line_first)
            for l in reversed(range(layers))
            for j, (m, box) in enumerate(back)
        ],
        len(back),
        r_send,
        r_recv,
        r_free,
        r_credit,
        r_local,
    )

    sub = lax.broadcasted_iota(jnp.int32, (8, width), 0)
    place = lax.broadcasted_iota(jnp.int32, (length, 128), 0)
    at_token = (place % 8) * chunk + place // 8 + s * length
    for r in range(rows):
        start = jnp.zeros((length, 128), F32)
        for j in range(doc_starts.shape[1]):
            start = jnp.where(at_token == doc_starts[r, j], 1.0, start)
        live[r] = 1.0 - start
    p_row = lax.broadcasted_iota(jnp.int32, (length, length), 0)
    p_col = lax.broadcasted_iota(jnp.int32, (length, length), 1)
    order = jnp.where((p_row % 8) * chunk + p_row // 8 == p_col, 1.0, 0.0).astype(LOW)
    order_back = jnp.where((p_col % 8) * chunk + p_col // 8 == p_row, 1.0, 0.0).astype(LOW)

    def spread(tile):
        return jnp.concatenate([tile] * (width // 128), axis=-1)

    def span(i):
        return pl.ds(pl.multiple_of(i * BLOCK, BLOCK), BLOCK)

    def span_on(i):
        return pl.ds(pl.multiple_of(i * BLOCK + 8, 8), BLOCK)

    def tile(i):
        return pl.ds(pl.multiple_of(i * 8, 8), 8)

    def flat(ref):
        return ref[...].reshape(tokens_total, ref.shape[-1])

    def wide(j, base=0, size=WIDE):
        return pl.ds(pl.multiple_of(base + j * size, 128), size)

    def fold(block):
        return jnp.sum(block.reshape(rows * BLOCK // 8, 8, width), axis=0)

    def add_vector(level, row, block):
        vectors[level, row] += fold(block)

    def saving(name, level):
        if level == 0:
            pltpu.make_async_copy(act[name], store[name], save_sem.at[names.index(name)]).start()

    def saved(name, level):
        if level == 1:
            pltpu.make_async_copy(act[name], store[name], save_sem.at[names.index(name)]).wait()

    def loading(some):
        for name in some:
            pltpu.make_async_copy(store[name], act[name], load_sem.at[names.index(name)]).start()

    def loaded(name, level):
        if level == 0:
            pltpu.make_async_copy(store[name], act[name], load_sem.at[names.index(name)]).wait()

    def hop(index, device):
        return remote(small.at[0, index], small.at[1, index], s_send.at[index], s_recv.at[index], device)

    edge_count = 4 * layers

    def edge_start(index, step, there):
        @pl.when(there)
        def _():
            hop(index, pos.later(step)).start()

    def edge_wait(index, step, there):
        @pl.when(there)
        def _():
            hop(index, pos.later(step)).wait_recv()

    def edge_sent(index, step, there):
        @pl.when(there)
        def _():
            hop(index, pos.later(step)).wait_send()

    def chain_hop(level, direction, k):
        slot = edge_count + (level * 2 + direction) * 3
        return remote(
            small.at[0, slot],
            small.at[1, slot + k - 1],
            s_send.at[slot + k - 1],
            s_recv.at[slot + k - 1],
            pos.later(k if direction == 0 else -k),
        )

    def chain_do(level, direction, what):
        for k in range(1, 4):
            inside = s + k <= last if direction == 0 else s - k >= 0
            from_inside = s - k >= 0 if direction == 0 else s + k <= last

            @pl.when(from_inside if what == "wait_recv" else inside)
            def _():
                getattr(chain_hop(level, direction, k), what)()

    def chain_total(level, direction, r):
        slot = edge_count + (level * 2 + direction) * 3
        numer = jnp.zeros((1, width), F32)
        denom = jnp.zeros((1, width), F32)
        for k in (3, 2, 1):
            through = small[1, slot + k - 1, 3 * r : 3 * r + 1, :]
            numer = through * numer + small[1, slot + k - 1, 3 * r + 1 : 3 * r + 2, :]
            denom = through * denom + small[1, slot + k - 1, 3 * r + 2 : 3 * r + 3, :]
        return numer, denom

    def centred(x):
        center = x - jnp.mean(x, -1, keepdims=True)
        spread_ = jnp.mean(center * center, -1, keepdims=True)
        scale = lax.rsqrt(spread_ + EPSILON)
        return center * scale, scale

    def normalize_into(x_ref, level, which):
        gain, bias = ln_gain[level, which : which + 1, :], ln_bias[level, which : which + 1, :]

        @pl.loop(0, blocks)
        def _(i):
            n, _ = centred(x_ref[:, span(i), :])
            padded[:, span_on(i), :] = n * gain + bias

    def wrap_in(index):
        for r in range(rows):
            moved = pltpu.roll(padded[r, length : length + 8, :], 1, 0)
            padded[r, 0:8, :] = jnp.where(sub == 0, small[1, index, r : r + 1, :], moved)

    def normalize_shift(x_ref, level, which, outs, rates):
        index = level * 2 + which
        normalize_into(x_ref, level, which)
        for r in range(rows):
            small[0, index, r : r + 1, :] = padded[r, length + 7 : length + 8, :]
        edge_start(index, 1, s < last)
        edge_wait(index, 1, s > 0)
        wrap_in(index)

        @pl.loop(0, blocks)
        def _(i):
            h = padded[:, span_on(i), :]
            before = padded[:, span(i), :] * spread(live[:, span(i), :])
            for out, j in zip(outs, rates):
                rate = mix[j, level : level + 1, :]
                out[:, span(i), :] = (h * rate + before * (1.0 - rate)).astype(LOW)

    def project(x_ref, w, base, count, put):
        @pl.loop(0, count // WIDE)
        def _(j):
            block = w[:, :, :, wide(j, base)].reshape(-1, WIDE)
            put(j, dot(flat(x_ref), block).reshape(rows, length, WIDE))

    def put_in(ref):
        def put(j, block):
            ref[:, :, wide(j)] = block

        return put

    def back_project(g_ref, w, base, count, out_ref):
        size = min(width, count)
        for j in range(count // size):
            block = w[:, :, :, base + j * size : base + (j + 1) * size].reshape(-1, size)
            got = dot_across(g_ref[:, :, j * size : (j + 1) * size].reshape(tokens_total, size), block)
            got = got.reshape(rows, length, width)
            if j == 0:
                out_ref[...] = got
            else:
                out_ref[...] += got

    def outer(x_ref, g_ref, w, base, count, g_base=0):
        turned[...] = flat(x_ref).T

        @pl.loop(0, count // WIDE)
        def _(j):
            g = g_ref[:, :, wide(j, g_base)].reshape(tokens_total, WIDE)
            got = dot(turned[...], g).astype(LOW)
            w[:, :, :, wide(j, base)] = got.reshape(lines, 2, width // (2 * lines), WIDE)

    def keep_rows(level):
        rate = jnp.exp(decay[level : level + 1, :])
        return jnp.broadcast_to(jnp.exp(-rate), (8, width)), rate

    def scan_local(level):
        keep, _ = keep_rows(level)

        def step(i, carry):
            out = []
            for r in range(rows):
                numer, denom, alive = carry[3 * r : 3 * r + 3]
                l128 = live[r, tile(i), :]
                l_now = spread(l128)
                lifted = jnp.exp(act["key"][r, tile(i), :])
                numer = keep * (numer * l_now) + lifted * act["value"][r, tile(i), :]
                denom = keep * (denom * l_now) + lifted
                out += [numer, denom, alive * l128]
            return tuple(out)

        zero = jnp.zeros((8, width), F32)
        carry = lax.fori_loop(0, chunk, step, (zero, zero, jnp.ones((8, 128), F32)) * rows, unroll=2)
        faded = keep
        for _ in range(chunk.bit_length() - 1):
            faded = faded * faded
        slot = edge_count + (level * 2) * 3
        before = []
        for r in range(rows):
            numer, denom, alive = carry[3 * r : 3 * r + 3]
            through = spread(alive) * faded
            vec[level, r] = through
            for shift in (1, 2, 4):
                inside = sub >= shift
                n_b, d_b, t_b = (pltpu.roll(a, shift, 0) for a in (numer, denom, through))
                numer = jnp.where(inside, through * n_b + numer, numer)
                denom = jnp.where(inside, through * d_b + denom, denom)
                through = jnp.where(inside, through * t_b, through)
            for j, a in enumerate((through, numer, denom)):
                small[0, slot, 3 * r + j : 3 * r + j + 1, :] = a[7:8, :]
            at_start = sub == 0
            n_b, d_b, t_b = (pltpu.roll(a, 1, 0) for a in (numer, denom, through))
            before.append(
                (jnp.where(at_start, 0.0, n_b), jnp.where(at_start, 0.0, d_b), jnp.where(at_start, 1.0, t_b))
            )
        chain_do(level, 0, "start")
        return before

    def scan_final(level, before):
        chain_do(level, 0, "wait_recv")
        keep, _ = keep_rows(level)
        bonus = jnp.broadcast_to(jnp.exp(first[level : level + 1, :]), (8, width))
        carry = []
        for r in range(rows):
            n_in, d_in = chain_total(level, 0, r)
            n_b, d_b, t_b = before[r]
            carry += [t_b * n_in + n_b, t_b * d_in + d_b]

        def step(i, carry):
            out = []
            for r in range(rows):
                numer, denom = carry[2 * r : 2 * r + 2]
                l_now = spread(live[r, tile(i), :])
                numer, denom = numer * l_now, denom * l_now
                act["numer"][r, tile(i), :] = numer
                act["denom"][r, tile(i), :] = denom
                value = act["value"][r, tile(i), :]
                lifted = jnp.exp(act["key"][r, tile(i), :])
                now = bonus * lifted
                main[r, tile(i), :] = (numer + now * value) / (denom + now)
                out += [keep * numer + lifted * value, keep * denom + lifted]
            return tuple(out)

        lax.fori_loop(0, chunk, step, tuple(carry), unroll=2)

    for r in range(rows):
        act["x"][r] = dot(order, tokens[r])

    def forward_layer(level):
        w_kvr, w_out, w_fkey, w_frec, w_fval = weights[level]
        base = level * per_layer
        for name in ("xk", "xv", "xr"):
            saved(name, level)
        normalize_shift(act["x"], level, 0, [act["xk"], act["xv"], act["xr"]], (0, 1, 2))
        saving("x", level)
        for j, (low, name) in enumerate((("xk", "key"), ("xv", "value"), ("xr", "logit"))):
            saving(low, level)
            saved(name, level)
            gather.need(base + j)
            project(act[low], w_kvr, j * width, width, put_in(act[name]))
            saving(name, level)
            if j == 1:
                before = scan_local(level)
        saved("numer", level)
        saved("denom", level)
        scan_final(level, before)
        saving("numer", level)
        saving("denom", level)
        saved("gated", level)

        @pl.loop(0, blocks)
        def _(i):
            act["gated"][:, span(i), :] = (
                jax.nn.sigmoid(act["logit"][:, span(i), :]) * main[:, span(i), :]
            ).astype(LOW)

        saving("gated", level)
        gather.need(base + 3)
        saved("x1", level)

        def put_x1(j, block):
            act["x1"][:, :, wide(j)] = act["x"][:, :, wide(j)] + block

        project(act["gated"], w_out, 0, width, put_x1)
        saving("x1", level)
        saved("xk2", level)
        saved("xr2", level)
        normalize_shift(act["x1"], level, 1, [act["xk2"], act["xr2"]], (3, 4))
        saving("xk2", level)
        saving("xr2", level)
        saved("squared", level)
        third = hidden // 3
        for j in range(3):
            gather.need(base + 4 + j)

            def put_squared(i, block, j=j):
                up = jnp.maximum(block, 0.0)
                act["squared"][:, :, wide(i, j * third)] = (up * up).astype(LOW)

            project(act["xk2"], w_fkey, j * third, third, put_squared)
        saving("squared", level)
        gather.need(base + 7)
        saved("recept", level)
        project(act["xr2"], w_frec, 0, width, put_in(act["recept"]))
        saving("recept", level)
        saved("value2", level)
        share = hidden // lines
        for j in range(width // WIDE):
            gather.need(base + 8 + j)
            total = None
            for z in range(lines):
                got = dot(
                    act["squared"][:, :, z * share : (z + 1) * share].reshape(tokens_total, share),
                    w_fval[z, :, :, j * WIDE : (j + 1) * WIDE].reshape(share, WIDE),
                )
                total = got if total is None else total + got
            act["value2"][:, :, j * WIDE : (j + 1) * WIDE] = total.reshape(rows, length, WIDE)
        saving("value2", level)
        saved("x", level + 1)

        @pl.loop(0, blocks)
        def _(i):
            up = jax.nn.sigmoid(act["recept"][:, span(i), :]) * act["value2"][:, span(i), :]
            after = act["x1"][:, span(i), :] + up
            if level + 1 < layers:
                act["x"][:, span(i), :] = after
            else:
                g_low[:, span(i), :] = after.astype(LOW)

    for level in range(layers):
        forward_layer(level)
    for r in range(rows):
        output[r] = dot(order_back, g_low[r]).astype(LOW)
        grad[r] = dot(order, cotangent[r])
    gather.finish()

    def blend_back(level, which, d_refs, rates):
        index = level * 2 + which
        wrap_in(index)

        @pl.loop(0, blocks)
        def _(i):
            l_now = spread(live[:, span(i), :])
            change = padded[:, span_on(i), :] - padded[:, span(i), :] * l_now
            direct, shifted = None, None
            for ref, j in zip(d_refs, rates):
                d = ref[:, span(i), :]
                rate = mix[j, level : level + 1, :]
                add_vector(level, 2 + j, d * change)
                direct = d * rate if direct is None else direct + d * rate
                shifted = d * (1.0 - rate) if shifted is None else shifted + d * (1.0 - rate)
            main[:, span(i), :] = direct
            d_refs[0][:, span(i), :] = shifted * l_now

        back_index = 2 * layers + index
        for r in range(rows):
            small[0, back_index, r : r + 1, :] = d_refs[0][r, 0:1, :]
        edge_start(back_index, -1, s > 0)

    def normalize_back(level, which, x_ref, q_ref, write):
        index = level * 2 + which
        back_index = 2 * layers + index
        edge_wait(back_index, -1, s < last)
        for r in range(rows):
            moved = pltpu.roll(q_ref[r, 0:8, :], 7, 0)
            padded[r, length : length + 8, :] = jnp.where(
                sub == 7, small[1, back_index, r : r + 1, :], moved
            )
            padded[r, 8:length, :] = q_ref[r, 8:length, :]
        gain = ln_gain[level, which : which + 1, :]

        @pl.loop(0, blocks)
        def _(i):
            d_h = main[:, span(i), :] + padded[:, span_on(i), :]
            n, scale = centred(x_ref[:, span(i), :])
            add_vector(level, 7 + which, d_h * n)
            add_vector(level, 9 + which, d_h)
            e = d_h * gain
            inner = e - jnp.mean(e, -1, keepdims=True) - n * jnp.mean(e * n, -1, keepdims=True)
            after = grad[:, span(i), :] + scale * inner
            grad[:, span(i), :] = after
            write(i, after)

    def wkv_terms(r, i, bonus):
        value = act["value"][r, tile(i), :]
        lifted = jnp.exp(act["key"][r, tile(i), :])
        now = bonus * lifted
        numer, denom = act["numer"][r, tile(i), :], act["denom"][r, tile(i), :]
        part = 1.0 / (denom + now)
        result = (numer + now * value) * part
        return value, lifted, now, numer, denom, part, result

    def scan_back_local(level):
        keep, _ = keep_rows(level)
        bonus = jnp.broadcast_to(jnp.exp(first[level : level + 1, :]), (8, width))

        def step(j, carry):
            i = chunk - 1 - j
            out = []
            for r in range(rows):
                h_n, h_d = carry[2 * r : 2 * r + 2]
                value, lifted, now, numer, denom, part, result = wkv_terms(r, i, bonus)
                gate = jax.nn.sigmoid(act["logit"][r, tile(i), :])
                d_gated = main[r, tile(i), :]
                d_wkv = d_gated * gate
                d_two[r, tile(i), :] = d_gated * result * gate * (1.0 - gate)
                main[r, tile(i), :] = d_wkv
                l_now = spread(live[r, tile(i), :])
                a = d_wkv * part
                out += [l_now * (a + keep * h_n), l_now * (keep * h_d - a * result)]
            return tuple(out)

        zero = jnp.zeros((8, width), F32)
        carry = lax.fori_loop(0, chunk, step, (zero, zero) * rows)
        slot = edge_count + (level * 2 + 1) * 3
        after = []
        for r in range(rows):
            h_n, h_d = carry[2 * r : 2 * r + 2]
            through = vec[level, r]
            for shift in (1, 2, 4):
                inside = sub < 8 - shift
                n_a, d_a, t_a = (pltpu.roll(a, 8 - shift, 0) for a in (h_n, h_d, through))
                h_n = jnp.where(inside, through * n_a + h_n, h_n)
                h_d = jnp.where(inside, through * d_a + h_d, h_d)
                through = jnp.where(inside, through * t_a, through)
            for j, a in enumerate((through, h_n, h_d)):
                small[0, slot, 3 * r + j : 3 * r + j + 1, :] = a[0:1, :]
            at_end = sub == 7
            n_a, d_a, t_a = (pltpu.roll(a, 7, 0) for a in (h_n, h_d, through))
            after.append(
                (jnp.where(at_end, 0.0, n_a), jnp.where(at_end, 0.0, d_a), jnp.where(at_end, 1.0, t_a))
            )
        chain_do(level, 1, "start")
        return after

    def scan_back_final(level, after):
        chain_do(level, 1, "wait_recv")
        keep, rate = keep_rows(level)
        bonus = jnp.broadcast_to(jnp.exp(first[level : level + 1, :]), (8, width))
        zero = jnp.zeros((8, width), F32)
        carry = [zero, zero]
        for r in range(rows):
            n_in, d_in = chain_total(level, 1, r)
            n_a, d_a, t_a = after[r]
            carry += [t_a * n_in + n_a, t_a * d_in + d_a]

        def step(j, carry):
            i = chunk - 1 - j
            d_keep, d_first = carry[:2]
            out = []
            for r in range(rows):
                h_n, h_d = carry[2 + 2 * r : 4 + 2 * r]
                value, lifted, now, numer, denom, part, result = wkv_terms(r, i, bonus)
                a = main[r, tile(i), :] * part
                d_now = a * (value - result) * now
                d_keep = d_keep + numer * h_n + denom * h_d
                d_first = d_first + d_now
                d_one[r, tile(i), :] = d_now + lifted * (value * h_n + h_d)
                d_two[r, tile(i), :] = a * now + lifted * h_n
                l_now = spread(live[r, tile(i), :])
                out += [l_now * (a + keep * h_n), l_now * (keep * h_d - a * result)]
            return (d_keep, d_first, *out)

        carry = lax.fori_loop(0, chunk, step, tuple(carry))
        vectors[level, 0] += carry[0] * (-rate * keep)
        vectors[level, 1] += carry[1]

    def to_low(src, dst):
        @pl.loop(0, blocks)
        def _(i):
            dst[:, span(i), :] = src[:, span(i), :].astype(LOW)

    ffn_names = ("value2", "recept", "squared", "xk2", "xr2", "x1")
    att_names = tuple(n for n in names if n not in ffn_names)

    def serve():
        reduce.serve(SITES[reduce.site])
        reduce.site += 1

    def backward_layer(level):
        w_kvr, w_out, w_fkey, w_frec, w_fval = weights[level]
        base = (layers - 1 - level) * per_layer
        third = hidden // 3
        share = hidden // lines
        loaded("value2", level)
        loaded("recept", level)

        @pl.loop(0, blocks)
        def _(i):
            gate = jax.nn.sigmoid(act["recept"][:, span(i), :])
            g = grad[:, span(i), :]
            g_low[:, span(i), :] = (g * gate).astype(LOW)
            g_low2[:, span(i), :] = (g * act["value2"][:, span(i), :] * gate * (1.0 - gate)).astype(LOW)

        loaded("xr2", level)
        back_project(g_low2, w_frec, 0, width, d_two)
        outer(act["xr2"], g_low2, w_frec, 0, width)
        reduce.emit(base)
        loaded("squared", level)

        @pl.loop(0, lines)
        def _(z):
            got = dot_across(flat(g_low), w_fval[z].reshape(share, width)).reshape(rows, length, share)
            root = jnp.sqrt(act["squared"][:, :, wide(z, 0, share)].astype(F32))
            g_key2[:, :, wide(z, 0, share)] = (got * (2.0 * root)).astype(LOW)

        serve()

        @pl.loop(0, lines)
        def _(z):
            turned[...] = act["squared"][:, :, wide(z, 0, share)].reshape(tokens_total, share).T
            for j in range(width // WIDE):
                g = g_low[:, :, j * WIDE : (j + 1) * WIDE].reshape(tokens_total, WIDE)
                got = dot(turned[...], g).astype(LOW)
                w_fval[z, :, :, j * WIDE : (j + 1) * WIDE] = got.reshape(2, share // 2, WIDE)

        for j in range(3):
            reduce.emit(base + 1 + j)
        serve()
        back_project(g_key2, w_fkey, 0, hidden, d_one)
        serve()
        loaded("xk2", level)
        for j in range(3):
            outer(act["xk2"], g_key2, w_fkey, j * third, third, j * third)
            reduce.emit(base + 4 + j)
            serve()
        loaded("x1", level)
        normalize_into(act["x1"], level, 1)
        blend_back(level, 1, [d_one, d_two], (3, 4))
        serve()

        def write_att(i, after):
            g_low3[:, span(i), :] = after.astype(LOW)

        normalize_back(level, 1, act["x1"], d_one, write_att)
        serve()
        if level == 1:
            loading(ffn_names)
        back_project(g_low3, w_out, 0, width, main)
        loaded("gated", level)
        outer(act["gated"], g_low3, w_out, 0, width)
        reduce.emit(base + 7)
        serve()
        for name in ("logit", "key", "value", "numer", "denom"):
            loaded(name, level)
        after = scan_back_local(level)
        serve()
        to_low(d_two, g_low)
        loaded("xr", level)
        back_project(g_low, w_kvr, 2 * width, width, d_three)
        outer(act["xr"], g_low, w_kvr, 2 * width, width)
        reduce.emit(base + 8)
        serve()
        scan_back_final(level, after)
        serve()
        to_low(d_one, g_low2)
        to_low(d_two, g_low3)
        loaded("xk", level)
        loaded("xv", level)
        back_project(g_low2, w_kvr, 0, width, d_one)
        outer(act["xk"], g_low2, w_kvr, 0, width)
        reduce.emit(base + 9)
        serve()
        back_project(g_low3, w_kvr, width, width, d_two)
        outer(act["xv"], g_low3, w_kvr, width, width)
        reduce.emit(base + 10)
        serve()
        loaded("x", level)
        normalize_into(act["x"], level, 0)
        blend_back(level, 0, [d_one, d_two, d_three], (0, 1, 2))
        serve()

        def write_none(i, after):
            g_low[:, span(i), :] = after.astype(LOW)

        normalize_back(level, 0, act["x"], d_one, write_none)
        serve()
        if level == 1:
            loading(att_names)

    for level in reversed(range(layers)):
        backward_layer(level)
    for r in range(rows):
        grad_tokens[r] = dot(order_back, g_low[r]).astype(LOW)

    count = vectors.shape[1]

    def vector_hop(j, device):
        source = min(j, 3)
        return remote(v_buf.at[0, source], v_buf.at[1, j], v_send.at[j], v_recv.at[j], device)

    def vector_stage(stage):
        if stage == 0:
            for level in range(layers):
                for row in range(count):
                    j = level * count + row
                    v_buf[0, 0, j : j + 1, :] = jnp.sum(vectors[level, row], axis=0, keepdims=True)
        elif stage < 4:
            vector_hop(stage - 1, pos.partner).wait_recv()
            v_buf[0, stage] = v_buf[0, stage - 1] + v_buf[1, stage - 1]
        if stage < 3:
            vector_hop(stage, (pos.partner, pos.first, pos.second)[stage]).start()
        elif stage == 3:
            for k in range(1, lines):
                vector_hop(2 + k, pos.along(k)).start()
        else:
            total = v_buf[0, 3]
            for k in range(1, lines):
                vector_hop(2 + k, pos.along(k)).wait_recv()
                total = total + v_buf[1, 2 + k]
            vector_out[...] = total

    for stage in range(5):
        vector_stage(stage)
        reduce.turn()
    while not reduce.done():
        reduce.turn()
    reduce.finish()
    for j, device in enumerate((pos.partner, pos.first, pos.second)):
        vector_hop(j, device).wait_send()
    for k in range(1, lines):
        vector_hop(2 + k, pos.along(k)).wait_send()
    for level in range(layers):
        for which in range(2):
            index = level * 2 + which
            edge_sent(index, 1, s < last)
            edge_sent(2 * layers + index, -1, s > 0)
        for direction in range(2):
            chain_do(level, direction, "wait_send")


def finish_kernel(dims, *refs):
    layers, share, moved = dims
    ins, sums = refs[:moved], refs[moved]
    outs = refs[moved + 1 : 2 * moved + 1]
    decay, first, mix, gain, bias = refs[2 * moved + 1 : 2 * moved + 6]
    came = refs[2 * moved + 6 : 3 * moved + 6]
    wide = came[:2] + refs[3 * moved + 6 : 4 * moved + 4]
    in_sem, out_sem = refs[4 * moved + 4 :]
    parts = [(i, j) for i in range(moved) for j in range(layers)]

    def arrive(i, j):
        return pltpu.make_async_copy(ins[i].at[j], came[i].at[j], in_sem.at[i, j])

    def leave(i, j):
        return pltpu.make_async_copy(wide[i].at[j], outs[i].at[j], out_sem.at[i, j])

    for part in parts:
        arrive(*part).start()
    offset = lax.axis_index("dp") * share
    width = sums.shape[1]
    own = pltpu.roll(sums[...], lax.rem(width - offset, width), 1)[:, :share]
    for level in range(layers):
        at = level * 11
        decay[level : level + 1, :] = own[at : at + 1]
        first[level : level + 1, :] = own[at + 1 : at + 2]
        for j in range(5):
            mix[j, level : level + 1, :] = own[at + 2 + j : at + 3 + j]
        for j in range(2):
            gain[level, j : j + 1, :] = own[at + 7 + j : at + 8 + j]
            bias[level, j : j + 1, :] = own[at + 9 + j : at + 10 + j]
    for i, j in parts:
        arrive(i, j).wait()
        if i >= 2:
            rows = ins[i].shape[1]

            @pl.loop(0, rows // 16)
            def _(k):
                at = pl.ds(pl.multiple_of(k * 16, 16), 16)
                wide[i][j, at, :] = came[i][j, at, :].astype(F32)

        leave(i, j).start()
    for part in parts:
        leave(*part).wait()


def fast_body(
    tokens, doc_starts, decay, first, mix, ln_gain, ln_bias,
    att_kvr, att_out, ffn_key, ffn_recept, ffn_value, cotangent,
):
    rows, length, width = tokens.shape
    layers, hidden = decay.shape[0], ffn_key.shape[2]
    lines = lax.axis_size("dp") // 2
    shards = (att_kvr, att_out, ffn_key, ffn_recept, ffn_value)
    plain, low = (rows, length, width), LOW
    saved = [jax.ShapeDtypeStruct(plain, F32)] * len(SAVED)
    saved += [jax.ShapeDtypeStruct(plain, low)] * len(SAVED_LOW)
    saved += [jax.ShapeDtypeStruct((rows, length, hidden), low)]
    vector_rows = -(-layers * 11 // 8) * 8
    outs = [
        jax.ShapeDtypeStruct(plain, low),
        jax.ShapeDtypeStruct(plain, low),
        jax.ShapeDtypeStruct((vector_rows, width), F32),
    ]
    outs += [jax.ShapeDtypeStruct(w.shape, low) for w in shards]
    outs += saved
    vmem, anywhere = pl.BlockSpec(memory_space=pltpu.VMEM), pl.BlockSpec(memory_space=pl.ANY)
    units = 11 * layers
    hops = 4 * layers + 6 * layers
    dma, plain_f32, plain_low = pltpu.SemaphoreType.DMA, pltpu.VMEM(plain, F32), pltpu.VMEM(plain, low)
    scratch = [pltpu.VMEM((lines, 2) + w.shape[1:], low) for _ in range(layers) for w in shards]
    scratch += [pltpu.VMEM((lines,) + w.shape[1:], low) for w in shards]
    scratch += [pltpu.VMEM(a.shape, a.dtype) for a in saved]
    scratch += [
        pltpu.VMEM((rows, length, 128), F32),
        pltpu.VMEM((rows, length + 8, width), F32),
        plain_f32,
        plain_f32,
        plain_f32,
        plain_f32,
        plain_f32,
        plain_low,
        plain_low,
        plain_low,
        pltpu.VMEM((rows, length, hidden), low),
        pltpu.VMEM((width, rows * length), low),
        pltpu.VMEM((layers, 11, 8, width), F32),
        pltpu.VMEM((2, hops, 8, width), F32),
        pltpu.VMEM((layers, rows, 8, width), F32),
        pltpu.VMEM((2, 6, vector_rows, width), F32),
        dma((units, 3 * lines - 2)),
        dma((units, 3 * lines - 2)),
        dma((layers, len(shards))),
        dma((units, 5 + lines)),
        dma((units, 5 + lines)),
        pltpu.SemaphoreType.REGULAR((units, 1 + lines)),
        pltpu.SemaphoreType.REGULAR((units // layers,)),
        dma((units,)),
        dma((len(saved),)),
        dma((len(saved),)),
        dma((hops,)),
        dma((hops,)),
        dma((6,)),
        dma((6,)),
    ]
    smem = pl.BlockSpec(memory_space=pltpu.SMEM)
    got = pl.pallas_call(
        functools.partial(train_kernel, (layers, lines, rows, length, width, hidden)),
        out_shape=outs,
        in_specs=[vmem, smem] + [vmem] * 5 + [anywhere] * len(shards) + [vmem],
        out_specs=[vmem] * 3 + [anywhere] * (len(outs) - 3),
        scratch_shapes=scratch,
        compiler_params=pltpu.CompilerParams(
            collective_id=0, has_side_effects=True, vmem_limit_bytes=VMEM_BYTES
        ),
    )(tokens, doc_starts, decay, first, jnp.swapaxes(mix, 0, 1), ln_gain, ln_bias, *shards, cotangent)
    share = width // lax.axis_size("dp")
    final = [jax.ShapeDtypeStruct(plain, low)] * 2
    final += [jax.ShapeDtypeStruct(w.shape, F32) for w in shards]
    final += [jax.ShapeDtypeStruct((layers, share), F32)] * 2
    final += [jax.ShapeDtypeStruct((5, layers, share), F32)]
    final += [jax.ShapeDtypeStruct((layers, 2, share), F32)] * 2
    moved = 2 + len(shards)
    done = pl.pallas_call(
        functools.partial(finish_kernel, (layers, share, moved)),
        out_shape=final,
        in_specs=[anywhere] * moved + [vmem],
        out_specs=[anywhere] * moved + [vmem] * 5,
        scratch_shapes=[pltpu.VMEM(a.shape, low) for a in final[:moved]]
        + [pltpu.VMEM(a.shape, F32) for a in final[2:moved]]
        + [dma((moved, layers)), dma((moved, layers))],
        compiler_params=pltpu.CompilerParams(vmem_limit_bytes=VMEM_BYTES),
    )(got[0], got[1], *got[3 : 3 + len(shards)], got[2])
    output, grad_tokens = done[:2]
    g_decay, g_first, g_mix, g_gain, g_bias = done[moved:]
    return (
        output,
        grad_tokens,
        g_decay,
        g_first,
        jnp.swapaxes(g_mix, 0, 1),
        g_gain,
        g_bias,
        *done[2:moved],
    )


def kernel_fits(tokens, decay, ffn_key, shards):
    rows, length, width = tokens.shape
    lines = lax.axis_size("dp") // 2
    return (
        lax.axis_size("seq") == 4
        and lax.axis_size("dp") == 2 * lines
        and lines > 1
        and decay.shape[0] == 2
        and rows == 2
        and length % BLOCK == 0
        and length & (length - 1) == 0
        and width % WIDE == 0
        and ffn_key.shape[2] == width * lines
        and all(w.shape[1] % 32 == 0 and w.shape[2] % WIDE == 0 for w in shards)
    )


def from_behind(block, axis, distance):
    devices = range(lax.axis_size(axis))
    route = [(i - distance, i) for i in devices if i - distance in devices]
    return lax.ppermute(block, axis, route)


def normalize(stream, gain_row, bias_row):
    center = stream - jnp.mean(stream, -1, keepdims=True)
    spread = jnp.mean(center * center, -1, keepdims=True)
    return center * lax.rsqrt(spread + EPSILON) * gain_row + bias_row


def blend(hidden, edge_row, rates, starts):
    earlier = (
        jnp.concatenate([edge_row[:, None, :], hidden[:, :-1, :]], axis=1)
        * (1.0 - starts)[:, :, None]
    )
    return tuple((hidden * rates[j] + earlier * (1.0 - rates[j]) for j in range(rates.shape[0])))


def product(inputs, matrix):
    return jnp.einsum("rcd,de->rce", inputs, matrix, preferred_element_type=jnp.float32)


def product_back(grads, matrix):
    return jnp.einsum("rce,de->rcd", grads, matrix, preferred_element_type=jnp.float32)


def outer_sum(inputs, grads):
    return jnp.einsum("rcd,rce->de", inputs, grads, preferred_element_type=jnp.float32)


def wkv_tokens(key_proj, value_proj, decay_row, foremost_line_entry, numer_in, denom_in, starts):
    rows, length, width = key_proj.shape
    block = math.gcd(length, 64)
    count = length // block
    rate = jnp.exp(decay_row)
    local = jnp.arange(block, dtype=jnp.float32)
    lower = (local[:, None] > local[None, :]).astype(jnp.float32)
    grow = jnp.exp(local[:, None] * rate[None, :])
    shrink = jnp.exp(-(local[:, None] - 1.0) * rate[None, :])
    fade = jnp.exp(-local[:, None] * rate[None, :])
    keep_rate = jnp.exp(-rate)

    def one_block(carry, inputs):
        accrued_dividend_total, accrued_divisor_total = carry
        present_lookup_entry, present_payload_entry, start_now = inputs
        counted = jnp.cumsum(start_now, axis=1)
        same = lower[None] * (counted[:, :, None] == counted[:, None, :]).astype(jnp.float32)
        alive = (counted == 0.0).astype(jnp.float32)[:, :, None]
        key_exp = jnp.exp(present_lookup_entry)
        lifted = grow[None] * key_exp
        numer_sum = jnp.einsum(
            "rji,ric->rjc", same, lifted * present_payload_entry, precision=lax.Precision.HIGHEST
        )
        denom_sum = jnp.einsum("rji,ric->rjc", same, lifted, precision=lax.Precision.HIGHEST)
        present_dividend_term = (
            shrink[None] * numer_sum + fade[None] * alive * accrued_dividend_total[:, None, :]
        )
        present_divisor_term = (
            shrink[None] * denom_sum + fade[None] * alive * accrued_divisor_total[:, None, :]
        )
        present_reward_term = jnp.exp(foremost_line_entry + present_lookup_entry)
        recurrence_result = (
            present_dividend_term + present_reward_term * present_payload_entry
        ) / (present_divisor_term + present_reward_term)
        numer_end = (
            keep_rate * present_dividend_term[:, -1] + key_exp[:, -1] * present_payload_entry[:, -1]
        )
        denom_end = keep_rate * present_divisor_term[:, -1] + key_exp[:, -1]
        return ((numer_end, denom_end), recurrence_result)

    def split(values):
        return jnp.swapaxes(values.reshape((rows, count, block) + values.shape[2:]), 0, 1)

    carry_end, results = lax.scan(
        one_block, (numer_in, denom_in), (split(key_proj), split(value_proj), split(starts))
    )
    return jnp.swapaxes(results, 0, 1).reshape(rows, length, width)


def span_transform(key_proj, value_proj, decay_row, starts):
    length = key_proj.shape[1]
    rate = jnp.exp(decay_row)
    steps = jnp.arange(length, dtype=jnp.float32)
    last_start = jnp.max(steps[None, :] * starts, axis=1)
    after = (steps[None, :] >= last_start[:, None]).astype(jnp.float32)
    weight = jnp.exp(key_proj - (length - 1.0 - steps)[None, :, None] * rate) * after[:, :, None]
    carry_numer = jnp.sum(weight * value_proj, axis=1)
    carry_denom = jnp.sum(weight, axis=1)
    through = jnp.prod(1.0 - starts, axis=1)[:, None] * jnp.exp(-length * rate)[None, :]
    return (through, carry_numer, carry_denom)


def body(
    tokens,
    doc_starts,
    decay,
    first,
    mix,
    ln_gain,
    ln_bias,
    att_kvr,
    att_out,
    ffn_key,
    ffn_recept,
    ffn_value,
    cotangent,
):
    shards = (att_kvr, att_out, ffn_key, ffn_recept, ffn_value)
    if kernel_fits(tokens, decay, ffn_key, shards):
        return fast_body(
            tokens, doc_starts, decay, first, mix, ln_gain, ln_bias, *shards, cotangent
        )
    row_total, token_total, width = tokens.shape
    layer_total = decay.shape[0]
    batches = 2
    per_batch = row_total // batches
    positions = lax.axis_index("seq") * token_total + jnp.arange(token_total, dtype=jnp.int32)
    starts_all = jnp.any(doc_starts[:, :, None] == positions[None, None, :], axis=1).astype(
        jnp.float32
    )
    empty = jnp.zeros((per_batch, width), jnp.float32)

    def edge_of(hidden):
        return from_behind(hidden[:, -1, :], "seq", 1)

    def edge_back(grad_edge):
        return from_behind(grad_edge, "seq", -1)

    def chain_forward(through, carry_numer, carry_denom):
        incoming = (empty, empty)
        sent_numer, sent_denom = (carry_numer, carry_denom)
        for relay_turn in range(lax.axis_size("seq") - 1):
            incoming = from_behind((sent_numer, sent_denom), "seq", 1)
            sent_numer = through * incoming[0] + carry_numer
            sent_denom = through * incoming[1] + carry_denom
        return incoming

    def forward_layer(stream, level, matrices, starts):
        w_kvr, w_out, w_fkey, w_frec, w_fval = matrices
        hidden, norm_one = jax.vjp(normalize, stream, ln_gain[level, 0], ln_bias[level, 0])
        edge_row = edge_of(hidden)
        blends, blend_one = jax.vjp(
            lambda h_in, e_in, r_in: blend(h_in, e_in, r_in, starts),
            hidden,
            edge_row,
            mix[level, :3],
        )
        xk_low, xv_low, xr_low = [b.astype(jnp.bfloat16) for b in blends]
        key_proj = product(xk_low, w_kvr[:, :width])
        value_proj = product(xv_low, w_kvr[:, width : 2 * width])
        logit = product(xr_low, w_kvr[:, 2 * width :])
        transform, transform_one = jax.vjp(
            lambda k_in, v_in, d_in: span_transform(k_in, v_in, d_in, starts),
            key_proj,
            value_proj,
            decay[level],
        )
        numer_in, denom_in = chain_forward(transform[0], transform[1], transform[2])
        mixed, tokens_one = jax.vjp(
            lambda k_in, v_in, d_in, f_in, n_in, z_in: wkv_tokens(
                k_in, v_in, d_in, f_in, n_in, z_in, starts
            ),
            key_proj,
            value_proj,
            decay[level],
            first[level],
            numer_in,
            denom_in,
        )
        gated, gate_one = jax.vjp(lambda g_in, m_in: jax.nn.sigmoid(g_in) * m_in, logit, mixed)
        gated_low = gated.astype(jnp.bfloat16)
        middle = stream + product(gated_low, w_out)
        hidden_two, norm_two = jax.vjp(normalize, middle, ln_gain[level, 1], ln_bias[level, 1])
        edge_two = edge_of(hidden_two)
        blends_two, blend_two = jax.vjp(
            lambda h_in, e_in, r_in: blend(h_in, e_in, r_in, starts),
            hidden_two,
            edge_two,
            mix[level, 3:],
        )
        xk2_low, xr2_low = [b.astype(jnp.bfloat16) for b in blends_two]
        key_two = product(xk2_low, w_fkey)
        squared, square_one = jax.vjp(lambda k_in: jnp.square(jax.nn.relu(k_in)), key_two)
        squared_low = squared.astype(jnp.bfloat16)
        value_two = product(squared_low, w_fval)
        recept = product(xr2_low, w_frec)
        branch, branch_one = jax.vjp(
            lambda r_in, v_in: jax.nn.sigmoid(r_in) * v_in, recept, value_two
        )
        record = (
            norm_one,
            blend_one,
            xk_low,
            xv_low,
            xr_low,
            transform[0],
            numer_in,
            denom_in,
            transform_one,
            tokens_one,
            gate_one,
            gated_low,
            norm_two,
            blend_two,
            xk2_low,
            xr2_low,
            square_one,
            squared_low,
            branch_one,
        )
        return (middle + branch, record)

    gathered = []
    for level in range(layer_total):
        gathered.append(
            (
                lax.all_gather(att_kvr[level], "dp", axis=0, tiled=True),
                lax.all_gather(att_out[level], "dp", axis=0, tiled=True),
                lax.all_gather(ffn_key[level], "dp", axis=0, tiled=True),
                lax.all_gather(ffn_recept[level], "dp", axis=0, tiled=True),
                lax.all_gather(ffn_value[level], "dp", axis=0, tiled=True),
            )
        )
    pair_lists = [[] for level in range(layer_total)]
    vector_sums = [None] * layer_total
    outputs = []
    grad_parts = []
    for batch in range(batches):
        low_row = batch * per_batch
        starts = starts_all[low_row : low_row + per_batch]
        stream = tokens[low_row : low_row + per_batch].astype(jnp.float32)
        records = []
        for level in range(layer_total):
            stream, record = forward_layer(stream, level, gathered[level], starts)
            records.append(record)
        outputs.append(stream.astype(jnp.bfloat16))
        gradient = cotangent[low_row : low_row + per_batch].astype(jnp.float32)
        for level in reversed(range(layer_total)):
            backward_w_kvr, backward_w_out, backward_w_fkey, backward_w_frec, backward_w_fval = (
                gathered[level]
            )
            (
                backward_norm_one,
                backward_blend_one,
                backward_xk_low,
                backward_xv_low,
                backward_xr_low,
                backward_through,
                backward_numer_in,
                backward_denom_in,
                backward_transform_one,
                backward_tokens_one,
                backward_gate_one,
                backward_gated_low,
                backward_norm_two,
                backward_blend_two,
                backward_xk2_low,
                backward_xr2_low,
                backward_square_one,
                backward_squared_low,
                backward_branch_one,
            ) = records[level]
            d_recept, d_value_two = backward_branch_one(gradient)
            g_value_two = d_value_two.astype(jnp.bfloat16)
            g_recept = d_recept.astype(jnp.bfloat16)
            (d_key_two,) = backward_square_one(product_back(g_value_two, backward_w_fval))
            g_key_two = d_key_two.astype(jnp.bfloat16)
            d_hidden_two, d_edge_two, d_rates_two = backward_blend_two(
                (product_back(g_key_two, backward_w_fkey), product_back(g_recept, backward_w_frec))
            )
            d_hidden_two = d_hidden_two.at[:, -1, :].add(edge_back(d_edge_two))
            d_middle_norm, d_gain_two, d_bias_two = backward_norm_two(d_hidden_two)
            d_middle = gradient + d_middle_norm
            g_att = d_middle.astype(jnp.bfloat16)
            d_logit, d_mixed = backward_gate_one(product_back(g_att, backward_w_out))
            g_logit = d_logit.astype(jnp.bfloat16)
            (
                d_key_one,
                d_value_one,
                d_decay_one,
                d_first,
                backward_direct_numer,
                backward_direct_denom,
            ) = backward_tokens_one(d_mixed)
            chain_incoming = (empty, empty)
            chain_sent_numer = backward_direct_numer
            chain_sent_denom = backward_direct_denom
            for chain_relay_turn in range(lax.axis_size("seq") - 1):
                chain_incoming = from_behind((chain_sent_numer, chain_sent_denom), "seq", -1)
                chain_sent_numer = backward_through * chain_incoming[0] + backward_direct_numer
                chain_sent_denom = backward_through * chain_incoming[1] + backward_direct_denom
            g_numer_out, g_denom_out = chain_incoming
            d_key_two_part, d_value_two_part, d_decay_two = backward_transform_one(
                (
                    g_numer_out * backward_numer_in + g_denom_out * backward_denom_in,
                    g_numer_out,
                    g_denom_out,
                )
            )
            g_key = (d_key_one + d_key_two_part).astype(jnp.bfloat16)
            g_value = (d_value_one + d_value_two_part).astype(jnp.bfloat16)
            d_blends = (
                product_back(g_key, backward_w_kvr[:, :width]),
                product_back(g_value, backward_w_kvr[:, width : 2 * width]),
                product_back(g_logit, backward_w_kvr[:, 2 * width :]),
            )
            d_hidden, d_edge, d_rates = backward_blend_one(d_blends)
            d_hidden = d_hidden.at[:, -1, :].add(edge_back(d_edge))
            d_stream_norm, d_gain_one, d_bias_one = backward_norm_one(d_hidden)
            pairs = (
                (backward_xk2_low, g_key_two),
                (backward_xr2_low, g_recept),
                (backward_squared_low, g_value_two),
                (backward_xk_low, g_key),
                (backward_xv_low, g_value),
                (backward_xr_low, g_logit),
                (backward_gated_low, g_att),
            )
            columns = (
                [d_decay_one + d_decay_two, d_first]
                + [d_rates[j] for j in range(3)]
                + [d_rates_two[j] for j in range(2)]
                + [d_gain_one, d_gain_two, d_bias_one, d_bias_two]
            )
            backward_vectors = jnp.stack(columns, axis=1)
            gradient, pairs, vectors = (d_middle + d_stream_norm, pairs, backward_vectors)
            pair_lists[level].append(pairs)
            vector_sums[level] = (
                vectors if vector_sums[level] is None else vector_sums[level] + vectors
            )
        grad_parts.append(gradient.astype(jnp.bfloat16))
    results = [None] * layer_total
    for level in reversed(range(layer_total)):
        pair_list = pair_lists[level]

        def summed(index):
            inputs = jnp.concatenate([p[index][0] for p in pair_list], axis=0)
            grads = jnp.concatenate([p[index][1] for p in pair_list], axis=0)
            return outer_sum(inputs, grads)

        ffn_part = (summed(0), summed(1), summed(2))
        finish_grad_kvr = jnp.concatenate([summed(3), summed(4), summed(5)], axis=1)
        totals = (
            lax.psum(
                lax.psum_scatter(ffn_part[0], "dp", scatter_dimension=0, tiled=True).astype(
                    jnp.bfloat16
                ),
                "seq",
            ).astype(jnp.float32),
            lax.psum(
                lax.psum_scatter(ffn_part[1], "dp", scatter_dimension=0, tiled=True).astype(
                    jnp.bfloat16
                ),
                "seq",
            ).astype(jnp.float32),
            lax.psum(
                lax.psum_scatter(ffn_part[2], "dp", scatter_dimension=0, tiled=True).astype(
                    jnp.bfloat16
                ),
                "seq",
            ).astype(jnp.float32),
            lax.psum(
                lax.psum_scatter(finish_grad_kvr, "dp", scatter_dimension=0, tiled=True).astype(
                    jnp.bfloat16
                ),
                "seq",
            ).astype(jnp.float32),
            lax.psum(
                lax.psum_scatter(summed(6), "dp", scatter_dimension=0, tiled=True).astype(
                    jnp.bfloat16
                ),
                "seq",
            ).astype(jnp.float32),
            lax.psum(
                lax.psum_scatter(vector_sums[level], "dp", scatter_dimension=0, tiled=True).astype(
                    jnp.bfloat16
                ),
                "seq",
            ).astype(jnp.float32),
        )
        ffn_part = (totals[0], totals[1], totals[2])
        att_part = (totals[3], totals[4], totals[5])
        results[level] = (ffn_part, att_part)
    output = jnp.concatenate(outputs, axis=0)
    grad_tokens = jnp.concatenate(grad_parts, axis=0)
    grad_ffn_key = jnp.stack([r[0][0] for r in results])
    grad_ffn_recept = jnp.stack([r[0][1] for r in results])
    grad_ffn_value = jnp.stack([r[0][2] for r in results])
    grad_kvr = jnp.stack([r[1][0] for r in results])
    grad_att_out = jnp.stack([r[1][1] for r in results])
    vector_rows = jnp.stack([r[1][2] for r in results])
    grad_decay = vector_rows[:, :, 0]
    grad_first = vector_rows[:, :, 1]
    grad_mix = jnp.swapaxes(vector_rows[:, :, 2:7], 1, 2)
    grad_gain = jnp.swapaxes(vector_rows[:, :, 7:9], 1, 2)
    grad_bias = jnp.swapaxes(vector_rows[:, :, 9:11], 1, 2)
    return (
        output,
        grad_tokens,
        grad_decay,
        grad_first,
        grad_mix,
        grad_gain,
        grad_bias,
        grad_kvr,
        grad_att_out,
        grad_ffn_key,
        grad_ffn_recept,
        grad_ffn_value,
    )


def solution(mesh):
    in_specs = (
        P("dp", "seq", None),
        P("dp", None),
        P(),
        P(),
        P(),
        P(),
        P(),
        P(None, "dp", None),
        P(None, "dp", None),
        P(None, "dp", None),
        P(None, "dp", None),
        P(None, "dp", None),
        P("dp", "seq", None),
    )
    out_specs = (
        P("dp", "seq", None),
        P("dp", "seq", None),
        P(None, "dp"),
        P(None, "dp"),
        P(None, None, "dp"),
        P(None, None, "dp"),
        P(None, None, "dp"),
        P(None, "dp", None),
        P(None, "dp", None),
        P(None, "dp", None),
        P(None, "dp", None),
        P(None, "dp", None),
    )
    return jax.shard_map(body, mesh=mesh, in_specs=in_specs, out_specs=out_specs, check_vma=False)
```

```python
import functools
import math

import jax
import jax.numpy as jnp
from jax import lax
from jax.experimental import pallas as pl
from jax.experimental.pallas import tpu as pltpu
from jax.sharding import PartitionSpec as P

EPSILON = 1e-05
MESH = pl.DeviceIdType.MESH
F32, LOW = jnp.float32, jnp.bfloat16


class Place:
    def __init__(self, lines):
        self.lines = lines
        s, d = lax.axis_index("seq"), lax.axis_index("dp")
        self.s, self.d = s, d
        self.c, self.z = lax.rem(d, 2), d // 2
        x, y, c = lax.rem(s, 2), s // 2, self.c
        self.f = x * (1 - c) + y * c
        self.g = y * (1 - c) + x * c
        flip_x, flip_y = s + 1 - 2 * x, s + 2 - 4 * y
        self.first = (flip_x * (1 - c) + flip_y * c, d)
        self.second = (flip_y * (1 - c) + flip_x * c, d)
        self.across = (3 - s, d)
        self.partner = (s, d + 1 - 2 * c)

    def line(self, k):
        return lax.rem(self.z + k + self.lines, self.lines)

    def along(self, k):
        return (self.s, self.line(k) * 2 + self.c)

    def later(self, k):
        return (self.s + k, self.d)


def remote(src, dst, send, recv, device):
    return pltpu.make_async_remote_copy(
        src_ref=src, dst_ref=dst, send_sem=send, recv_sem=recv, device_id=device, device_id_type=MESH
    )


def signal(semaphore, device):
    pl.semaphore_signal(semaphore, inc=1, device_id=device, device_id_type=MESH)


def half(start, size, which, align):
    return pl.ds(pl.multiple_of(start + which * (size // 2), align), size // 2)


class Gather:
    def __init__(self, pos, units, send, recv, ahead):
        self.pos, self.units, self.ahead = pos, units, ahead
        self.turns = self.settled = 0
        lines = pos.lines
        self.stages = []
        self.plan, self.ready = {}, []
        for u in reversed(range(len(units))):
            at = u
            for stage, lag in enumerate((0, *GATHER_LAGS)):
                at += lag
                self.plan.setdefault(at, []).append((stage, u))
            self.ready.insert(0, at)
        for u, (w, (r0, rows, c0, cols), _) in enumerate(units):
            gh, fh = half(r0, rows, pos.g, 16), half(c0, cols, pos.f, 128)
            ar, ac = pl.ds(r0, rows), pl.ds(c0, cols)
            stages = [[], [], [], []]
            for k in range(1, lines):
                far = pos.line(-k)
                own = w.at[pos.z, pos.c, gh, fh]
                stages[0].append(remote(own, own, send.at[u, k - 1], recv.at[u, k - 1], pos.along(k)))
                j = lines - 1 + k - 1
                block = w.at[far, pos.c, gh, fh]
                stages[1].append(remote(block, block, send.at[u, j], recv.at[u, j], pos.second))
                j = 2 * (lines - 1) + k - 1
                block = w.at[far, pos.c, ar, fh]
                stages[2].append(remote(block, block, send.at[u, j], recv.at[u, j], pos.first))
            j = 3 * (lines - 1)
            block = w.at[:, pos.c, ar, ac]
            stages[3].append(remote(block, block, send.at[u, j], recv.at[u, j], pos.partner))
            self.stages.append(stages)

    def begin(self, u):
        if u < len(self.units):
            own = self.units[u][2]
            if own is not None:
                own.wait()
            for copy in self.stages[u][0]:
                copy.start()

    def turn(self):
        turn = self.turns
        self.turns += 1
        self.begin(turn + self.ahead)
        for stage, u in self.plan.get(turn, ()):
            for i, copy in enumerate(self.stages[u][stage]):
                copy.wait_recv()
                if stage < 2:
                    self.stages[u][stage + 1][i].start()
            if stage == 2:
                self.stages[u][3][0].start()
        self.settle(turn - sum(GATHER_LAGS) - 1)

    def need(self, u):
        while self.turns <= self.ready[u]:
            self.turn()

    def settle(self, count):
        while self.settled < min(count, len(self.units)):
            for stage in self.stages[self.settled]:
                for copy in stage:
                    copy.wait_send()
            self.settled += 1


class Reduce:
    def __init__(self, pos, units, shared, send, recv, free, credit, local):
        self.pos, self.units, self.shared = pos, units, shared
        self.send, self.recv, self.free, self.credit, self.local = send, recv, free, credit, local
        self.turns = self.emitted = self.cleared = self.paired = self.mark = self.settled = 0
        self.copies = {}
        self.steps = self.plan()
        self.site = 0

    def copy(self, u, j, src, dst, device):
        made = remote(src, dst, self.send.at[u, j], self.recv.at[u, j], device)
        self.copies[u, j] = made
        made.start()

    def views(self, u):
        w, landing, out, (r0, rows, c0, cols), _ = self.units[u]
        pos = self.pos
        v = {
            "ar": pl.ds(r0, rows),
            "ac": pl.ds(c0, cols),
            "gh": half(r0, rows, pos.g, 16),
            "go": half(r0, rows, 1 - pos.g, 16),
            "fh": half(c0, cols, pos.f, 128),
            "fo": half(c0, cols, 1 - pos.f, 128),
            "r0": pl.ds(r0, rows // 2),
            "r1": pl.ds(r0 + rows // 2, rows // 2),
            "c0": pl.ds(c0, cols // 2),
            "c1": pl.ds(c0 + cols // 2, cols // 2),
        }
        return w, landing, out, v

    def emit(self, u):
        w, landing, _, v = self.views(u)
        pos = self.pos
        assert u == self.emitted
        self.emitted += 1
        if u >= self.shared:
            pl.semaphore_wait(self.credit.at[u - self.shared], 1)
        self.copy(
            u, 0, w.at[:, 1 - pos.c, v["ar"], v["ac"]], landing.at[:, v["ar"], v["ac"]], pos.partner
        )

    def clear(self, u):
        pos = self.pos
        self.copies[u, 0].wait_send()
        signal(self.free.at[u, 0], pos.first)
        signal(self.free.at[u, 1], pos.second)
        for k in range(1, pos.lines):
            signal(self.free.at[u, 1 + k], pos.along(-k))

    def pair(self, u):
        w, landing, _, v = self.views(u)
        pos, c = self.pos, self.pos.c
        self.copies[u, 0].wait_recv()

        @pl.loop(0, pos.lines)
        def _(z):
            w[z, c, v["ar"], v["ac"]] += landing[z, v["ar"], v["ac"]]

        if u < self.shared:
            signal(self.credit.at[u], pos.partner)
        if self.units[u][4]:
            for k in range(1, pos.lines):
                pl.semaphore_wait(self.free.at[u, 1 + k], 1)
                self.copy(
                    u,
                    2 + k,
                    w.at[pos.line(k), c, v["ar"], v["ac"]],
                    w.at[k - 1, 1 - c, v["ar"], v["ac"]],
                    pos.along(k),
                )
            return
        pl.semaphore_wait(self.free.at[u, 0], 1)
        self.copy(u, 1, w.at[:, c, v["ar"], v["fo"]], w.at[:, 1 - c, v["ar"], v["c0"]], pos.first)

    def one(self, u):
        w, _, _, v = self.views(u)
        pos, c = self.pos, self.pos.c
        self.copies[u, 1].wait_recv()

        @pl.loop(0, pos.lines)
        def _(z):
            w[z, c, v["ar"], v["fh"]] += w[z, 1 - c, v["ar"], v["c0"]]

        pl.semaphore_wait(self.free.at[u, 1], 1)
        self.copy(u, 2, w.at[:, c, v["go"], v["fh"]], w.at[:, 1 - c, v["r0"], v["c1"]], pos.second)

    def two(self, u):
        w, _, _, v = self.views(u)
        pos, c = self.pos, self.pos.c
        self.copies[u, 2].wait_recv()

        @pl.loop(0, pos.lines)
        def _(z):
            w[z, c, v["gh"], v["fh"]] += w[z, 1 - c, v["r0"], v["c1"]]

        for k in range(1, pos.lines):
            pl.semaphore_wait(self.free.at[u, 1 + k], 1)
            self.copy(
                u,
                2 + k,
                w.at[pos.line(k), c, v["gh"], v["fh"]],
                w.at[k - 1, 1 - c, v["r1"], v["c1"]],
                pos.along(k),
            )

    def line(self, u):
        w, _, out, v = self.views(u)
        pos, c, lines = self.pos, self.pos.c, self.pos.lines
        for k in range(1, lines):
            self.copies[u, 2 + k].wait_recv()
        total = w[pos.z, c, v["gh"], v["fh"]].astype(F32)
        for k in range(1, lines):
            total = total + w[k - 1, 1 - c, v["r1"], v["c1"]].astype(F32)
        w[pos.z, c, v["gh"], v["fh"]] = total.astype(LOW)
        self.spread(u)

    def keep(self, u, j, src, there):
        made = pltpu.make_async_copy(src, there, self.local.at[u, j])
        self.copies[u, "local", j] = made
        made.start()

    def spread(self, u):
        w, _, out, v = self.views(u)
        pos, c, lines = self.pos, self.pos.c, self.pos.lines
        mine, there = w.at[pos.z, c, v["gh"], v["fh"]], out.at[v["gh"], v["fh"]]
        self.copy(u, 2 + lines, mine, w.at[lines - 1, 1 - c, v["r1"], v["c1"]], pos.second)
        self.copy(u, 3 + lines, mine, there, pos.first)
        self.keep(u, 0, mine, there)

    def relay(self, u):
        w, _, out, v = self.views(u)
        pos, c, lines = self.pos, self.pos.c, self.pos.lines
        self.copies[u, 2 + lines].wait_recv()
        came, there = w.at[lines - 1, 1 - c, v["r1"], v["c1"]], out.at[v["go"], v["fh"]]
        self.copy(u, 4 + lines, came, there, pos.first)
        self.keep(u, 1, came, there)

    def line_whole(self, u):
        w, _, _, v = self.views(u)
        pos, c, lines = self.pos, self.pos.c, self.pos.lines
        for k in range(1, lines):
            self.copies[u, 2 + k].wait_recv()
        total = w[pos.z, c, v["ar"], v["ac"]].astype(F32)
        for k in range(1, lines):
            total = total + w[k - 1, 1 - c, v["ar"], v["ac"]].astype(F32)
        w[pos.z, c, v["ar"], v["ac"]] = total.astype(LOW)
        pl.semaphore_wait(self.free.at[u, 0], 1)
        self.copy(
            u,
            1,
            w.at[pos.z, c, v["ar"], v["fo"]],
            w.at[lines - 1, 1 - c, v["ar"], v["c0"]],
            pos.first,
        )

    def one_share(self, u):
        w, _, _, v = self.views(u)
        pos, c, lines = self.pos, self.pos.c, self.pos.lines
        self.copies[u, 1].wait_recv()
        w[pos.z, c, v["ar"], v["fh"]] += w[lines - 1, 1 - c, v["ar"], v["c0"]]
        pl.semaphore_wait(self.free.at[u, 1], 1)
        self.copy(
            u,
            2,
            w.at[pos.z, c, v["go"], v["fh"]],
            w.at[lines - 1, 1 - c, v["r0"], v["c1"]],
            pos.second,
        )

    def two_share(self, u):
        w, _, _, v = self.views(u)
        pos, c, lines = self.pos, self.pos.c, self.pos.lines
        self.copies[u, 2].wait_recv()
        w[pos.z, c, v["gh"], v["fh"]] += w[lines - 1, 1 - c, v["r0"], v["c1"]]
        self.spread(u)

    def clears(self, count):
        while self.cleared < count:
            self.clear(self.cleared)
            self.cleared += 1

    def pairs(self, count):
        self.clears(count)
        while self.paired < count:
            self.pair(self.paired)
            self.paired += 1

    def serve(self, turns, eager=False):
        self.pairs(min(self.cleared, self.turns + LEAD))
        self.clears(self.emitted if eager else self.mark)
        self.mark = self.emitted
        for _ in range(turns):
            if all(u < self.paired for _, u in self.steps.get(self.turns, ())):
                self.turn()

    def plan(self):
        plan = {}
        for u in reversed(range(len(self.units))):
            whole = self.units[u][4]
            steps = (self.one, self.two, self.line)
            if whole:
                steps = (self.line_whole, self.one_share, self.two_share)
            steps = (*steps, self.relay)
            usual = LAGS if u < len(self.units) - LAST else LAST_LAGS
            lags = (WHOLE_LAG, *LAGS[:2], LAGS[3]) if whole else usual
            at = u
            for step, lag in zip(steps, lags):
                at += lag
                plan.setdefault(at, []).append((step, u))
        return plan

    def done(self):
        return self.turns > max(self.steps)

    def turn(self):
        if not self.done():
            steps = self.steps.get(self.turns, ())
            self.turns += 1
            self.pairs(max([u + 1 for _, u in steps] + [self.paired]))
            for step, u in steps:
                step(u)
            last = max(at for at, steps in self.steps.items() for _, u in steps if u == self.settled)
            if last <= self.turns - 4:
                self.settle(self.settled + 1)

    def settle(self, count):
        lines = self.pos.lines
        while self.settled < min(count, len(self.units)):
            u = self.settled
            for j in range(1, 5 + lines):
                self.copies[u, j].wait_send()
            for j in range(3 + lines, 5 + lines):
                self.copies[u, j].wait_recv()
            for j in range(2):
                self.copies[u, "local", j].wait()
            self.settled += 1


def dot(a, b):
    return jnp.dot(a, b, preferred_element_type=F32)


def dot_across(a, b):
    return lax.dot_general(a, b, (((1,), (1,)), ((), ())), preferred_element_type=F32)


SAVED = ("x", "x1", "key", "value", "logit", "numer", "denom", "value2", "recept")
SAVED_LOW = ("xk", "xv", "xr", "gated", "xk2", "xr2")
WIDE = 256
BLOCK = 32
LEAD = 12
GATHER_LAGS = (1, 1, 1)
VECTOR_TURNS = 3
AHEAD = 2
FIRST_PIECES = 1
LINE_FIRST = (1,7)
LAGS = (2,3,7,5)
LAST = 3
LAST_LAGS = (3,3,5,3)
WHOLE_LAG = 5
SITES = (1,0,1,1,1,0,0,0,0,0,1,1,0,0,1,1,0,1,0,2,0,1,1,0,0,1,1,1,1,0,1,1,1,1)
VMEM_BYTES = 63 * 2**20


def train_kernel(dims, *refs):
    layers, lines, rows, length, width, hidden = dims
    refs = list(refs)

    def take(count):
        got = refs[:count]
        del refs[:count]
        return got

    matrices = 5
    tokens, doc_starts, decay, first, mix, ln_gain, ln_bias = take(7)
    shards = take(matrices)
    (cotangent,) = take(1)
    output, grad_tokens, vector_out = take(3)
    grad_out = take(matrices)
    names = SAVED + SAVED_LOW + ("squared",)
    store = dict(zip(names, take(len(names))))
    weights = [take(matrices) for _ in range(layers)]
    landing = take(matrices)
    act = dict(zip(names, take(len(names))))
    (live, padded, grad, main, d_one, d_two, d_three, g_low, g_low2, g_low3, g_key2, turned) = take(12)
    vectors, small, vec, v_buf = take(4)
    (g_send, g_recv, own_sem, r_send, r_recv, r_free, r_credit, r_local, save_sem, load_sem, s_send, s_recv, v_send, v_recv) = take(14)
    tokens_total = rows * length
    blocks = length // BLOCK
    chunk = length // 8
    pos = Place(lines)
    s, last = pos.s, 3

    own = {}
    for l in range(layers):
        for m in range(matrices):
            own[l, m] = pltpu.make_async_copy(
                shards[m].at[l], weights[l][m].at[pos.z, pos.c], own_sem.at[l, m]
            )
            own[l, m].start()
    small[...] = jnp.zeros_like(small)
    vectors[...] = jnp.zeros_like(vectors)
    barrier = pltpu.get_barrier_semaphore()
    peers = [pos.along(k) for k in range(1, lines)]
    peers += [pos.first, pos.second, pos.across, pos.partner]
    for peer in peers:
        signal(barrier, peer)
    pl.semaphore_wait(barrier, len(peers))

    def pieces(m, count):
        _, _, r, c = weights[0][m].shape
        if m == 4:
            return [(m, (j * (r // count), r // count, 0, c)) for j in range(count)]
        return [(m, (0, r, j * (c // count), c // count)) for j in range(count)]

    def columns(m, count):
        _, _, r, c = weights[0][m].shape
        return [(m, (0, r, j * (c // count), c // count)) for j in range(count)]

    kvr = pieces(0, 3)
    start_units = [(0, (0, kvr[0][1][1], j * (width // FIRST_PIECES), width // FIRST_PIECES)) for j in range(FIRST_PIECES)]
    rest = kvr[1:] + pieces(1, 1) + pieces(2, 3) + pieces(3, 1) + columns(4, 3)
    layout = [start_units + rest, kvr[:1] + rest]
    base_of = [FIRST_PIECES - 1, FIRST_PIECES + len(rest)]
    gather = Gather(
        pos,
        [(weights[l][m], box, own.pop((l, m), None)) for l in range(layers) for m, box in layout[l]],
        g_send,
        g_recv,
        AHEAD,
    )
    for u in range(gather.ahead):
        gather.begin(u)

    back = pieces(3, 1) + pieces(4, 3) + pieces(2, 3) + pieces(1, 1) + [kvr[2], kvr[0], kvr[1]]
    line_first = LINE_FIRST
    reduce = Reduce(
        pos,
        [
            (weights[l][m], landing[m], grad_out[m].at[l], box, j in line_first)
            for l in reversed(range(layers))
            for j, (m, box) in enumerate(back)
        ],
        len(back),
        r_send,
        r_recv,
        r_free,
        r_credit,
        r_local,
    )

    sub = lax.broadcasted_iota(jnp.int32, (8, width), 0)
    place = lax.broadcasted_iota(jnp.int32, (length, 128), 0)
    at_token = (place % 8) * chunk + place // 8 + s * length
    for r in range(rows):
        start = jnp.zeros((length, 128), F32)
        for j in range(doc_starts.shape[1]):
            start = jnp.where(at_token == doc_starts[r, j], 1.0, start)
        live[r] = 1.0 - start
    p_row = lax.broadcasted_iota(jnp.int32, (length, length), 0)
    p_col = lax.broadcasted_iota(jnp.int32, (length, length), 1)
    order = jnp.where((p_row % 8) * chunk + p_row // 8 == p_col, 1.0, 0.0).astype(LOW)
    order_back = jnp.where((p_col % 8) * chunk + p_col // 8 == p_row, 1.0, 0.0).astype(LOW)

    def spread(tile):
        return jnp.concatenate([tile] * (width // 128), axis=-1)

    def span(i):
        return pl.ds(pl.multiple_of(i * BLOCK, BLOCK), BLOCK)

    def span_on(i):
        return pl.ds(pl.multiple_of(i * BLOCK + 8, 8), BLOCK)

    def tile(i):
        return pl.ds(pl.multiple_of(i * 8, 8), 8)

    def flat(ref):
        return ref[...].reshape(tokens_total, ref.shape[-1])

    def wide(j, base=0, size=WIDE):
        return pl.ds(pl.multiple_of(base + j * size, 128), size)

    def fold(block):
        return jnp.sum(block.reshape(rows * BLOCK // 8, 8, width), axis=0)

    def add_vector(level, row, block):
        vectors[level, row] += fold(block)

    def saving(name, level):
        if level == 0:
            pltpu.make_async_copy(act[name], store[name], save_sem.at[names.index(name)]).start()

    def saved(name, level):
        if level == 1:
            pltpu.make_async_copy(act[name], store[name], save_sem.at[names.index(name)]).wait()

    def loading(some):
        for name in some:
            pltpu.make_async_copy(store[name], act[name], load_sem.at[names.index(name)]).start()

    def loaded(name, level):
        if level == 0:
            pltpu.make_async_copy(store[name], act[name], load_sem.at[names.index(name)]).wait()

    def hop(index, device):
        return remote(small.at[0, index], small.at[1, index], s_send.at[index], s_recv.at[index], device)

    edge_count = 4 * layers

    def edge_start(index, step, there):
        @pl.when(there)
        def _():
            hop(index, pos.later(step)).start()

    def edge_wait(index, step, there):
        @pl.when(there)
        def _():
            hop(index, pos.later(step)).wait_recv()

    def edge_sent(index, step, there):
        @pl.when(there)
        def _():
            hop(index, pos.later(step)).wait_send()

    def chain_hop(level, direction, k):
        slot = edge_count + (level * 2 + direction) * 3
        return remote(
            small.at[0, slot],
            small.at[1, slot + k - 1],
            s_send.at[slot + k - 1],
            s_recv.at[slot + k - 1],
            pos.later(k if direction == 0 else -k),
        )

    def chain_do(level, direction, what):
        for k in range(1, 4):
            inside = s + k <= last if direction == 0 else s - k >= 0
            from_inside = s - k >= 0 if direction == 0 else s + k <= last

            @pl.when(from_inside if what == "wait_recv" else inside)
            def _():
                getattr(chain_hop(level, direction, k), what)()

    def chain_total(level, direction, r):
        slot = edge_count + (level * 2 + direction) * 3
        numer = jnp.zeros((1, width), F32)
        denom = jnp.zeros((1, width), F32)
        for k in (3, 2, 1):
            through = small[1, slot + k - 1, 3 * r : 3 * r + 1, :]
            numer = through * numer + small[1, slot + k - 1, 3 * r + 1 : 3 * r + 2, :]
            denom = through * denom + small[1, slot + k - 1, 3 * r + 2 : 3 * r + 3, :]
        return numer, denom

    def centred(x):
        center = x - jnp.mean(x, -1, keepdims=True)
        spread_ = jnp.mean(center * center, -1, keepdims=True)
        scale = lax.rsqrt(spread_ + EPSILON)
        return center * scale, scale

    def normalize_into(x_ref, level, which):
        gain, bias = ln_gain[level, which : which + 1, :], ln_bias[level, which : which + 1, :]

        @pl.loop(0, blocks)
        def _(i):
            n, _ = centred(x_ref[:, span(i), :])
            padded[:, span_on(i), :] = n * gain + bias

    def wrap_in(index):
        for r in range(rows):
            moved = pltpu.roll(padded[r, length : length + 8, :], 1, 0)
            padded[r, 0:8, :] = jnp.where(sub == 0, small[1, index, r : r + 1, :], moved)

    def normalize_shift(x_ref, level, which, outs, rates, unit):
        index = level * 2 + which
        normalize_into(x_ref, level, which)
        for r in range(rows):
            small[0, index, r : r + 1, :] = padded[r, length + 7 : length + 8, :]
        edge_start(index, 1, s < last)
        gather.need(unit)
        edge_wait(index, 1, s > 0)
        wrap_in(index)

        @pl.loop(0, blocks)
        def _(i):
            h = padded[:, span_on(i), :]
            before = padded[:, span(i), :] * spread(live[:, span(i), :])
            for out, j in zip(outs, rates):
                rate = mix[j, level : level + 1, :]
                out[:, span(i), :] = (h * rate + before * (1.0 - rate)).astype(LOW)

    def project(x_ref, w, base, count, put):
        for j in range(count // WIDE):
            block = w[:, :, :, base + j * WIDE : base + (j + 1) * WIDE].reshape(-1, WIDE)
            put(j, dot(flat(x_ref), block).reshape(rows, length, WIDE))

    def put_in(ref):
        def put(j, block):
            ref[:, :, wide(j)] = block

        return put

    def back_project(g_ref, w, base, count, out_ref):
        size = min(width, count)
        for j in range(count // size):
            block = w[:, :, :, base + j * size : base + (j + 1) * size].reshape(-1, size)
            got = dot_across(g_ref[:, :, j * size : (j + 1) * size].reshape(tokens_total, size), block)
            got = got.reshape(rows, length, width)
            if j == 0:
                out_ref[...] = got
            else:
                out_ref[...] += got

    def outer(x_ref, g_ref, w, base, count, g_base=0):
        turned[...] = flat(x_ref).T

        for j in range(count // WIDE):
            at = g_base + j * WIDE
            g = g_ref[:, :, at : at + WIDE].reshape(tokens_total, WIDE)
            got = dot(turned[...], g).astype(LOW)
            at = base + j * WIDE
            w[:, :, :, at : at + WIDE] = got.reshape(lines, 2, width // (2 * lines), WIDE)

    def keep_rows(level):
        rate = jnp.exp(decay[level : level + 1, :])
        return jnp.broadcast_to(jnp.exp(-rate), (8, width)), rate

    def scan_local(level):
        keep, _ = keep_rows(level)

        def step(i, carry):
            out = []
            for r in range(rows):
                numer, denom, alive = carry[3 * r : 3 * r + 3]
                l128 = live[r, tile(i), :]
                l_now = spread(l128)
                lifted = jnp.exp(act["key"][r, tile(i), :])
                numer = keep * (numer * l_now) + lifted * act["value"][r, tile(i), :]
                denom = keep * (denom * l_now) + lifted
                out += [numer, denom, alive * l128]
            return tuple(out)

        zero = jnp.zeros((8, width), F32)
        carry = lax.fori_loop(0, chunk, step, (zero, zero, jnp.ones((8, 128), F32)) * rows, unroll=2)
        faded = keep
        for _ in range(chunk.bit_length() - 1):
            faded = faded * faded
        slot = edge_count + (level * 2) * 3
        before = []
        for r in range(rows):
            numer, denom, alive = carry[3 * r : 3 * r + 3]
            through = spread(alive) * faded
            vec[level, r] = through
            for shift in (1, 2, 4):
                inside = sub >= shift
                n_b, d_b, t_b = (pltpu.roll(a, shift, 0) for a in (numer, denom, through))
                numer = jnp.where(inside, through * n_b + numer, numer)
                denom = jnp.where(inside, through * d_b + denom, denom)
                through = jnp.where(inside, through * t_b, through)
            for j, a in enumerate((through, numer, denom)):
                small[0, slot, 3 * r + j : 3 * r + j + 1, :] = a[7:8, :]
            at_start = sub == 0
            n_b, d_b, t_b = (pltpu.roll(a, 1, 0) for a in (numer, denom, through))
            before.append(
                (jnp.where(at_start, 0.0, n_b), jnp.where(at_start, 0.0, d_b), jnp.where(at_start, 1.0, t_b))
            )
        chain_do(level, 0, "start")
        return before

    def scan_final(level, before):
        chain_do(level, 0, "wait_recv")
        keep, _ = keep_rows(level)
        bonus = jnp.broadcast_to(jnp.exp(first[level : level + 1, :]), (8, width))
        carry = []
        for r in range(rows):
            n_in, d_in = chain_total(level, 0, r)
            n_b, d_b, t_b = before[r]
            carry += [t_b * n_in + n_b, t_b * d_in + d_b]

        def step(i, carry):
            out = []
            for r in range(rows):
                numer, denom = carry[2 * r : 2 * r + 2]
                l_now = spread(live[r, tile(i), :])
                numer, denom = numer * l_now, denom * l_now
                act["numer"][r, tile(i), :] = numer
                act["denom"][r, tile(i), :] = denom
                value = act["value"][r, tile(i), :]
                lifted = jnp.exp(act["key"][r, tile(i), :])
                now = bonus * lifted
                main[r, tile(i), :] = (numer + now * value) / (denom + now)
                out += [keep * numer + lifted * value, keep * denom + lifted]
            return tuple(out)

        lax.fori_loop(0, chunk, step, tuple(carry), unroll=2)

    for r in range(rows):
        act["x"][r] = dot(order, tokens[r])
        grad[r] = dot(order, cotangent[r])

    def forward_layer(level):
        w_kvr, w_out, w_fkey, w_frec, w_fval = weights[level]
        base = base_of[level]
        for name in ("xk", "xv", "xr"):
            saved(name, level)
        normalize_shift(act["x"], level, 0, [act["xk"], act["xv"], act["xr"]], (0, 1, 2), base)
        saving("x", level)
        for j, (low, name) in enumerate((("xk", "key"), ("xv", "value"), ("xr", "logit"))):
            saving(low, level)
            saved(name, level)
            gather.need(base + j)
            project(act[low], w_kvr, j * width, width, put_in(act[name]))
            saving(name, level)
            if j == 1:
                before = scan_local(level)
        saved("numer", level)
        saved("denom", level)
        scan_final(level, before)
        saving("numer", level)
        saving("denom", level)
        saved("gated", level)

        @pl.loop(0, blocks)
        def _(i):
            act["gated"][:, span(i), :] = (
                jax.nn.sigmoid(act["logit"][:, span(i), :]) * main[:, span(i), :]
            ).astype(LOW)

        saving("gated", level)
        gather.need(base + 3)
        saved("x1", level)

        def put_x1(j, block):
            act["x1"][:, :, wide(j)] = act["x"][:, :, wide(j)] + block

        project(act["gated"], w_out, 0, width, put_x1)
        saving("x1", level)
        saved("xk2", level)
        saved("xr2", level)
        normalize_shift(act["x1"], level, 1, [act["xk2"], act["xr2"]], (3, 4), base + 4)
        saving("xk2", level)
        saving("xr2", level)
        saved("squared", level)
        third = hidden // 3
        for j in range(3):
            gather.need(base + 4 + j)

            def put_squared(i, block, j=j):
                up = jnp.maximum(block, 0.0)
                act["squared"][:, :, wide(i, j * third)] = (up * up).astype(LOW)

            project(act["xk2"], w_fkey, j * third, third, put_squared)
        saving("squared", level)
        gather.need(base + 7)
        saved("recept", level)
        project(act["xr2"], w_frec, 0, width, put_in(act["recept"]))
        saving("recept", level)
        saved("value2", level)
        share = hidden // lines
        for j in range(width // WIDE):
            gather.need(base + 8 + j)
            total = None
            for z in range(lines):
                got = dot(
                    act["squared"][:, :, z * share : (z + 1) * share].reshape(tokens_total, share),
                    w_fval[z, :, :, j * WIDE : (j + 1) * WIDE].reshape(share, WIDE),
                )
                total = got if total is None else total + got
            act["value2"][:, :, j * WIDE : (j + 1) * WIDE] = total.reshape(rows, length, WIDE)
        saving("value2", level)
        saved("x", level + 1)

        @pl.loop(0, blocks)
        def _(i):
            up = jax.nn.sigmoid(act["recept"][:, span(i), :]) * act["value2"][:, span(i), :]
            after = act["x1"][:, span(i), :] + up
            if level + 1 < layers:
                act["x"][:, span(i), :] = after
            else:
                g_low3[:, span(i), :] = after.astype(LOW)

    for level in range(layers):
        forward_layer(level)
    def blend_back(level, which, d_refs, rates):
        index = level * 2 + which
        wrap_in(index)

        @pl.loop(0, blocks)
        def _(i):
            l_now = spread(live[:, span(i), :])
            change = padded[:, span_on(i), :] - padded[:, span(i), :] * l_now
            direct, shifted = None, None
            for ref, j in zip(d_refs, rates):
                d = ref[:, span(i), :]
                rate = mix[j, level : level + 1, :]
                add_vector(level, 2 + j, d * change)
                direct = d * rate if direct is None else direct + d * rate
                shifted = d * (1.0 - rate) if shifted is None else shifted + d * (1.0 - rate)
            main[:, span(i), :] = direct
            d_refs[0][:, span(i), :] = shifted * l_now

        back_index = 2 * layers + index
        for r in range(rows):
            small[0, back_index, r : r + 1, :] = d_refs[0][r, 0:1, :]
        edge_start(back_index, -1, s > 0)

    def normalize_back(level, which, x_ref, q_ref, write):
        index = level * 2 + which
        back_index = 2 * layers + index
        edge_wait(back_index, -1, s < last)
        for r in range(rows):
            moved = pltpu.roll(q_ref[r, 0:8, :], 7, 0)
            padded[r, length : length + 8, :] = jnp.where(
                sub == 7, small[1, back_index, r : r + 1, :], moved
            )
            padded[r, 8:length, :] = q_ref[r, 8:length, :]
        gain = ln_gain[level, which : which + 1, :]

        @pl.loop(0, blocks)
        def _(i):
            d_h = main[:, span(i), :] + padded[:, span_on(i), :]
            n, scale = centred(x_ref[:, span(i), :])
            add_vector(level, 7 + which, d_h * n)
            add_vector(level, 9 + which, d_h)
            e = d_h * gain
            inner = e - jnp.mean(e, -1, keepdims=True) - n * jnp.mean(e * n, -1, keepdims=True)
            after = grad[:, span(i), :] + scale * inner
            grad[:, span(i), :] = after
            write(i, after)

    def wkv_terms(r, i, bonus):
        value = act["value"][r, tile(i), :]
        lifted = jnp.exp(act["key"][r, tile(i), :])
        now = bonus * lifted
        numer, denom = act["numer"][r, tile(i), :], act["denom"][r, tile(i), :]
        part = 1.0 / (denom + now)
        result = (numer + now * value) * part
        return value, lifted, now, numer, denom, part, result

    def scan_back_local(level):
        keep, _ = keep_rows(level)
        bonus = jnp.broadcast_to(jnp.exp(first[level : level + 1, :]), (8, width))

        def step(j, carry):
            i = chunk - 1 - j
            out = []
            for r in range(rows):
                h_n, h_d = carry[2 * r : 2 * r + 2]
                value, lifted, now, numer, denom, part, result = wkv_terms(r, i, bonus)
                gate = jax.nn.sigmoid(act["logit"][r, tile(i), :])
                d_gated = main[r, tile(i), :]
                d_wkv = d_gated * gate
                d_two[r, tile(i), :] = d_gated * result * gate * (1.0 - gate)
                main[r, tile(i), :] = d_wkv
                l_now = spread(live[r, tile(i), :])
                a = d_wkv * part
                out += [l_now * (a + keep * h_n), l_now * (keep * h_d - a * result)]
            return tuple(out)

        zero = jnp.zeros((8, width), F32)
        carry = lax.fori_loop(0, chunk, step, (zero, zero) * rows)
        slot = edge_count + (level * 2 + 1) * 3
        after = []
        for r in range(rows):
            h_n, h_d = carry[2 * r : 2 * r + 2]
            through = vec[level, r]
            for shift in (1, 2, 4):
                inside = sub < 8 - shift
                n_a, d_a, t_a = (pltpu.roll(a, 8 - shift, 0) for a in (h_n, h_d, through))
                h_n = jnp.where(inside, through * n_a + h_n, h_n)
                h_d = jnp.where(inside, through * d_a + h_d, h_d)
                through = jnp.where(inside, through * t_a, through)
            for j, a in enumerate((through, h_n, h_d)):
                small[0, slot, 3 * r + j : 3 * r + j + 1, :] = a[0:1, :]
            at_end = sub == 7
            n_a, d_a, t_a = (pltpu.roll(a, 7, 0) for a in (h_n, h_d, through))
            after.append(
                (jnp.where(at_end, 0.0, n_a), jnp.where(at_end, 0.0, d_a), jnp.where(at_end, 1.0, t_a))
            )
        chain_do(level, 1, "start")
        return after

    def scan_back_final(level, after):
        chain_do(level, 1, "wait_recv")
        keep, rate = keep_rows(level)
        bonus = jnp.broadcast_to(jnp.exp(first[level : level + 1, :]), (8, width))
        zero = jnp.zeros((8, width), F32)
        carry = [zero, zero]
        for r in range(rows):
            n_in, d_in = chain_total(level, 1, r)
            n_a, d_a, t_a = after[r]
            carry += [t_a * n_in + n_a, t_a * d_in + d_a]

        def step(j, carry):
            i = chunk - 1 - j
            d_keep, d_first = carry[:2]
            out = []
            for r in range(rows):
                h_n, h_d = carry[2 + 2 * r : 4 + 2 * r]
                value, lifted, now, numer, denom, part, result = wkv_terms(r, i, bonus)
                a = main[r, tile(i), :] * part
                d_now = a * (value - result) * now
                d_keep = d_keep + numer * h_n + denom * h_d
                d_first = d_first + d_now
                d_one[r, tile(i), :] = d_now + lifted * (value * h_n + h_d)
                d_two[r, tile(i), :] = a * now + lifted * h_n
                l_now = spread(live[r, tile(i), :])
                out += [l_now * (a + keep * h_n), l_now * (keep * h_d - a * result)]
            return (d_keep, d_first, *out)

        carry = lax.fori_loop(0, chunk, step, tuple(carry))
        vectors[level, 0] += carry[0] * (-rate * keep)
        vectors[level, 1] += carry[1]

    def to_low(src, dst):
        @pl.loop(0, blocks)
        def _(i):
            dst[:, span(i), :] = src[:, span(i), :].astype(LOW)

    ffn_names = ("value2", "recept", "squared", "xk2", "xr2", "x1")
    att_names = tuple(n for n in names if n not in ffn_names)

    def serve(eager=False):
        reduce.serve(SITES[reduce.site], eager)
        reduce.site += 1

    def backward_layer(level):
        w_kvr, w_out, w_fkey, w_frec, w_fval = weights[level]
        base = (layers - 1 - level) * len(back)
        third = hidden // 3
        share = hidden // lines
        loaded("value2", level)
        loaded("recept", level)

        @pl.loop(0, blocks)
        def _(i):
            gate = jax.nn.sigmoid(act["recept"][:, span(i), :])
            g = grad[:, span(i), :]
            g_low[:, span(i), :] = (g * gate).astype(LOW)
            g_low2[:, span(i), :] = (g * act["value2"][:, span(i), :] * gate * (1.0 - gate)).astype(LOW)

        loaded("xr2", level)
        back_project(g_low2, w_frec, 0, width, d_two)
        gather.settle(len(gather.units))
        outer(act["xr2"], g_low2, w_frec, 0, width)
        reduce.emit(base)
        if level == layers - 1:
            for r in range(rows):
                output[r] = dot(order_back, g_low3[r]).astype(LOW)
        loaded("squared", level)

        for half_way in range(2):

            @pl.loop(half_way * (lines // 2), (half_way + 1) * (lines // 2))
            def _(z):
                got = dot_across(flat(g_low), w_fval[z].reshape(share, width))
                got = got.reshape(rows, length, share)
                root = jnp.sqrt(act["squared"][:, :, wide(z, 0, share)].astype(F32))
                g_key2[:, :, wide(z, 0, share)] = (got * (2.0 * root)).astype(LOW)

            serve(True)

        @pl.loop(0, lines)
        def _(z):
            turned[...] = act["squared"][:, :, wide(z, 0, share)].reshape(tokens_total, share).T
            for j in range(width // WIDE):
                g = g_low[:, :, j * WIDE : (j + 1) * WIDE].reshape(tokens_total, WIDE)
                got = dot(turned[...], g).astype(LOW)
                w_fval[z, :, :, j * WIDE : (j + 1) * WIDE] = got.reshape(2, share // 2, WIDE)

        for j in range(3):
            reduce.emit(base + 1 + j)
        serve()
        back_project(g_key2, w_fkey, 0, hidden, d_one)
        serve()
        loaded("xk2", level)
        for j in range(3):
            outer(act["xk2"], g_key2, w_fkey, j * third, third, j * third)
            reduce.emit(base + 4 + j)
            serve()
        loaded("x1", level)
        normalize_into(act["x1"], level, 1)
        blend_back(level, 1, [d_one, d_two], (3, 4))
        serve()

        def write_att(i, after):
            g_low3[:, span(i), :] = after.astype(LOW)

        normalize_back(level, 1, act["x1"], d_one, write_att)
        serve()
        if level == 1:
            loading(ffn_names)
        back_project(g_low3, w_out, 0, width, main)
        loaded("gated", level)
        outer(act["gated"], g_low3, w_out, 0, width)
        reduce.emit(base + 7)
        serve()
        for name in ("logit", "key", "value", "numer", "denom"):
            loaded(name, level)
        after = scan_back_local(level)
        serve()
        to_low(d_two, g_low)
        loaded("xr", level)
        back_project(g_low, w_kvr, 2 * width, width, d_three)
        outer(act["xr"], g_low, w_kvr, 2 * width, width)
        reduce.emit(base + 8)
        serve()
        scan_back_final(level, after)
        serve()
        to_low(d_one, g_low2)
        to_low(d_two, g_low3)
        loaded("xk", level)
        loaded("xv", level)
        back_project(g_low2, w_kvr, 0, width, d_one)
        outer(act["xk"], g_low2, w_kvr, 0, width)
        reduce.emit(base + 9)
        serve()
        back_project(g_low3, w_kvr, width, width, d_two)
        outer(act["xv"], g_low3, w_kvr, width, width)
        reduce.emit(base + 10)
        serve()
        loaded("x", level)
        normalize_into(act["x"], level, 0)
        blend_back(level, 0, [d_one, d_two, d_three], (0, 1, 2))
        serve()

        def write_none(i, after):
            g_low[:, span(i), :] = after.astype(LOW)

        normalize_back(level, 0, act["x"], d_one, write_none)
        serve()
        if level == 1:
            loading(att_names)

    for level in reversed(range(layers)):
        backward_layer(level)
    for r in range(rows):
        grad_tokens[r] = dot(order_back, g_low[r]).astype(LOW)

    count = vectors.shape[1]

    def vector_hop(j, device):
        source = min(j, 3)
        return remote(v_buf.at[0, source], v_buf.at[1, j], v_send.at[j], v_recv.at[j], device)

    def vector_stage(stage):
        if stage == 0:
            for level in range(layers):
                for row in range(count):
                    j = level * count + row
                    v_buf[0, 0, j : j + 1, :] = jnp.sum(vectors[level, row], axis=0, keepdims=True)
        elif stage < 4:
            vector_hop(stage - 1, pos.partner).wait_recv()
            v_buf[0, stage] = v_buf[0, stage - 1] + v_buf[1, stage - 1]
        if stage < 3:
            vector_hop(stage, (pos.partner, pos.first, pos.second)[stage]).start()
        elif stage == 3:
            for k in range(1, lines):
                vector_hop(2 + k, pos.along(k)).start()
        else:
            total = v_buf[0, 3]
            for k in range(1, lines):
                vector_hop(2 + k, pos.along(k)).wait_recv()
                total = total + v_buf[1, 2 + k]
            vector_out[...] = total

    for stage in range(5):
        vector_stage(stage)
        for _ in range(VECTOR_TURNS):
            reduce.turn()
    while not reduce.done():
        reduce.turn()
    reduce.settle(len(reduce.units))
    for j, device in enumerate((pos.partner, pos.first, pos.second)):
        vector_hop(j, device).wait_send()
    for k in range(1, lines):
        vector_hop(2 + k, pos.along(k)).wait_send()
    for level in range(layers):
        for which in range(2):
            index = level * 2 + which
            edge_sent(index, 1, s < last)
            edge_sent(2 * layers + index, -1, s > 0)
        for direction in range(2):
            chain_do(level, direction, "wait_send")


def finish_kernel(dims, *refs):
    layers, share, moved = dims
    ins, sums = refs[:moved], refs[moved]
    outs = refs[moved + 1 : 2 * moved + 1]
    decay, first, mix, gain, bias = refs[2 * moved + 1 : 2 * moved + 6]
    came = refs[2 * moved + 6 : 3 * moved + 6]
    wide = came[:2] + refs[3 * moved + 6 : 4 * moved + 4]
    in_sem, out_sem = refs[4 * moved + 4 :]
    parts = [(i, j) for i in range(moved) for j in range(layers)]

    def arrive(i, j):
        return pltpu.make_async_copy(ins[i].at[j], came[i].at[j], in_sem.at[i, j])

    def leave(i, j):
        return pltpu.make_async_copy(wide[i].at[j], outs[i].at[j], out_sem.at[i, j])

    for part in parts:
        arrive(*part).start()
    offset = lax.axis_index("dp") * share
    width = sums.shape[1]
    own = pltpu.roll(sums[...], lax.rem(width - offset, width), 1)[:, :share]
    for level in range(layers):
        at = level * 11
        decay[level : level + 1, :] = own[at : at + 1]
        first[level : level + 1, :] = own[at + 1 : at + 2]
        for j in range(5):
            mix[j, level : level + 1, :] = own[at + 2 + j : at + 3 + j]
        for j in range(2):
            gain[level, j : j + 1, :] = own[at + 7 + j : at + 8 + j]
            bias[level, j : j + 1, :] = own[at + 9 + j : at + 10 + j]
    for i, j in parts:
        arrive(i, j).wait()
        if i >= 2:
            rows = ins[i].shape[1]

            @pl.loop(0, rows // 16)
            def _(k):
                at = pl.ds(pl.multiple_of(k * 16, 16), 16)
                wide[i][j, at, :] = came[i][j, at, :].astype(F32)

        leave(i, j).start()
    for part in parts:
        leave(*part).wait()


def fast_body(
    tokens, doc_starts, decay, first, mix, ln_gain, ln_bias,
    att_kvr, att_out, ffn_key, ffn_recept, ffn_value, cotangent,
):
    rows, length, width = tokens.shape
    layers, hidden = decay.shape[0], ffn_key.shape[2]
    lines = lax.axis_size("dp") // 2
    shards = (att_kvr, att_out, ffn_key, ffn_recept, ffn_value)
    plain, low = (rows, length, width), LOW
    saved = [jax.ShapeDtypeStruct(plain, F32)] * len(SAVED)
    saved += [jax.ShapeDtypeStruct(plain, low)] * len(SAVED_LOW)
    saved += [jax.ShapeDtypeStruct((rows, length, hidden), low)]
    vector_rows = -(-layers * 11 // 8) * 8
    outs = [
        jax.ShapeDtypeStruct(plain, low),
        jax.ShapeDtypeStruct(plain, low),
        jax.ShapeDtypeStruct((vector_rows, width), F32),
    ]
    outs += [jax.ShapeDtypeStruct(w.shape, low) for w in shards]
    outs += saved
    vmem, anywhere = pl.BlockSpec(memory_space=pltpu.VMEM), pl.BlockSpec(memory_space=pl.ANY)
    units = 11 * layers + FIRST_PIECES - 1
    hops = 4 * layers + 6 * layers
    dma, plain_f32, plain_low = pltpu.SemaphoreType.DMA, pltpu.VMEM(plain, F32), pltpu.VMEM(plain, low)
    scratch = [pltpu.VMEM((lines, 2) + w.shape[1:], low) for _ in range(layers) for w in shards]
    scratch += [pltpu.VMEM((lines,) + w.shape[1:], low) for w in shards]
    scratch += [pltpu.VMEM(a.shape, a.dtype) for a in saved]
    scratch += [
        pltpu.VMEM((rows, length, 128), F32),
        pltpu.VMEM((rows, length + 8, width), F32),
        plain_f32,
        plain_f32,
        plain_f32,
        plain_f32,
        plain_f32,
        plain_low,
        plain_low,
        plain_low,
        pltpu.VMEM((rows, length, hidden), low),
        pltpu.VMEM((width, rows * length), low),
        pltpu.VMEM((layers, 11, 8, width), F32),
        pltpu.VMEM((2, hops, 8, width), F32),
        pltpu.VMEM((layers, rows, 8, width), F32),
        pltpu.VMEM((2, 6, vector_rows, width), F32),
        dma((units, 3 * lines - 2)),
        dma((units, 3 * lines - 2)),
        dma((layers, len(shards))),
        dma((units, 5 + lines)),
        dma((units, 5 + lines)),
        pltpu.SemaphoreType.REGULAR((units, 1 + lines)),
        pltpu.SemaphoreType.REGULAR((11,)),
        dma((units, 2)),
        dma((len(saved),)),
        dma((len(saved),)),
        dma((hops,)),
        dma((hops,)),
        dma((6,)),
        dma((6,)),
    ]
    smem = pl.BlockSpec(memory_space=pltpu.SMEM)
    got = pl.pallas_call(
        functools.partial(train_kernel, (layers, lines, rows, length, width, hidden)),
        out_shape=outs,
        in_specs=[vmem, smem] + [vmem] * 5 + [anywhere] * len(shards) + [vmem],
        out_specs=[vmem] * 3 + [anywhere] * (len(outs) - 3),
        scratch_shapes=scratch,
        compiler_params=pltpu.CompilerParams(
            collective_id=0, has_side_effects=True, vmem_limit_bytes=VMEM_BYTES
        ),
    )(tokens, doc_starts, decay, first, jnp.swapaxes(mix, 0, 1), ln_gain, ln_bias, *shards, cotangent)
    share = width // lax.axis_size("dp")
    final = [jax.ShapeDtypeStruct(plain, low)] * 2
    final += [jax.ShapeDtypeStruct(w.shape, F32) for w in shards]
    final += [jax.ShapeDtypeStruct((layers, share), F32)] * 2
    final += [jax.ShapeDtypeStruct((5, layers, share), F32)]
    final += [jax.ShapeDtypeStruct((layers, 2, share), F32)] * 2
    moved = 2 + len(shards)
    done = pl.pallas_call(
        functools.partial(finish_kernel, (layers, share, moved)),
        out_shape=final,
        in_specs=[anywhere] * moved + [vmem],
        out_specs=[anywhere] * moved + [vmem] * 5,
        scratch_shapes=[pltpu.VMEM(a.shape, low) for a in final[:moved]]
        + [pltpu.VMEM(a.shape, F32) for a in final[2:moved]]
        + [dma((moved, layers)), dma((moved, layers))],
        compiler_params=pltpu.CompilerParams(vmem_limit_bytes=VMEM_BYTES),
    )(got[0], got[1], *got[3 : 3 + len(shards)], got[2])
    output, grad_tokens = done[:2]
    g_decay, g_first, g_mix, g_gain, g_bias = done[moved:]
    return (
        output,
        grad_tokens,
        g_decay,
        g_first,
        jnp.swapaxes(g_mix, 0, 1),
        g_gain,
        g_bias,
        *done[2:moved],
    )


def kernel_fits(tokens, decay, ffn_key, shards):
    rows, length, width = tokens.shape
    lines = lax.axis_size("dp") // 2
    return (
        lax.axis_size("seq") == 4
        and lax.axis_size("dp") == 2 * lines
        and lines > 1
        and decay.shape[0] == 2
        and rows == 2
        and length % BLOCK == 0
        and length & (length - 1) == 0
        and width % WIDE == 0
        and ffn_key.shape[2] == width * lines
        and all(w.shape[1] % 32 == 0 and w.shape[2] % WIDE == 0 for w in shards)
    )


def from_behind(block, axis, distance):
    devices = range(lax.axis_size(axis))
    route = [(i - distance, i) for i in devices if i - distance in devices]
    return lax.ppermute(block, axis, route)


def normalize(stream, gain_row, bias_row):
    center = stream - jnp.mean(stream, -1, keepdims=True)
    spread = jnp.mean(center * center, -1, keepdims=True)
    return center * lax.rsqrt(spread + EPSILON) * gain_row + bias_row


def blend(hidden, edge_row, rates, starts):
    earlier = (
        jnp.concatenate([edge_row[:, None, :], hidden[:, :-1, :]], axis=1)
        * (1.0 - starts)[:, :, None]
    )
    return tuple((hidden * rates[j] + earlier * (1.0 - rates[j]) for j in range(rates.shape[0])))


def product(inputs, matrix):
    return jnp.einsum("rcd,de->rce", inputs, matrix, preferred_element_type=jnp.float32)


def product_back(grads, matrix):
    return jnp.einsum("rce,de->rcd", grads, matrix, preferred_element_type=jnp.float32)


def outer_sum(inputs, grads):
    return jnp.einsum("rcd,rce->de", inputs, grads, preferred_element_type=jnp.float32)


def wkv_tokens(key_proj, value_proj, decay_row, foremost_line_entry, numer_in, denom_in, starts):
    rows, length, width = key_proj.shape
    block = math.gcd(length, 64)
    count = length // block
    rate = jnp.exp(decay_row)
    local = jnp.arange(block, dtype=jnp.float32)
    lower = (local[:, None] > local[None, :]).astype(jnp.float32)
    grow = jnp.exp(local[:, None] * rate[None, :])
    shrink = jnp.exp(-(local[:, None] - 1.0) * rate[None, :])
    fade = jnp.exp(-local[:, None] * rate[None, :])
    keep_rate = jnp.exp(-rate)

    def one_block(carry, inputs):
        accrued_dividend_total, accrued_divisor_total = carry
        present_lookup_entry, present_payload_entry, start_now = inputs
        counted = jnp.cumsum(start_now, axis=1)
        same = lower[None] * (counted[:, :, None] == counted[:, None, :]).astype(jnp.float32)
        alive = (counted == 0.0).astype(jnp.float32)[:, :, None]
        key_exp = jnp.exp(present_lookup_entry)
        lifted = grow[None] * key_exp
        numer_sum = jnp.einsum(
            "rji,ric->rjc", same, lifted * present_payload_entry, precision=lax.Precision.HIGHEST
        )
        denom_sum = jnp.einsum("rji,ric->rjc", same, lifted, precision=lax.Precision.HIGHEST)
        present_dividend_term = (
            shrink[None] * numer_sum + fade[None] * alive * accrued_dividend_total[:, None, :]
        )
        present_divisor_term = (
            shrink[None] * denom_sum + fade[None] * alive * accrued_divisor_total[:, None, :]
        )
        present_reward_term = jnp.exp(foremost_line_entry + present_lookup_entry)
        recurrence_result = (
            present_dividend_term + present_reward_term * present_payload_entry
        ) / (present_divisor_term + present_reward_term)
        numer_end = (
            keep_rate * present_dividend_term[:, -1] + key_exp[:, -1] * present_payload_entry[:, -1]
        )
        denom_end = keep_rate * present_divisor_term[:, -1] + key_exp[:, -1]
        return ((numer_end, denom_end), recurrence_result)

    def split(values):
        return jnp.swapaxes(values.reshape((rows, count, block) + values.shape[2:]), 0, 1)

    carry_end, results = lax.scan(
        one_block, (numer_in, denom_in), (split(key_proj), split(value_proj), split(starts))
    )
    return jnp.swapaxes(results, 0, 1).reshape(rows, length, width)


def span_transform(key_proj, value_proj, decay_row, starts):
    length = key_proj.shape[1]
    rate = jnp.exp(decay_row)
    steps = jnp.arange(length, dtype=jnp.float32)
    last_start = jnp.max(steps[None, :] * starts, axis=1)
    after = (steps[None, :] >= last_start[:, None]).astype(jnp.float32)
    weight = jnp.exp(key_proj - (length - 1.0 - steps)[None, :, None] * rate) * after[:, :, None]
    carry_numer = jnp.sum(weight * value_proj, axis=1)
    carry_denom = jnp.sum(weight, axis=1)
    through = jnp.prod(1.0 - starts, axis=1)[:, None] * jnp.exp(-length * rate)[None, :]
    return (through, carry_numer, carry_denom)


def body(
    tokens,
    doc_starts,
    decay,
    first,
    mix,
    ln_gain,
    ln_bias,
    att_kvr,
    att_out,
    ffn_key,
    ffn_recept,
    ffn_value,
    cotangent,
):
    shards = (att_kvr, att_out, ffn_key, ffn_recept, ffn_value)
    if kernel_fits(tokens, decay, ffn_key, shards):
        return fast_body(
            tokens, doc_starts, decay, first, mix, ln_gain, ln_bias, *shards, cotangent
        )
    row_total, token_total, width = tokens.shape
    layer_total = decay.shape[0]
    batches = 2
    per_batch = row_total // batches
    positions = lax.axis_index("seq") * token_total + jnp.arange(token_total, dtype=jnp.int32)
    starts_all = jnp.any(doc_starts[:, :, None] == positions[None, None, :], axis=1).astype(
        jnp.float32
    )
    empty = jnp.zeros((per_batch, width), jnp.float32)

    def edge_of(hidden):
        return from_behind(hidden[:, -1, :], "seq", 1)

    def edge_back(grad_edge):
        return from_behind(grad_edge, "seq", -1)

    def chain_forward(through, carry_numer, carry_denom):
        incoming = (empty, empty)
        sent_numer, sent_denom = (carry_numer, carry_denom)
        for relay_turn in range(lax.axis_size("seq") - 1):
            incoming = from_behind((sent_numer, sent_denom), "seq", 1)
            sent_numer = through * incoming[0] + carry_numer
            sent_denom = through * incoming[1] + carry_denom
        return incoming

    def forward_layer(stream, level, matrices, starts):
        w_kvr, w_out, w_fkey, w_frec, w_fval = matrices
        hidden, norm_one = jax.vjp(normalize, stream, ln_gain[level, 0], ln_bias[level, 0])
        edge_row = edge_of(hidden)
        blends, blend_one = jax.vjp(
            lambda h_in, e_in, r_in: blend(h_in, e_in, r_in, starts),
            hidden,
            edge_row,
            mix[level, :3],
        )
        xk_low, xv_low, xr_low = [b.astype(jnp.bfloat16) for b in blends]
        key_proj = product(xk_low, w_kvr[:, :width])
        value_proj = product(xv_low, w_kvr[:, width : 2 * width])
        logit = product(xr_low, w_kvr[:, 2 * width :])
        transform, transform_one = jax.vjp(
            lambda k_in, v_in, d_in: span_transform(k_in, v_in, d_in, starts),
            key_proj,
            value_proj,
            decay[level],
        )
        numer_in, denom_in = chain_forward(transform[0], transform[1], transform[2])
        mixed, tokens_one = jax.vjp(
            lambda k_in, v_in, d_in, f_in, n_in, z_in: wkv_tokens(
                k_in, v_in, d_in, f_in, n_in, z_in, starts
            ),
            key_proj,
            value_proj,
            decay[level],
            first[level],
            numer_in,
            denom_in,
        )
        gated, gate_one = jax.vjp(lambda g_in, m_in: jax.nn.sigmoid(g_in) * m_in, logit, mixed)
        gated_low = gated.astype(jnp.bfloat16)
        middle = stream + product(gated_low, w_out)
        hidden_two, norm_two = jax.vjp(normalize, middle, ln_gain[level, 1], ln_bias[level, 1])
        edge_two = edge_of(hidden_two)
        blends_two, blend_two = jax.vjp(
            lambda h_in, e_in, r_in: blend(h_in, e_in, r_in, starts),
            hidden_two,
            edge_two,
            mix[level, 3:],
        )
        xk2_low, xr2_low = [b.astype(jnp.bfloat16) for b in blends_two]
        key_two = product(xk2_low, w_fkey)
        squared, square_one = jax.vjp(lambda k_in: jnp.square(jax.nn.relu(k_in)), key_two)
        squared_low = squared.astype(jnp.bfloat16)
        value_two = product(squared_low, w_fval)
        recept = product(xr2_low, w_frec)
        branch, branch_one = jax.vjp(
            lambda r_in, v_in: jax.nn.sigmoid(r_in) * v_in, recept, value_two
        )
        record = (
            norm_one,
            blend_one,
            xk_low,
            xv_low,
            xr_low,
            transform[0],
            numer_in,
            denom_in,
            transform_one,
            tokens_one,
            gate_one,
            gated_low,
            norm_two,
            blend_two,
            xk2_low,
            xr2_low,
            square_one,
            squared_low,
            branch_one,
        )
        return (middle + branch, record)

    gathered = []
    for level in range(layer_total):
        gathered.append(
            (
                lax.all_gather(att_kvr[level], "dp", axis=0, tiled=True),
                lax.all_gather(att_out[level], "dp", axis=0, tiled=True),
                lax.all_gather(ffn_key[level], "dp", axis=0, tiled=True),
                lax.all_gather(ffn_recept[level], "dp", axis=0, tiled=True),
                lax.all_gather(ffn_value[level], "dp", axis=0, tiled=True),
            )
        )
    pair_lists = [[] for level in range(layer_total)]
    vector_sums = [None] * layer_total
    outputs = []
    grad_parts = []
    for batch in range(batches):
        low_row = batch * per_batch
        starts = starts_all[low_row : low_row + per_batch]
        stream = tokens[low_row : low_row + per_batch].astype(jnp.float32)
        records = []
        for level in range(layer_total):
            stream, record = forward_layer(stream, level, gathered[level], starts)
            records.append(record)
        outputs.append(stream.astype(jnp.bfloat16))
        gradient = cotangent[low_row : low_row + per_batch].astype(jnp.float32)
        for level in reversed(range(layer_total)):
            backward_w_kvr, backward_w_out, backward_w_fkey, backward_w_frec, backward_w_fval = (
                gathered[level]
            )
            (
                backward_norm_one,
                backward_blend_one,
                backward_xk_low,
                backward_xv_low,
                backward_xr_low,
                backward_through,
                backward_numer_in,
                backward_denom_in,
                backward_transform_one,
                backward_tokens_one,
                backward_gate_one,
                backward_gated_low,
                backward_norm_two,
                backward_blend_two,
                backward_xk2_low,
                backward_xr2_low,
                backward_square_one,
                backward_squared_low,
                backward_branch_one,
            ) = records[level]
            d_recept, d_value_two = backward_branch_one(gradient)
            g_value_two = d_value_two.astype(jnp.bfloat16)
            g_recept = d_recept.astype(jnp.bfloat16)
            (d_key_two,) = backward_square_one(product_back(g_value_two, backward_w_fval))
            g_key_two = d_key_two.astype(jnp.bfloat16)
            d_hidden_two, d_edge_two, d_rates_two = backward_blend_two(
                (product_back(g_key_two, backward_w_fkey), product_back(g_recept, backward_w_frec))
            )
            d_hidden_two = d_hidden_two.at[:, -1, :].add(edge_back(d_edge_two))
            d_middle_norm, d_gain_two, d_bias_two = backward_norm_two(d_hidden_two)
            d_middle = gradient + d_middle_norm
            g_att = d_middle.astype(jnp.bfloat16)
            d_logit, d_mixed = backward_gate_one(product_back(g_att, backward_w_out))
            g_logit = d_logit.astype(jnp.bfloat16)
            (
                d_key_one,
                d_value_one,
                d_decay_one,
                d_first,
                backward_direct_numer,
                backward_direct_denom,
            ) = backward_tokens_one(d_mixed)
            chain_incoming = (empty, empty)
            chain_sent_numer = backward_direct_numer
            chain_sent_denom = backward_direct_denom
            for chain_relay_turn in range(lax.axis_size("seq") - 1):
                chain_incoming = from_behind((chain_sent_numer, chain_sent_denom), "seq", -1)
                chain_sent_numer = backward_through * chain_incoming[0] + backward_direct_numer
                chain_sent_denom = backward_through * chain_incoming[1] + backward_direct_denom
            g_numer_out, g_denom_out = chain_incoming
            d_key_two_part, d_value_two_part, d_decay_two = backward_transform_one(
                (
                    g_numer_out * backward_numer_in + g_denom_out * backward_denom_in,
                    g_numer_out,
                    g_denom_out,
                )
            )
            g_key = (d_key_one + d_key_two_part).astype(jnp.bfloat16)
            g_value = (d_value_one + d_value_two_part).astype(jnp.bfloat16)
            d_blends = (
                product_back(g_key, backward_w_kvr[:, :width]),
                product_back(g_value, backward_w_kvr[:, width : 2 * width]),
                product_back(g_logit, backward_w_kvr[:, 2 * width :]),
            )
            d_hidden, d_edge, d_rates = backward_blend_one(d_blends)
            d_hidden = d_hidden.at[:, -1, :].add(edge_back(d_edge))
            d_stream_norm, d_gain_one, d_bias_one = backward_norm_one(d_hidden)
            pairs = (
                (backward_xk2_low, g_key_two),
                (backward_xr2_low, g_recept),
                (backward_squared_low, g_value_two),
                (backward_xk_low, g_key),
                (backward_xv_low, g_value),
                (backward_xr_low, g_logit),
                (backward_gated_low, g_att),
            )
            columns = (
                [d_decay_one + d_decay_two, d_first]
                + [d_rates[j] for j in range(3)]
                + [d_rates_two[j] for j in range(2)]
                + [d_gain_one, d_gain_two, d_bias_one, d_bias_two]
            )
            backward_vectors = jnp.stack(columns, axis=1)
            gradient, pairs, vectors = (d_middle + d_stream_norm, pairs, backward_vectors)
            pair_lists[level].append(pairs)
            vector_sums[level] = (
                vectors if vector_sums[level] is None else vector_sums[level] + vectors
            )
        grad_parts.append(gradient.astype(jnp.bfloat16))
    results = [None] * layer_total
    for level in reversed(range(layer_total)):
        pair_list = pair_lists[level]

        def summed(index):
            inputs = jnp.concatenate([p[index][0] for p in pair_list], axis=0)
            grads = jnp.concatenate([p[index][1] for p in pair_list], axis=0)
            return outer_sum(inputs, grads)

        ffn_part = (summed(0), summed(1), summed(2))
        finish_grad_kvr = jnp.concatenate([summed(3), summed(4), summed(5)], axis=1)
        totals = (
            lax.psum(
                lax.psum_scatter(ffn_part[0], "dp", scatter_dimension=0, tiled=True).astype(
                    jnp.bfloat16
                ),
                "seq",
            ).astype(jnp.float32),
            lax.psum(
                lax.psum_scatter(ffn_part[1], "dp", scatter_dimension=0, tiled=True).astype(
                    jnp.bfloat16
                ),
                "seq",
            ).astype(jnp.float32),
            lax.psum(
                lax.psum_scatter(ffn_part[2], "dp", scatter_dimension=0, tiled=True).astype(
                    jnp.bfloat16
                ),
                "seq",
            ).astype(jnp.float32),
            lax.psum(
                lax.psum_scatter(finish_grad_kvr, "dp", scatter_dimension=0, tiled=True).astype(
                    jnp.bfloat16
                ),
                "seq",
            ).astype(jnp.float32),
            lax.psum(
                lax.psum_scatter(summed(6), "dp", scatter_dimension=0, tiled=True).astype(
                    jnp.bfloat16
                ),
                "seq",
            ).astype(jnp.float32),
            lax.psum(
                lax.psum_scatter(vector_sums[level], "dp", scatter_dimension=0, tiled=True).astype(
                    jnp.bfloat16
                ),
                "seq",
            ).astype(jnp.float32),
        )
        ffn_part = (totals[0], totals[1], totals[2])
        att_part = (totals[3], totals[4], totals[5])
        results[level] = (ffn_part, att_part)
    output = jnp.concatenate(outputs, axis=0)
    grad_tokens = jnp.concatenate(grad_parts, axis=0)
    grad_ffn_key = jnp.stack([r[0][0] for r in results])
    grad_ffn_recept = jnp.stack([r[0][1] for r in results])
    grad_ffn_value = jnp.stack([r[0][2] for r in results])
    grad_kvr = jnp.stack([r[1][0] for r in results])
    grad_att_out = jnp.stack([r[1][1] for r in results])
    vector_rows = jnp.stack([r[1][2] for r in results])
    grad_decay = vector_rows[:, :, 0]
    grad_first = vector_rows[:, :, 1]
    grad_mix = jnp.swapaxes(vector_rows[:, :, 2:7], 1, 2)
    grad_gain = jnp.swapaxes(vector_rows[:, :, 7:9], 1, 2)
    grad_bias = jnp.swapaxes(vector_rows[:, :, 9:11], 1, 2)
    return (
        output,
        grad_tokens,
        grad_decay,
        grad_first,
        grad_mix,
        grad_gain,
        grad_bias,
        grad_kvr,
        grad_att_out,
        grad_ffn_key,
        grad_ffn_recept,
        grad_ffn_value,
    )


def solution(mesh):
    in_specs = (
        P("dp", "seq", None),
        P("dp", None),
        P(),
        P(),
        P(),
        P(),
        P(),
        P(None, "dp", None),
        P(None, "dp", None),
        P(None, "dp", None),
        P(None, "dp", None),
        P(None, "dp", None),
        P("dp", "seq", None),
    )
    out_specs = (
        P("dp", "seq", None),
        P("dp", "seq", None),
        P(None, "dp"),
        P(None, "dp"),
        P(None, None, "dp"),
        P(None, None, "dp"),
        P(None, None, "dp"),
        P(None, "dp", None),
        P(None, "dp", None),
        P(None, "dp", None),
        P(None, "dp", None),
        P(None, "dp", None),
    )
    return jax.shard_map(body, mesh=mesh, in_specs=in_specs, out_specs=out_specs, check_vma=False)
```

```python
import functools
import math

import jax
import jax.numpy as jnp
from jax import lax
from jax.experimental import pallas as pl
from jax.experimental.pallas import tpu as pltpu
from jax.sharding import PartitionSpec as P

EPSILON = 1e-05
MESH = pl.DeviceIdType.MESH
F32, LOW = jnp.float32, jnp.bfloat16


class Place:
    def __init__(self, lines):
        self.lines = lines
        s, d = lax.axis_index("seq"), lax.axis_index("dp")
        self.s, self.d = s, d
        self.c, self.z = lax.rem(d, 2), d // 2
        x, y, c = lax.rem(s, 2), s // 2, self.c
        self.f = x * (1 - c) + y * c
        self.g = y * (1 - c) + x * c
        flip_x, flip_y = s + 1 - 2 * x, s + 2 - 4 * y
        self.first = (flip_x * (1 - c) + flip_y * c, d)
        self.second = (flip_y * (1 - c) + flip_x * c, d)
        self.across = (3 - s, d)
        self.partner = (s, d + 1 - 2 * c)

    def line(self, k):
        return lax.rem(self.z + k + self.lines, self.lines)

    def along(self, k):
        return (self.s, self.line(k) * 2 + self.c)

    def later(self, k):
        return (self.s + k, self.d)


def remote(src, dst, send, recv, device):
    return pltpu.make_async_remote_copy(
        src_ref=src, dst_ref=dst, send_sem=send, recv_sem=recv, device_id=device, device_id_type=MESH
    )


def signal(semaphore, device):
    pl.semaphore_signal(semaphore, inc=1, device_id=device, device_id_type=MESH)


def half(start, size, which, align):
    return pl.ds(pl.multiple_of(start + which * (size // 2), align), size // 2)


class Gather:
    def __init__(self, pos, units, send, recv, ahead):
        self.pos, self.units, self.ahead = pos, units, ahead
        self.turns = self.settled = 0
        lines = pos.lines
        self.stages = []
        self.plan, self.ready = {}, []
        for u in reversed(range(len(units))):
            at = u
            for stage, lag in enumerate((0, *GATHER_LAGS)):
                at += lag
                self.plan.setdefault(at, []).append((stage, u))
            self.ready.insert(0, at)
        for u, (w, (r0, rows, c0, cols), _) in enumerate(units):
            gh, fh = half(r0, rows, pos.g, 16), half(c0, cols, pos.f, 128)
            ar, ac = pl.ds(r0, rows), pl.ds(c0, cols)
            stages = [[], [], [], []]
            for k in range(1, lines):
                far = pos.line(-k)
                own = w.at[pos.z, pos.c, gh, fh]
                stages[0].append(remote(own, own, send.at[u, k - 1], recv.at[u, k - 1], pos.along(k)))
                j = lines - 1 + k - 1
                block = w.at[far, pos.c, gh, fh]
                stages[1].append(remote(block, block, send.at[u, j], recv.at[u, j], pos.second))
                j = 2 * (lines - 1) + k - 1
                block = w.at[far, pos.c, ar, fh]
                stages[2].append(remote(block, block, send.at[u, j], recv.at[u, j], pos.first))
            j = 3 * (lines - 1)
            block = w.at[:, pos.c, ar, ac]
            stages[3].append(remote(block, block, send.at[u, j], recv.at[u, j], pos.partner))
            self.stages.append(stages)

    def begin(self, u):
        if u < len(self.units):
            own = self.units[u][2]
            if own is not None:
                own.wait()
            for copy in self.stages[u][0]:
                copy.start()

    def turn(self):
        turn = self.turns
        self.turns += 1
        self.begin(turn + self.ahead)
        for stage, u in self.plan.get(turn, ()):
            for i, copy in enumerate(self.stages[u][stage]):
                copy.wait_recv()
                if stage < 2:
                    self.stages[u][stage + 1][i].start()
            if stage == 2:
                self.stages[u][3][0].start()
        self.settle(turn - sum(GATHER_LAGS) - 1)

    def need(self, u):
        while self.turns <= self.ready[u]:
            self.turn()

    def settle(self, count):
        while self.settled < min(count, len(self.units)):
            for stage in self.stages[self.settled]:
                for copy in stage:
                    copy.wait_send()
            self.settled += 1


class Reduce:
    def __init__(self, pos, units, shared, send, recv, free, credit, local):
        self.pos, self.units, self.shared = pos, units, shared
        self.send, self.recv, self.free, self.credit, self.local = send, recv, free, credit, local
        self.turns = self.emitted = self.cleared = self.paired = self.mark = self.settled = 0
        self.copies = {}
        self.steps = self.plan()
        self.site = 0

    def copy(self, u, j, src, dst, device):
        made = remote(src, dst, self.send.at[u, j], self.recv.at[u, j], device)
        self.copies[u, j] = made
        made.start()

    def views(self, u):
        w, landing, out, (r0, rows, c0, cols), _ = self.units[u]
        pos = self.pos
        v = {
            "ar": pl.ds(r0, rows),
            "ac": pl.ds(c0, cols),
            "gh": half(r0, rows, pos.g, 16),
            "go": half(r0, rows, 1 - pos.g, 16),
            "fh": half(c0, cols, pos.f, 128),
            "fo": half(c0, cols, 1 - pos.f, 128),
            "r0": pl.ds(r0, rows // 2),
            "r1": pl.ds(r0 + rows // 2, rows // 2),
            "c0": pl.ds(c0, cols // 2),
            "c1": pl.ds(c0 + cols // 2, cols // 2),
        }
        return w, landing, out, v

    def emit(self, u):
        w, landing, _, v = self.views(u)
        pos = self.pos
        assert u == self.emitted
        self.emitted += 1
        if u >= self.shared:
            pl.semaphore_wait(self.credit.at[u - self.shared], 1)
        self.copy(
            u, 0, w.at[:, 1 - pos.c, v["ar"], v["ac"]], landing.at[:, v["ar"], v["ac"]], pos.partner
        )

    def clear(self, u):
        pos = self.pos
        self.copies[u, 0].wait_send()
        signal(self.free.at[u, 0], pos.first)
        signal(self.free.at[u, 1], pos.second)
        for k in range(1, pos.lines):
            signal(self.free.at[u, 1 + k], pos.along(-k))

    def pair(self, u):
        w, landing, _, v = self.views(u)
        pos, c = self.pos, self.pos.c
        self.copies[u, 0].wait_recv()

        @pl.loop(0, pos.lines)
        def _(z):
            w[z, c, v["ar"], v["ac"]] += landing[z, v["ar"], v["ac"]]

        if u < self.shared:
            signal(self.credit.at[u], pos.partner)
        if self.units[u][4]:
            for k in range(1, pos.lines):
                pl.semaphore_wait(self.free.at[u, 1 + k], 1)
                self.copy(
                    u,
                    2 + k,
                    w.at[pos.line(k), c, v["ar"], v["ac"]],
                    w.at[k - 1, 1 - c, v["ar"], v["ac"]],
                    pos.along(k),
                )
            return
        pl.semaphore_wait(self.free.at[u, 0], 1)
        self.copy(u, 1, w.at[:, c, v["ar"], v["fo"]], w.at[:, 1 - c, v["ar"], v["c0"]], pos.first)

    def one(self, u):
        w, _, _, v = self.views(u)
        pos, c = self.pos, self.pos.c
        self.copies[u, 1].wait_recv()

        @pl.loop(0, pos.lines)
        def _(z):
            w[z, c, v["ar"], v["fh"]] += w[z, 1 - c, v["ar"], v["c0"]]

        pl.semaphore_wait(self.free.at[u, 1], 1)
        self.copy(u, 2, w.at[:, c, v["go"], v["fh"]], w.at[:, 1 - c, v["r0"], v["c1"]], pos.second)

    def two(self, u):
        w, _, _, v = self.views(u)
        pos, c = self.pos, self.pos.c
        self.copies[u, 2].wait_recv()

        @pl.loop(0, pos.lines)
        def _(z):
            w[z, c, v["gh"], v["fh"]] += w[z, 1 - c, v["r0"], v["c1"]]

        for k in range(1, pos.lines):
            pl.semaphore_wait(self.free.at[u, 1 + k], 1)
            self.copy(
                u,
                2 + k,
                w.at[pos.line(k), c, v["gh"], v["fh"]],
                w.at[k - 1, 1 - c, v["r1"], v["c1"]],
                pos.along(k),
            )

    def line(self, u):
        w, _, out, v = self.views(u)
        pos, c, lines = self.pos, self.pos.c, self.pos.lines
        for k in range(1, lines):
            self.copies[u, 2 + k].wait_recv()
        total = w[pos.z, c, v["gh"], v["fh"]].astype(F32)
        for k in range(1, lines):
            total = total + w[k - 1, 1 - c, v["r1"], v["c1"]].astype(F32)
        w[pos.z, c, v["gh"], v["fh"]] = total.astype(LOW)
        self.spread(u)

    def keep(self, u, j, src, there):
        made = pltpu.make_async_copy(src, there, self.local.at[u, j])
        self.copies[u, "local", j] = made
        made.start()

    def spread(self, u):
        w, _, out, v = self.views(u)
        pos, c, lines = self.pos, self.pos.c, self.pos.lines
        mine, there = w.at[pos.z, c, v["gh"], v["fh"]], out.at[v["gh"], v["fh"]]
        self.copy(u, 2 + lines, mine, w.at[lines - 1, 1 - c, v["r1"], v["c1"]], pos.second)
        self.copy(u, 3 + lines, mine, there, pos.first)
        self.keep(u, 0, mine, there)

    def relay(self, u):
        w, _, out, v = self.views(u)
        pos, c, lines = self.pos, self.pos.c, self.pos.lines
        self.copies[u, 2 + lines].wait_recv()
        came, there = w.at[lines - 1, 1 - c, v["r1"], v["c1"]], out.at[v["go"], v["fh"]]
        self.copy(u, 4 + lines, came, there, pos.first)
        self.keep(u, 1, came, there)

    def line_whole(self, u):
        w, _, _, v = self.views(u)
        pos, c, lines = self.pos, self.pos.c, self.pos.lines
        for k in range(1, lines):
            self.copies[u, 2 + k].wait_recv()
        total = w[pos.z, c, v["ar"], v["ac"]].astype(F32)
        for k in range(1, lines):
            total = total + w[k - 1, 1 - c, v["ar"], v["ac"]].astype(F32)
        w[pos.z, c, v["ar"], v["ac"]] = total.astype(LOW)
        pl.semaphore_wait(self.free.at[u, 0], 1)
        self.copy(
            u,
            1,
            w.at[pos.z, c, v["ar"], v["fo"]],
            w.at[lines - 1, 1 - c, v["ar"], v["c0"]],
            pos.first,
        )

    def one_share(self, u):
        w, _, _, v = self.views(u)
        pos, c, lines = self.pos, self.pos.c, self.pos.lines
        self.copies[u, 1].wait_recv()
        w[pos.z, c, v["ar"], v["fh"]] += w[lines - 1, 1 - c, v["ar"], v["c0"]]
        pl.semaphore_wait(self.free.at[u, 1], 1)
        self.copy(
            u,
            2,
            w.at[pos.z, c, v["go"], v["fh"]],
            w.at[lines - 1, 1 - c, v["r0"], v["c1"]],
            pos.second,
        )

    def two_share(self, u):
        w, _, _, v = self.views(u)
        pos, c, lines = self.pos, self.pos.c, self.pos.lines
        self.copies[u, 2].wait_recv()
        w[pos.z, c, v["gh"], v["fh"]] += w[lines - 1, 1 - c, v["r0"], v["c1"]]
        self.spread(u)

    def clears(self, count):
        while self.cleared < count:
            self.clear(self.cleared)
            self.cleared += 1

    def pairs(self, count):
        self.clears(count)
        while self.paired < count:
            self.pair(self.paired)
            self.paired += 1

    def serve(self, turns, eager=False):
        self.pairs(min(self.cleared, self.turns + LEAD))
        self.clears(self.emitted if eager else self.mark)
        self.mark = self.emitted
        for _ in range(turns):
            if all(u < self.paired for _, u in self.steps.get(self.turns, ())):
                self.turn()

    def plan(self):
        plan = {}
        for u in reversed(range(len(self.units))):
            whole = self.units[u][4]
            steps = (self.one, self.two, self.line)
            if whole:
                steps = (self.line_whole, self.one_share, self.two_share)
            steps = (*steps, self.relay)
            usual = LAGS if u < len(self.units) - LAST else LAST_LAGS
            lags = (WHOLE_LAG, *LAGS[:2], LAGS[3]) if whole else usual
            at = u
            for step, lag in zip(steps, lags):
                at += lag
                plan.setdefault(at, []).append((step, u))
        return plan

    def done(self):
        return self.turns > max(self.steps)

    def turn(self):
        if not self.done():
            steps = self.steps.get(self.turns, ())
            self.turns += 1
            self.pairs(max([u + 1 for _, u in steps] + [self.paired]))
            for step, u in steps:
                step(u)
            last = max(at for at, steps in self.steps.items() for _, u in steps if u == self.settled)
            if last <= self.turns - 4:
                self.settle(self.settled + 1)

    def settle(self, count):
        lines = self.pos.lines
        while self.settled < min(count, len(self.units)):
            u = self.settled
            for j in range(1, 5 + lines):
                self.copies[u, j].wait_send()
            for j in range(3 + lines, 5 + lines):
                self.copies[u, j].wait_recv()
            for j in range(2):
                self.copies[u, "local", j].wait()
            self.settled += 1


def dot(a, b):
    return jnp.dot(a, b, preferred_element_type=F32)


def dot_across(a, b):
    return lax.dot_general(a, b, (((1,), (1,)), ((), ())), preferred_element_type=F32)


SAVED = ("x", "x1", "key", "value", "logit", "numer", "denom", "value2", "recept")
SAVED_LOW = ("xk", "xv", "xr", "gated", "xk2", "xr2")
WIDE = 256
BLOCK = 32
LEAD = 12
GATHER_LAGS = (1, 1, 1)
VECTOR_TURNS = 3
AHEAD = 2
FIRST_PIECES = 1
LINE_FIRST = (1,7)
LAGS = (2,3,7,5)
LAST = 3
LAST_LAGS = (3,3,5,3)
WHOLE_LAG = 5
SITES = (1,0,1,1,1,0,0,0,0,0,1,1,0,0,1,1,0,1,0,2,0,1,1,0,0,1,1,1,1,0,1,1,1,1)
VMEM_BYTES = 63 * 2**20


def train_kernel(dims, *refs):
    layers, lines, rows, length, width, hidden = dims
    refs = list(refs)

    def take(count):
        got = refs[:count]
        del refs[:count]
        return got

    matrices = 5
    tokens, doc_starts, decay, first, mix, ln_gain, ln_bias = take(7)
    shards = take(matrices)
    (cotangent,) = take(1)
    output, grad_tokens, vector_out = take(3)
    grad_out = take(matrices)
    names = SAVED + SAVED_LOW + ("squared",)
    store = dict(zip(names, take(len(names))))
    weights = [take(matrices) for _ in range(layers)]
    landing = take(matrices)
    act = dict(zip(names, take(len(names))))
    (live, padded, grad, main, d_one, d_two, d_three, g_low, g_low2, g_low3, g_key2, turned) = take(12)
    vectors, small, vec, v_buf = take(4)
    (g_send, g_recv, own_sem, r_send, r_recv, r_free, r_credit, r_local, save_sem, load_sem, s_send, s_recv, v_send, v_recv) = take(14)
    tokens_total = rows * length
    blocks = length // BLOCK
    chunk = length // 8
    pos = Place(lines)
    s, last = pos.s, 3

    own = {}
    for l in range(layers):
        for m in range(matrices):
            own[l, m] = pltpu.make_async_copy(
                shards[m].at[l], weights[l][m].at[pos.z, pos.c], own_sem.at[l, m]
            )
            own[l, m].start()
    small[...] = jnp.zeros_like(small)
    vectors[...] = jnp.zeros_like(vectors)
    barrier = pltpu.get_barrier_semaphore()
    peers = [pos.along(k) for k in range(1, lines)]
    peers += [pos.first, pos.second, pos.across, pos.partner]
    for peer in peers:
        signal(barrier, peer)
    pl.semaphore_wait(barrier, len(peers))

    def pieces(m, count):
        _, _, r, c = weights[0][m].shape
        if m == 4:
            return [(m, (j * (r // count), r // count, 0, c)) for j in range(count)]
        return [(m, (0, r, j * (c // count), c // count)) for j in range(count)]

    def columns(m, count):
        _, _, r, c = weights[0][m].shape
        return [(m, (0, r, j * (c // count), c // count)) for j in range(count)]

    kvr = pieces(0, 3)
    start_units = [(0, (0, kvr[0][1][1], j * (width // FIRST_PIECES), width // FIRST_PIECES)) for j in range(FIRST_PIECES)]
    rest = kvr[1:] + pieces(1, 1) + pieces(2, 3) + pieces(3, 1) + columns(4, 3)
    layout = [start_units + rest, kvr[:1] + rest]
    base_of = [FIRST_PIECES - 1, FIRST_PIECES + len(rest)]
    gather = Gather(
        pos,
        [(weights[l][m], box, own.pop((l, m), None)) for l in range(layers) for m, box in layout[l]],
        g_send,
        g_recv,
        AHEAD,
    )
    for u in range(gather.ahead):
        gather.begin(u)

    back = pieces(3, 1) + pieces(4, 3) + pieces(2, 3) + pieces(1, 1) + [kvr[2], kvr[0], kvr[1]]
    line_first = LINE_FIRST
    reduce = Reduce(
        pos,
        [
            (weights[l][m], landing[m], grad_out[m].at[l], box, j in line_first)
            for l in reversed(range(layers))
            for j, (m, box) in enumerate(back)
        ],
        len(back),
        r_send,
        r_recv,
        r_free,
        r_credit,
        r_local,
    )

    sub = lax.broadcasted_iota(jnp.int32, (8, width), 0)
    place = lax.broadcasted_iota(jnp.int32, (length, 128), 0)
    at_token = (place % 8) * chunk + place // 8 + s * length
    for r in range(rows):
        start = jnp.zeros((length, 128), F32)
        for j in range(doc_starts.shape[1]):
            start = jnp.where(at_token == doc_starts[r, j], 1.0, start)
        live[r] = 1.0 - start
    p_row = lax.broadcasted_iota(jnp.int32, (length, length), 0)
    p_col = lax.broadcasted_iota(jnp.int32, (length, length), 1)
    order = jnp.where((p_row % 8) * chunk + p_row // 8 == p_col, 1.0, 0.0).astype(LOW)
    order_back = jnp.where((p_col % 8) * chunk + p_col // 8 == p_row, 1.0, 0.0).astype(LOW)

    def spread(tile):
        return jnp.concatenate([tile] * (width // 128), axis=-1)

    def span(i):
        return pl.ds(pl.multiple_of(i * BLOCK, BLOCK), BLOCK)

    def span_on(i):
        return pl.ds(pl.multiple_of(i * BLOCK + 8, 8), BLOCK)

    def tile(i):
        return pl.ds(pl.multiple_of(i * 8, 8), 8)

    def flat(ref):
        return ref[...].reshape(tokens_total, ref.shape[-1])

    def wide(j, base=0, size=WIDE):
        return pl.ds(pl.multiple_of(base + j * size, 128), size)

    def fold(block):
        return jnp.sum(block.reshape(rows * BLOCK // 8, 8, width), axis=0)

    def add_vector(level, row, block):
        vectors[level, row] += fold(block)

    def saving(name, level):
        if level == 0:
            pltpu.make_async_copy(act[name], store[name], save_sem.at[names.index(name)]).start()

    def saved(name, level):
        if level == 1:
            pltpu.make_async_copy(act[name], store[name], save_sem.at[names.index(name)]).wait()

    def loading(some):
        for name in some:
            pltpu.make_async_copy(store[name], act[name], load_sem.at[names.index(name)]).start()

    def loaded(name, level):
        if level == 0:
            pltpu.make_async_copy(store[name], act[name], load_sem.at[names.index(name)]).wait()

    def hop(index, device):
        return remote(small.at[0, index], small.at[1, index], s_send.at[index], s_recv.at[index], device)

    edge_count = 4 * layers

    def edge_start(index, step, there):
        @pl.when(there)
        def _():
            hop(index, pos.later(step)).start()

    def edge_wait(index, step, there):
        @pl.when(there)
        def _():
            hop(index, pos.later(step)).wait_recv()

    def edge_sent(index, step, there):
        @pl.when(there)
        def _():
            hop(index, pos.later(step)).wait_send()

    def chain_hop(level, direction, k):
        slot = edge_count + (level * 2 + direction) * 3
        return remote(
            small.at[0, slot],
            small.at[1, slot + k - 1],
            s_send.at[slot + k - 1],
            s_recv.at[slot + k - 1],
            pos.later(k if direction == 0 else -k),
        )

    def chain_do(level, direction, what):
        for k in range(1, 4):
            inside = s + k <= last if direction == 0 else s - k >= 0
            from_inside = s - k >= 0 if direction == 0 else s + k <= last

            @pl.when(from_inside if what == "wait_recv" else inside)
            def _():
                getattr(chain_hop(level, direction, k), what)()

    def chain_total(level, direction, r):
        slot = edge_count + (level * 2 + direction) * 3
        numer = jnp.zeros((1, width), F32)
        denom = jnp.zeros((1, width), F32)
        for k in (3, 2, 1):
            through = small[1, slot + k - 1, 3 * r : 3 * r + 1, :]
            numer = through * numer + small[1, slot + k - 1, 3 * r + 1 : 3 * r + 2, :]
            denom = through * denom + small[1, slot + k - 1, 3 * r + 2 : 3 * r + 3, :]
        return numer, denom

    def centred(x):
        center = x - jnp.mean(x, -1, keepdims=True)
        spread_ = jnp.mean(center * center, -1, keepdims=True)
        scale = lax.rsqrt(spread_ + EPSILON)
        return center * scale, scale

    def normalize_into(x_ref, level, which):
        gain, bias = ln_gain[level, which : which + 1, :], ln_bias[level, which : which + 1, :]

        @pl.loop(0, blocks)
        def _(i):
            n, _ = centred(x_ref[:, span(i), :])
            padded[:, span_on(i), :] = n * gain + bias

    def wrap_in(index):
        for r in range(rows):
            moved = pltpu.roll(padded[r, length : length + 8, :], 1, 0)
            padded[r, 0:8, :] = jnp.where(sub == 0, small[1, index, r : r + 1, :], moved)

    def normalize_shift(x_ref, level, which, outs, rates, unit):
        index = level * 2 + which
        normalize_into(x_ref, level, which)
        for r in range(rows):
            small[0, index, r : r + 1, :] = padded[r, length + 7 : length + 8, :]
        edge_start(index, 1, s < last)
        gather.need(unit)
        edge_wait(index, 1, s > 0)
        wrap_in(index)

        @pl.loop(0, blocks)
        def _(i):
            h = padded[:, span_on(i), :]
            before = padded[:, span(i), :] * spread(live[:, span(i), :])
            for out, j in zip(outs, rates):
                rate = mix[j, level : level + 1, :]
                out[:, span(i), :] = (h * rate + before * (1.0 - rate)).astype(LOW)

    def project(x_ref, w, base, count, put):
        @pl.loop(0, count // WIDE)
        def _(j):
            block = w[:, :, :, wide(j, base)].reshape(-1, WIDE)
            put(j, dot(flat(x_ref), block).reshape(rows, length, WIDE))

    def put_in(ref):
        def put(j, block):
            ref[:, :, wide(j)] = block

        return put

    def back_project(g_ref, w, base, count, out_ref):
        size = min(width, count)
        for j in range(count // size):
            block = w[:, :, :, base + j * size : base + (j + 1) * size].reshape(-1, size)
            got = dot_across(g_ref[:, :, j * size : (j + 1) * size].reshape(tokens_total, size), block)
            got = got.reshape(rows, length, width)
            if j == 0:
                out_ref[...] = got
            else:
                out_ref[...] += got

    def outer(x_ref, g_ref, w, base, count, g_base=0):
        turned[...] = flat(x_ref).T

        @pl.loop(0, count // WIDE)
        def _(j):
            g = g_ref[:, :, wide(j, g_base)].reshape(tokens_total, WIDE)
            got = dot(turned[...], g).astype(LOW)
            w[:, :, :, wide(j, base)] = got.reshape(lines, 2, width // (2 * lines), WIDE)

    def keep_rows(level):
        rate = jnp.exp(decay[level : level + 1, :])
        return jnp.broadcast_to(jnp.exp(-rate), (8, width)), rate

    def scan_local(level):
        keep, _ = keep_rows(level)

        def step(i, carry):
            out = []
            for r in range(rows):
                numer, denom, alive = carry[3 * r : 3 * r + 3]
                l128 = live[r, tile(i), :]
                l_now = spread(l128)
                lifted = jnp.exp(act["key"][r, tile(i), :])
                numer = keep * (numer * l_now) + lifted * act["value"][r, tile(i), :]
                denom = keep * (denom * l_now) + lifted
                out += [numer, denom, alive * l128]
            return tuple(out)

        zero = jnp.zeros((8, width), F32)
        carry = lax.fori_loop(0, chunk, step, (zero, zero, jnp.ones((8, 128), F32)) * rows, unroll=2)
        faded = keep
        for _ in range(chunk.bit_length() - 1):
            faded = faded * faded
        slot = edge_count + (level * 2) * 3
        before = []
        for r in range(rows):
            numer, denom, alive = carry[3 * r : 3 * r + 3]
            through = spread(alive) * faded
            vec[level, r] = through
            for shift in (1, 2, 4):
                inside = sub >= shift
                n_b, d_b, t_b = (pltpu.roll(a, shift, 0) for a in (numer, denom, through))
                numer = jnp.where(inside, through * n_b + numer, numer)
                denom = jnp.where(inside, through * d_b + denom, denom)
                through = jnp.where(inside, through * t_b, through)
            for j, a in enumerate((through, numer, denom)):
                small[0, slot, 3 * r + j : 3 * r + j + 1, :] = a[7:8, :]
            at_start = sub == 0
            n_b, d_b, t_b = (pltpu.roll(a, 1, 0) for a in (numer, denom, through))
            before.append(
                (jnp.where(at_start, 0.0, n_b), jnp.where(at_start, 0.0, d_b), jnp.where(at_start, 1.0, t_b))
            )
        chain_do(level, 0, "start")
        return before

    def scan_final(level, before):
        chain_do(level, 0, "wait_recv")
        keep, _ = keep_rows(level)
        bonus = jnp.broadcast_to(jnp.exp(first[level : level + 1, :]), (8, width))
        carry = []
        for r in range(rows):
            n_in, d_in = chain_total(level, 0, r)
            n_b, d_b, t_b = before[r]
            carry += [t_b * n_in + n_b, t_b * d_in + d_b]

        def step(i, carry):
            out = []
            for r in range(rows):
                numer, denom = carry[2 * r : 2 * r + 2]
                l_now = spread(live[r, tile(i), :])
                numer, denom = numer * l_now, denom * l_now
                act["numer"][r, tile(i), :] = numer
                act["denom"][r, tile(i), :] = denom
                value = act["value"][r, tile(i), :]
                lifted = jnp.exp(act["key"][r, tile(i), :])
                now = bonus * lifted
                main[r, tile(i), :] = (numer + now * value) / (denom + now)
                out += [keep * numer + lifted * value, keep * denom + lifted]
            return tuple(out)

        lax.fori_loop(0, chunk, step, tuple(carry), unroll=2)

    for r in range(rows):
        act["x"][r] = dot(order, tokens[r])
        grad[r] = dot(order, cotangent[r])

    def forward_layer(level):
        w_kvr, w_out, w_fkey, w_frec, w_fval = weights[level]
        base = base_of[level]
        for name in ("xk", "xv", "xr"):
            saved(name, level)
        normalize_shift(act["x"], level, 0, [act["xk"], act["xv"], act["xr"]], (0, 1, 2), base)
        saving("x", level)
        for j, (low, name) in enumerate((("xk", "key"), ("xv", "value"), ("xr", "logit"))):
            saving(low, level)
            saved(name, level)
            gather.need(base + j)
            project(act[low], w_kvr, j * width, width, put_in(act[name]))
            saving(name, level)
            if j == 1:
                before = scan_local(level)
        saved("numer", level)
        saved("denom", level)
        scan_final(level, before)
        saving("numer", level)
        saving("denom", level)
        saved("gated", level)

        @pl.loop(0, blocks)
        def _(i):
            act["gated"][:, span(i), :] = (
                jax.nn.sigmoid(act["logit"][:, span(i), :]) * main[:, span(i), :]
            ).astype(LOW)

        saving("gated", level)
        gather.need(base + 3)
        saved("x1", level)

        def put_x1(j, block):
            act["x1"][:, :, wide(j)] = act["x"][:, :, wide(j)] + block

        project(act["gated"], w_out, 0, width, put_x1)
        saving("x1", level)
        saved("xk2", level)
        saved("xr2", level)
        normalize_shift(act["x1"], level, 1, [act["xk2"], act["xr2"]], (3, 4), base + 4)
        saving("xk2", level)
        saving("xr2", level)
        saved("squared", level)
        third = hidden // 3
        for j in range(3):
            gather.need(base + 4 + j)

            def put_squared(i, block, j=j):
                up = jnp.maximum(block, 0.0)
                act["squared"][:, :, wide(i, j * third)] = (up * up).astype(LOW)

            project(act["xk2"], w_fkey, j * third, third, put_squared)
        saving("squared", level)
        gather.need(base + 7)
        saved("recept", level)
        project(act["xr2"], w_frec, 0, width, put_in(act["recept"]))
        saving("recept", level)
        saved("value2", level)
        share = hidden // lines
        for j in range(width // WIDE):
            gather.need(base + 8 + j)
            total = None
            for z in range(lines):
                got = dot(
                    act["squared"][:, :, z * share : (z + 1) * share].reshape(tokens_total, share),
                    w_fval[z, :, :, j * WIDE : (j + 1) * WIDE].reshape(share, WIDE),
                )
                total = got if total is None else total + got
            act["value2"][:, :, j * WIDE : (j + 1) * WIDE] = total.reshape(rows, length, WIDE)
        saving("value2", level)
        saved("x", level + 1)

        @pl.loop(0, blocks)
        def _(i):
            up = jax.nn.sigmoid(act["recept"][:, span(i), :]) * act["value2"][:, span(i), :]
            after = act["x1"][:, span(i), :] + up
            if level + 1 < layers:
                act["x"][:, span(i), :] = after
            else:
                g_low3[:, span(i), :] = after.astype(LOW)

    for level in range(layers):
        forward_layer(level)
    def blend_back(level, which, d_refs, rates):
        index = level * 2 + which
        wrap_in(index)

        @pl.loop(0, blocks)
        def _(i):
            l_now = spread(live[:, span(i), :])
            change = padded[:, span_on(i), :] - padded[:, span(i), :] * l_now
            direct, shifted = None, None
            for ref, j in zip(d_refs, rates):
                d = ref[:, span(i), :]
                rate = mix[j, level : level + 1, :]
                add_vector(level, 2 + j, d * change)
                direct = d * rate if direct is None else direct + d * rate
                shifted = d * (1.0 - rate) if shifted is None else shifted + d * (1.0 - rate)
            main[:, span(i), :] = direct
            d_refs[0][:, span(i), :] = shifted * l_now

        back_index = 2 * layers + index
        for r in range(rows):
            small[0, back_index, r : r + 1, :] = d_refs[0][r, 0:1, :]
        edge_start(back_index, -1, s > 0)

    def normalize_back(level, which, x_ref, q_ref, write):
        index = level * 2 + which
        back_index = 2 * layers + index
        edge_wait(back_index, -1, s < last)
        for r in range(rows):
            moved = pltpu.roll(q_ref[r, 0:8, :], 7, 0)
            padded[r, length : length + 8, :] = jnp.where(
                sub == 7, small[1, back_index, r : r + 1, :], moved
            )
            padded[r, 8:length, :] = q_ref[r, 8:length, :]
        gain = ln_gain[level, which : which + 1, :]

        @pl.loop(0, blocks)
        def _(i):
            d_h = main[:, span(i), :] + padded[:, span_on(i), :]
            n, scale = centred(x_ref[:, span(i), :])
            add_vector(level, 7 + which, d_h * n)
            add_vector(level, 9 + which, d_h)
            e = d_h * gain
            inner = e - jnp.mean(e, -1, keepdims=True) - n * jnp.mean(e * n, -1, keepdims=True)
            after = grad[:, span(i), :] + scale * inner
            grad[:, span(i), :] = after
            write(i, after)

    def wkv_terms(r, i, bonus):
        value = act["value"][r, tile(i), :]
        lifted = jnp.exp(act["key"][r, tile(i), :])
        now = bonus * lifted
        numer, denom = act["numer"][r, tile(i), :], act["denom"][r, tile(i), :]
        part = 1.0 / (denom + now)
        result = (numer + now * value) * part
        return value, lifted, now, numer, denom, part, result

    def scan_back_local(level):
        keep, _ = keep_rows(level)
        bonus = jnp.broadcast_to(jnp.exp(first[level : level + 1, :]), (8, width))

        def step(j, carry):
            i = chunk - 1 - j
            out = []
            for r in range(rows):
                h_n, h_d = carry[2 * r : 2 * r + 2]
                value, lifted, now, numer, denom, part, result = wkv_terms(r, i, bonus)
                gate = jax.nn.sigmoid(act["logit"][r, tile(i), :])
                d_gated = main[r, tile(i), :]
                d_wkv = d_gated * gate
                d_two[r, tile(i), :] = d_gated * result * gate * (1.0 - gate)
                main[r, tile(i), :] = d_wkv
                l_now = spread(live[r, tile(i), :])
                a = d_wkv * part
                out += [l_now * (a + keep * h_n), l_now * (keep * h_d - a * result)]
            return tuple(out)

        zero = jnp.zeros((8, width), F32)
        carry = lax.fori_loop(0, chunk, step, (zero, zero) * rows)
        slot = edge_count + (level * 2 + 1) * 3
        after = []
        for r in range(rows):
            h_n, h_d = carry[2 * r : 2 * r + 2]
            through = vec[level, r]
            for shift in (1, 2, 4):
                inside = sub < 8 - shift
                n_a, d_a, t_a = (pltpu.roll(a, 8 - shift, 0) for a in (h_n, h_d, through))
                h_n = jnp.where(inside, through * n_a + h_n, h_n)
                h_d = jnp.where(inside, through * d_a + h_d, h_d)
                through = jnp.where(inside, through * t_a, through)
            for j, a in enumerate((through, h_n, h_d)):
                small[0, slot, 3 * r + j : 3 * r + j + 1, :] = a[0:1, :]
            at_end = sub == 7
            n_a, d_a, t_a = (pltpu.roll(a, 7, 0) for a in (h_n, h_d, through))
            after.append(
                (jnp.where(at_end, 0.0, n_a), jnp.where(at_end, 0.0, d_a), jnp.where(at_end, 1.0, t_a))
            )
        chain_do(level, 1, "start")
        return after

    def scan_back_final(level, after):
        chain_do(level, 1, "wait_recv")
        keep, rate = keep_rows(level)
        bonus = jnp.broadcast_to(jnp.exp(first[level : level + 1, :]), (8, width))
        zero = jnp.zeros((8, width), F32)
        carry = [zero, zero]
        for r in range(rows):
            n_in, d_in = chain_total(level, 1, r)
            n_a, d_a, t_a = after[r]
            carry += [t_a * n_in + n_a, t_a * d_in + d_a]

        def step(j, carry):
            i = chunk - 1 - j
            d_keep, d_first = carry[:2]
            out = []
            for r in range(rows):
                h_n, h_d = carry[2 + 2 * r : 4 + 2 * r]
                value, lifted, now, numer, denom, part, result = wkv_terms(r, i, bonus)
                a = main[r, tile(i), :] * part
                d_now = a * (value - result) * now
                d_keep = d_keep + numer * h_n + denom * h_d
                d_first = d_first + d_now
                d_one[r, tile(i), :] = d_now + lifted * (value * h_n + h_d)
                d_two[r, tile(i), :] = a * now + lifted * h_n
                l_now = spread(live[r, tile(i), :])
                out += [l_now * (a + keep * h_n), l_now * (keep * h_d - a * result)]
            return (d_keep, d_first, *out)

        carry = lax.fori_loop(0, chunk, step, tuple(carry))
        vectors[level, 0] += carry[0] * (-rate * keep)
        vectors[level, 1] += carry[1]

    def to_low(src, dst):
        @pl.loop(0, blocks)
        def _(i):
            dst[:, span(i), :] = src[:, span(i), :].astype(LOW)

    ffn_names = ("value2", "recept", "squared", "xk2", "xr2", "x1")
    att_names = tuple(n for n in names if n not in ffn_names)

    def serve(eager=False):
        reduce.serve(SITES[reduce.site], eager)
        reduce.site += 1

    def backward_layer(level):
        w_kvr, w_out, w_fkey, w_frec, w_fval = weights[level]
        base = (layers - 1 - level) * len(back)
        third = hidden // 3
        share = hidden // lines
        loaded("value2", level)
        loaded("recept", level)

        @pl.loop(0, blocks)
        def _(i):
            gate = jax.nn.sigmoid(act["recept"][:, span(i), :])
            g = grad[:, span(i), :]
            g_low[:, span(i), :] = (g * gate).astype(LOW)
            g_low2[:, span(i), :] = (g * act["value2"][:, span(i), :] * gate * (1.0 - gate)).astype(LOW)

        loaded("xr2", level)
        back_project(g_low2, w_frec, 0, width, d_two)
        gather.settle(len(gather.units))
        outer(act["xr2"], g_low2, w_frec, 0, width)
        reduce.emit(base)
        if level == layers - 1:
            for r in range(rows):
                output[r] = dot(order_back, g_low3[r]).astype(LOW)
        loaded("squared", level)

        for half_way in range(2):

            @pl.loop(half_way * (lines // 2), (half_way + 1) * (lines // 2))
            def _(z):
                got = dot_across(flat(g_low), w_fval[z].reshape(share, width))
                got = got.reshape(rows, length, share)
                root = jnp.sqrt(act["squared"][:, :, wide(z, 0, share)].astype(F32))
                g_key2[:, :, wide(z, 0, share)] = (got * (2.0 * root)).astype(LOW)

            serve(True)

        @pl.loop(0, lines)
        def _(z):
            turned[...] = act["squared"][:, :, wide(z, 0, share)].reshape(tokens_total, share).T
            for j in range(width // WIDE):
                g = g_low[:, :, j * WIDE : (j + 1) * WIDE].reshape(tokens_total, WIDE)
                got = dot(turned[...], g).astype(LOW)
                w_fval[z, :, :, j * WIDE : (j + 1) * WIDE] = got.reshape(2, share // 2, WIDE)

        for j in range(3):
            reduce.emit(base + 1 + j)
        serve()
        back_project(g_key2, w_fkey, 0, hidden, d_one)
        serve()
        loaded("xk2", level)
        for j in range(3):
            outer(act["xk2"], g_key2, w_fkey, j * third, third, j * third)
            reduce.emit(base + 4 + j)
            serve()
        loaded("x1", level)
        normalize_into(act["x1"], level, 1)
        blend_back(level, 1, [d_one, d_two], (3, 4))
        serve()

        def write_att(i, after):
            g_low3[:, span(i), :] = after.astype(LOW)

        normalize_back(level, 1, act["x1"], d_one, write_att)
        serve()
        if level == 1:
            loading(ffn_names)
        back_project(g_low3, w_out, 0, width, main)
        loaded("gated", level)
        outer(act["gated"], g_low3, w_out, 0, width)
        reduce.emit(base + 7)
        serve()
        for name in ("logit", "key", "value", "numer", "denom"):
            loaded(name, level)
        after = scan_back_local(level)
        serve()
        to_low(d_two, g_low)
        loaded("xr", level)
        back_project(g_low, w_kvr, 2 * width, width, d_three)
        outer(act["xr"], g_low, w_kvr, 2 * width, width)
        reduce.emit(base + 8)
        serve()
        scan_back_final(level, after)
        serve()
        to_low(d_one, g_low2)
        to_low(d_two, g_low3)
        loaded("xk", level)
        loaded("xv", level)
        back_project(g_low2, w_kvr, 0, width, d_one)
        outer(act["xk"], g_low2, w_kvr, 0, width)
        reduce.emit(base + 9)
        serve()
        back_project(g_low3, w_kvr, width, width, d_two)
        outer(act["xv"], g_low3, w_kvr, width, width)
        reduce.emit(base + 10)
        serve()
        loaded("x", level)
        normalize_into(act["x"], level, 0)
        blend_back(level, 0, [d_one, d_two, d_three], (0, 1, 2))
        serve()

        def write_none(i, after):
            g_low[:, span(i), :] = after.astype(LOW)

        normalize_back(level, 0, act["x"], d_one, write_none)
        serve()
        if level == 1:
            loading(att_names)

    for level in reversed(range(layers)):
        backward_layer(level)
    for r in range(rows):
        grad_tokens[r] = dot(order_back, g_low[r]).astype(LOW)

    count = vectors.shape[1]

    def vector_hop(j, device):
        source = min(j, 3)
        return remote(v_buf.at[0, source], v_buf.at[1, j], v_send.at[j], v_recv.at[j], device)

    def vector_stage(stage):
        if stage == 0:
            for level in range(layers):
                for row in range(count):
                    j = level * count + row
                    v_buf[0, 0, j : j + 1, :] = jnp.sum(vectors[level, row], axis=0, keepdims=True)
        elif stage < 4:
            vector_hop(stage - 1, pos.partner).wait_recv()
            v_buf[0, stage] = v_buf[0, stage - 1] + v_buf[1, stage - 1]
        if stage < 3:
            vector_hop(stage, (pos.partner, pos.first, pos.second)[stage]).start()
        elif stage == 3:
            for k in range(1, lines):
                vector_hop(2 + k, pos.along(k)).start()
        else:
            total = v_buf[0, 3]
            for k in range(1, lines):
                vector_hop(2 + k, pos.along(k)).wait_recv()
                total = total + v_buf[1, 2 + k]
            vector_out[...] = total

    for stage in range(5):
        vector_stage(stage)
        for _ in range(VECTOR_TURNS):
            reduce.turn()
    while not reduce.done():
        reduce.turn()
    reduce.settle(len(reduce.units))
    for j, device in enumerate((pos.partner, pos.first, pos.second)):
        vector_hop(j, device).wait_send()
    for k in range(1, lines):
        vector_hop(2 + k, pos.along(k)).wait_send()
    for level in range(layers):
        for which in range(2):
            index = level * 2 + which
            edge_sent(index, 1, s < last)
            edge_sent(2 * layers + index, -1, s > 0)
        for direction in range(2):
            chain_do(level, direction, "wait_send")


def finish_kernel(dims, *refs):
    layers, share, moved = dims
    ins, sums = refs[:moved], refs[moved]
    outs = refs[moved + 1 : 2 * moved + 1]
    decay, first, mix, gain, bias = refs[2 * moved + 1 : 2 * moved + 6]
    came = refs[2 * moved + 6 : 3 * moved + 6]
    wide = came[:2] + refs[3 * moved + 6 : 4 * moved + 4]
    in_sem, out_sem = refs[4 * moved + 4 :]
    parts = [(i, j) for i in range(moved) for j in range(layers)]

    def arrive(i, j):
        return pltpu.make_async_copy(ins[i].at[j], came[i].at[j], in_sem.at[i, j])

    def leave(i, j):
        return pltpu.make_async_copy(wide[i].at[j], outs[i].at[j], out_sem.at[i, j])

    for part in parts:
        arrive(*part).start()
    offset = lax.axis_index("dp") * share
    width = sums.shape[1]
    own = pltpu.roll(sums[...], lax.rem(width - offset, width), 1)[:, :share]
    for level in range(layers):
        at = level * 11
        decay[level : level + 1, :] = own[at : at + 1]
        first[level : level + 1, :] = own[at + 1 : at + 2]
        for j in range(5):
            mix[j, level : level + 1, :] = own[at + 2 + j : at + 3 + j]
        for j in range(2):
            gain[level, j : j + 1, :] = own[at + 7 + j : at + 8 + j]
            bias[level, j : j + 1, :] = own[at + 9 + j : at + 10 + j]
    for i, j in parts:
        arrive(i, j).wait()
        if i >= 2:
            rows = ins[i].shape[1]

            @pl.loop(0, rows // 16)
            def _(k):
                at = pl.ds(pl.multiple_of(k * 16, 16), 16)
                wide[i][j, at, :] = came[i][j, at, :].astype(F32)

        leave(i, j).start()
    for part in parts:
        leave(*part).wait()


def fast_body(
    tokens, doc_starts, decay, first, mix, ln_gain, ln_bias,
    att_kvr, att_out, ffn_key, ffn_recept, ffn_value, cotangent,
):
    rows, length, width = tokens.shape
    layers, hidden = decay.shape[0], ffn_key.shape[2]
    lines = lax.axis_size("dp") // 2
    shards = (att_kvr, att_out, ffn_key, ffn_recept, ffn_value)
    plain, low = (rows, length, width), LOW
    saved = [jax.ShapeDtypeStruct(plain, F32)] * len(SAVED)
    saved += [jax.ShapeDtypeStruct(plain, low)] * len(SAVED_LOW)
    saved += [jax.ShapeDtypeStruct((rows, length, hidden), low)]
    vector_rows = -(-layers * 11 // 8) * 8
    outs = [
        jax.ShapeDtypeStruct(plain, low),
        jax.ShapeDtypeStruct(plain, low),
        jax.ShapeDtypeStruct((vector_rows, width), F32),
    ]
    outs += [jax.ShapeDtypeStruct(w.shape, low) for w in shards]
    outs += saved
    vmem, anywhere = pl.BlockSpec(memory_space=pltpu.VMEM), pl.BlockSpec(memory_space=pl.ANY)
    units = 11 * layers + FIRST_PIECES - 1
    hops = 4 * layers + 6 * layers
    dma, plain_f32, plain_low = pltpu.SemaphoreType.DMA, pltpu.VMEM(plain, F32), pltpu.VMEM(plain, low)
    scratch = [pltpu.VMEM((lines, 2) + w.shape[1:], low) for _ in range(layers) for w in shards]
    scratch += [pltpu.VMEM((lines,) + w.shape[1:], low) for w in shards]
    scratch += [pltpu.VMEM(a.shape, a.dtype) for a in saved]
    scratch += [
        pltpu.VMEM((rows, length, 128), F32),
        pltpu.VMEM((rows, length + 8, width), F32),
        plain_f32,
        plain_f32,
        plain_f32,
        plain_f32,
        plain_f32,
        plain_low,
        plain_low,
        plain_low,
        pltpu.VMEM((rows, length, hidden), low),
        pltpu.VMEM((width, rows * length), low),
        pltpu.VMEM((layers, 11, 8, width), F32),
        pltpu.VMEM((2, hops, 8, width), F32),
        pltpu.VMEM((layers, rows, 8, width), F32),
        pltpu.VMEM((2, 6, vector_rows, width), F32),
        dma((units, 3 * lines - 2)),
        dma((units, 3 * lines - 2)),
        dma((layers, len(shards))),
        dma((units, 5 + lines)),
        dma((units, 5 + lines)),
        pltpu.SemaphoreType.REGULAR((units, 1 + lines)),
        pltpu.SemaphoreType.REGULAR((11,)),
        dma((units, 2)),
        dma((len(saved),)),
        dma((len(saved),)),
        dma((hops,)),
        dma((hops,)),
        dma((6,)),
        dma((6,)),
    ]
    smem = pl.BlockSpec(memory_space=pltpu.SMEM)
    got = pl.pallas_call(
        functools.partial(train_kernel, (layers, lines, rows, length, width, hidden)),
        out_shape=outs,
        in_specs=[vmem, smem] + [vmem] * 5 + [anywhere] * len(shards) + [vmem],
        out_specs=[vmem] * 3 + [anywhere] * (len(outs) - 3),
        scratch_shapes=scratch,
        compiler_params=pltpu.CompilerParams(
            collective_id=0, has_side_effects=True, vmem_limit_bytes=VMEM_BYTES
        ),
    )(tokens, doc_starts, decay, first, jnp.swapaxes(mix, 0, 1), ln_gain, ln_bias, *shards, cotangent)
    share = width // lax.axis_size("dp")
    final = [jax.ShapeDtypeStruct(plain, low)] * 2
    final += [jax.ShapeDtypeStruct(w.shape, F32) for w in shards]
    final += [jax.ShapeDtypeStruct((layers, share), F32)] * 2
    final += [jax.ShapeDtypeStruct((5, layers, share), F32)]
    final += [jax.ShapeDtypeStruct((layers, 2, share), F32)] * 2
    moved = 2 + len(shards)
    done = pl.pallas_call(
        functools.partial(finish_kernel, (layers, share, moved)),
        out_shape=final,
        in_specs=[anywhere] * moved + [vmem],
        out_specs=[anywhere] * moved + [vmem] * 5,
        scratch_shapes=[pltpu.VMEM(a.shape, low) for a in final[:moved]]
        + [pltpu.VMEM(a.shape, F32) for a in final[2:moved]]
        + [dma((moved, layers)), dma((moved, layers))],
        compiler_params=pltpu.CompilerParams(vmem_limit_bytes=VMEM_BYTES),
    )(got[0], got[1], *got[3 : 3 + len(shards)], got[2])
    output, grad_tokens = done[:2]
    g_decay, g_first, g_mix, g_gain, g_bias = done[moved:]
    return (
        output,
        grad_tokens,
        g_decay,
        g_first,
        jnp.swapaxes(g_mix, 0, 1),
        g_gain,
        g_bias,
        *done[2:moved],
    )


def kernel_fits(tokens, decay, ffn_key, shards):
    rows, length, width = tokens.shape
    lines = lax.axis_size("dp") // 2
    return (
        lax.axis_size("seq") == 4
        and lax.axis_size("dp") == 2 * lines
        and lines > 1
        and decay.shape[0] == 2
        and rows == 2
        and length % BLOCK == 0
        and length & (length - 1) == 0
        and width % WIDE == 0
        and ffn_key.shape[2] == width * lines
        and all(w.shape[1] % 32 == 0 and w.shape[2] % WIDE == 0 for w in shards)
    )


def from_behind(block, axis, distance):
    devices = range(lax.axis_size(axis))
    route = [(i - distance, i) for i in devices if i - distance in devices]
    return lax.ppermute(block, axis, route)


def normalize(stream, gain_row, bias_row):
    center = stream - jnp.mean(stream, -1, keepdims=True)
    spread = jnp.mean(center * center, -1, keepdims=True)
    return center * lax.rsqrt(spread + EPSILON) * gain_row + bias_row


def blend(hidden, edge_row, rates, starts):
    earlier = (
        jnp.concatenate([edge_row[:, None, :], hidden[:, :-1, :]], axis=1)
        * (1.0 - starts)[:, :, None]
    )
    return tuple((hidden * rates[j] + earlier * (1.0 - rates[j]) for j in range(rates.shape[0])))


def product(inputs, matrix):
    return jnp.einsum("rcd,de->rce", inputs, matrix, preferred_element_type=jnp.float32)


def product_back(grads, matrix):
    return jnp.einsum("rce,de->rcd", grads, matrix, preferred_element_type=jnp.float32)


def outer_sum(inputs, grads):
    return jnp.einsum("rcd,rce->de", inputs, grads, preferred_element_type=jnp.float32)


def wkv_tokens(key_proj, value_proj, decay_row, foremost_line_entry, numer_in, denom_in, starts):
    rows, length, width = key_proj.shape
    block = math.gcd(length, 64)
    count = length // block
    rate = jnp.exp(decay_row)
    local = jnp.arange(block, dtype=jnp.float32)
    lower = (local[:, None] > local[None, :]).astype(jnp.float32)
    grow = jnp.exp(local[:, None] * rate[None, :])
    shrink = jnp.exp(-(local[:, None] - 1.0) * rate[None, :])
    fade = jnp.exp(-local[:, None] * rate[None, :])
    keep_rate = jnp.exp(-rate)

    def one_block(carry, inputs):
        accrued_dividend_total, accrued_divisor_total = carry
        present_lookup_entry, present_payload_entry, start_now = inputs
        counted = jnp.cumsum(start_now, axis=1)
        same = lower[None] * (counted[:, :, None] == counted[:, None, :]).astype(jnp.float32)
        alive = (counted == 0.0).astype(jnp.float32)[:, :, None]
        key_exp = jnp.exp(present_lookup_entry)
        lifted = grow[None] * key_exp
        numer_sum = jnp.einsum(
            "rji,ric->rjc", same, lifted * present_payload_entry, precision=lax.Precision.HIGHEST
        )
        denom_sum = jnp.einsum("rji,ric->rjc", same, lifted, precision=lax.Precision.HIGHEST)
        present_dividend_term = (
            shrink[None] * numer_sum + fade[None] * alive * accrued_dividend_total[:, None, :]
        )
        present_divisor_term = (
            shrink[None] * denom_sum + fade[None] * alive * accrued_divisor_total[:, None, :]
        )
        present_reward_term = jnp.exp(foremost_line_entry + present_lookup_entry)
        recurrence_result = (
            present_dividend_term + present_reward_term * present_payload_entry
        ) / (present_divisor_term + present_reward_term)
        numer_end = (
            keep_rate * present_dividend_term[:, -1] + key_exp[:, -1] * present_payload_entry[:, -1]
        )
        denom_end = keep_rate * present_divisor_term[:, -1] + key_exp[:, -1]
        return ((numer_end, denom_end), recurrence_result)

    def split(values):
        return jnp.swapaxes(values.reshape((rows, count, block) + values.shape[2:]), 0, 1)

    carry_end, results = lax.scan(
        one_block, (numer_in, denom_in), (split(key_proj), split(value_proj), split(starts))
    )
    return jnp.swapaxes(results, 0, 1).reshape(rows, length, width)


def span_transform(key_proj, value_proj, decay_row, starts):
    length = key_proj.shape[1]
    rate = jnp.exp(decay_row)
    steps = jnp.arange(length, dtype=jnp.float32)
    last_start = jnp.max(steps[None, :] * starts, axis=1)
    after = (steps[None, :] >= last_start[:, None]).astype(jnp.float32)
    weight = jnp.exp(key_proj - (length - 1.0 - steps)[None, :, None] * rate) * after[:, :, None]
    carry_numer = jnp.sum(weight * value_proj, axis=1)
    carry_denom = jnp.sum(weight, axis=1)
    through = jnp.prod(1.0 - starts, axis=1)[:, None] * jnp.exp(-length * rate)[None, :]
    return (through, carry_numer, carry_denom)


def body(
    tokens,
    doc_starts,
    decay,
    first,
    mix,
    ln_gain,
    ln_bias,
    att_kvr,
    att_out,
    ffn_key,
    ffn_recept,
    ffn_value,
    cotangent,
):
    shards = (att_kvr, att_out, ffn_key, ffn_recept, ffn_value)
    if kernel_fits(tokens, decay, ffn_key, shards):
        return fast_body(
            tokens, doc_starts, decay, first, mix, ln_gain, ln_bias, *shards, cotangent
        )
    row_total, token_total, width = tokens.shape
    layer_total = decay.shape[0]
    batches = 2
    per_batch = row_total // batches
    positions = lax.axis_index("seq") * token_total + jnp.arange(token_total, dtype=jnp.int32)
    starts_all = jnp.any(doc_starts[:, :, None] == positions[None, None, :], axis=1).astype(
        jnp.float32
    )
    empty = jnp.zeros((per_batch, width), jnp.float32)

    def edge_of(hidden):
        return from_behind(hidden[:, -1, :], "seq", 1)

    def edge_back(grad_edge):
        return from_behind(grad_edge, "seq", -1)

    def chain_forward(through, carry_numer, carry_denom):
        incoming = (empty, empty)
        sent_numer, sent_denom = (carry_numer, carry_denom)
        for relay_turn in range(lax.axis_size("seq") - 1):
            incoming = from_behind((sent_numer, sent_denom), "seq", 1)
            sent_numer = through * incoming[0] + carry_numer
            sent_denom = through * incoming[1] + carry_denom
        return incoming

    def forward_layer(stream, level, matrices, starts):
        w_kvr, w_out, w_fkey, w_frec, w_fval = matrices
        hidden, norm_one = jax.vjp(normalize, stream, ln_gain[level, 0], ln_bias[level, 0])
        edge_row = edge_of(hidden)
        blends, blend_one = jax.vjp(
            lambda h_in, e_in, r_in: blend(h_in, e_in, r_in, starts),
            hidden,
            edge_row,
            mix[level, :3],
        )
        xk_low, xv_low, xr_low = [b.astype(jnp.bfloat16) for b in blends]
        key_proj = product(xk_low, w_kvr[:, :width])
        value_proj = product(xv_low, w_kvr[:, width : 2 * width])
        logit = product(xr_low, w_kvr[:, 2 * width :])
        transform, transform_one = jax.vjp(
            lambda k_in, v_in, d_in: span_transform(k_in, v_in, d_in, starts),
            key_proj,
            value_proj,
            decay[level],
        )
        numer_in, denom_in = chain_forward(transform[0], transform[1], transform[2])
        mixed, tokens_one = jax.vjp(
            lambda k_in, v_in, d_in, f_in, n_in, z_in: wkv_tokens(
                k_in, v_in, d_in, f_in, n_in, z_in, starts
            ),
            key_proj,
            value_proj,
            decay[level],
            first[level],
            numer_in,
            denom_in,
        )
        gated, gate_one = jax.vjp(lambda g_in, m_in: jax.nn.sigmoid(g_in) * m_in, logit, mixed)
        gated_low = gated.astype(jnp.bfloat16)
        middle = stream + product(gated_low, w_out)
        hidden_two, norm_two = jax.vjp(normalize, middle, ln_gain[level, 1], ln_bias[level, 1])
        edge_two = edge_of(hidden_two)
        blends_two, blend_two = jax.vjp(
            lambda h_in, e_in, r_in: blend(h_in, e_in, r_in, starts),
            hidden_two,
            edge_two,
            mix[level, 3:],
        )
        xk2_low, xr2_low = [b.astype(jnp.bfloat16) for b in blends_two]
        key_two = product(xk2_low, w_fkey)
        squared, square_one = jax.vjp(lambda k_in: jnp.square(jax.nn.relu(k_in)), key_two)
        squared_low = squared.astype(jnp.bfloat16)
        value_two = product(squared_low, w_fval)
        recept = product(xr2_low, w_frec)
        branch, branch_one = jax.vjp(
            lambda r_in, v_in: jax.nn.sigmoid(r_in) * v_in, recept, value_two
        )
        record = (
            norm_one,
            blend_one,
            xk_low,
            xv_low,
            xr_low,
            transform[0],
            numer_in,
            denom_in,
            transform_one,
            tokens_one,
            gate_one,
            gated_low,
            norm_two,
            blend_two,
            xk2_low,
            xr2_low,
            square_one,
            squared_low,
            branch_one,
        )
        return (middle + branch, record)

    gathered = []
    for level in range(layer_total):
        gathered.append(
            (
                lax.all_gather(att_kvr[level], "dp", axis=0, tiled=True),
                lax.all_gather(att_out[level], "dp", axis=0, tiled=True),
                lax.all_gather(ffn_key[level], "dp", axis=0, tiled=True),
                lax.all_gather(ffn_recept[level], "dp", axis=0, tiled=True),
                lax.all_gather(ffn_value[level], "dp", axis=0, tiled=True),
            )
        )
    pair_lists = [[] for level in range(layer_total)]
    vector_sums = [None] * layer_total
    outputs = []
    grad_parts = []
    for batch in range(batches):
        low_row = batch * per_batch
        starts = starts_all[low_row : low_row + per_batch]
        stream = tokens[low_row : low_row + per_batch].astype(jnp.float32)
        records = []
        for level in range(layer_total):
            stream, record = forward_layer(stream, level, gathered[level], starts)
            records.append(record)
        outputs.append(stream.astype(jnp.bfloat16))
        gradient = cotangent[low_row : low_row + per_batch].astype(jnp.float32)
        for level in reversed(range(layer_total)):
            backward_w_kvr, backward_w_out, backward_w_fkey, backward_w_frec, backward_w_fval = (
                gathered[level]
            )
            (
                backward_norm_one,
                backward_blend_one,
                backward_xk_low,
                backward_xv_low,
                backward_xr_low,
                backward_through,
                backward_numer_in,
                backward_denom_in,
                backward_transform_one,
                backward_tokens_one,
                backward_gate_one,
                backward_gated_low,
                backward_norm_two,
                backward_blend_two,
                backward_xk2_low,
                backward_xr2_low,
                backward_square_one,
                backward_squared_low,
                backward_branch_one,
            ) = records[level]
            d_recept, d_value_two = backward_branch_one(gradient)
            g_value_two = d_value_two.astype(jnp.bfloat16)
            g_recept = d_recept.astype(jnp.bfloat16)
            (d_key_two,) = backward_square_one(product_back(g_value_two, backward_w_fval))
            g_key_two = d_key_two.astype(jnp.bfloat16)
            d_hidden_two, d_edge_two, d_rates_two = backward_blend_two(
                (product_back(g_key_two, backward_w_fkey), product_back(g_recept, backward_w_frec))
            )
            d_hidden_two = d_hidden_two.at[:, -1, :].add(edge_back(d_edge_two))
            d_middle_norm, d_gain_two, d_bias_two = backward_norm_two(d_hidden_two)
            d_middle = gradient + d_middle_norm
            g_att = d_middle.astype(jnp.bfloat16)
            d_logit, d_mixed = backward_gate_one(product_back(g_att, backward_w_out))
            g_logit = d_logit.astype(jnp.bfloat16)
            (
                d_key_one,
                d_value_one,
                d_decay_one,
                d_first,
                backward_direct_numer,
                backward_direct_denom,
            ) = backward_tokens_one(d_mixed)
            chain_incoming = (empty, empty)
            chain_sent_numer = backward_direct_numer
            chain_sent_denom = backward_direct_denom
            for chain_relay_turn in range(lax.axis_size("seq") - 1):
                chain_incoming = from_behind((chain_sent_numer, chain_sent_denom), "seq", -1)
                chain_sent_numer = backward_through * chain_incoming[0] + backward_direct_numer
                chain_sent_denom = backward_through * chain_incoming[1] + backward_direct_denom
            g_numer_out, g_denom_out = chain_incoming
            d_key_two_part, d_value_two_part, d_decay_two = backward_transform_one(
                (
                    g_numer_out * backward_numer_in + g_denom_out * backward_denom_in,
                    g_numer_out,
                    g_denom_out,
                )
            )
            g_key = (d_key_one + d_key_two_part).astype(jnp.bfloat16)
            g_value = (d_value_one + d_value_two_part).astype(jnp.bfloat16)
            d_blends = (
                product_back(g_key, backward_w_kvr[:, :width]),
                product_back(g_value, backward_w_kvr[:, width : 2 * width]),
                product_back(g_logit, backward_w_kvr[:, 2 * width :]),
            )
            d_hidden, d_edge, d_rates = backward_blend_one(d_blends)
            d_hidden = d_hidden.at[:, -1, :].add(edge_back(d_edge))
            d_stream_norm, d_gain_one, d_bias_one = backward_norm_one(d_hidden)
            pairs = (
                (backward_xk2_low, g_key_two),
                (backward_xr2_low, g_recept),
                (backward_squared_low, g_value_two),
                (backward_xk_low, g_key),
                (backward_xv_low, g_value),
                (backward_xr_low, g_logit),
                (backward_gated_low, g_att),
            )
            columns = (
                [d_decay_one + d_decay_two, d_first]
                + [d_rates[j] for j in range(3)]
                + [d_rates_two[j] for j in range(2)]
                + [d_gain_one, d_gain_two, d_bias_one, d_bias_two]
            )
            backward_vectors = jnp.stack(columns, axis=1)
            gradient, pairs, vectors = (d_middle + d_stream_norm, pairs, backward_vectors)
            pair_lists[level].append(pairs)
            vector_sums[level] = (
                vectors if vector_sums[level] is None else vector_sums[level] + vectors
            )
        grad_parts.append(gradient.astype(jnp.bfloat16))
    results = [None] * layer_total
    for level in reversed(range(layer_total)):
        pair_list = pair_lists[level]

        def summed(index):
            inputs = jnp.concatenate([p[index][0] for p in pair_list], axis=0)
            grads = jnp.concatenate([p[index][1] for p in pair_list], axis=0)
            return outer_sum(inputs, grads)

        ffn_part = (summed(0), summed(1), summed(2))
        finish_grad_kvr = jnp.concatenate([summed(3), summed(4), summed(5)], axis=1)
        totals = (
            lax.psum(
                lax.psum_scatter(ffn_part[0], "dp", scatter_dimension=0, tiled=True).astype(
                    jnp.bfloat16
                ),
                "seq",
            ).astype(jnp.float32),
            lax.psum(
                lax.psum_scatter(ffn_part[1], "dp", scatter_dimension=0, tiled=True).astype(
                    jnp.bfloat16
                ),
                "seq",
            ).astype(jnp.float32),
            lax.psum(
                lax.psum_scatter(ffn_part[2], "dp", scatter_dimension=0, tiled=True).astype(
                    jnp.bfloat16
                ),
                "seq",
            ).astype(jnp.float32),
            lax.psum(
                lax.psum_scatter(finish_grad_kvr, "dp", scatter_dimension=0, tiled=True).astype(
                    jnp.bfloat16
                ),
                "seq",
            ).astype(jnp.float32),
            lax.psum(
                lax.psum_scatter(summed(6), "dp", scatter_dimension=0, tiled=True).astype(
                    jnp.bfloat16
                ),
                "seq",
            ).astype(jnp.float32),
            lax.psum(
                lax.psum_scatter(vector_sums[level], "dp", scatter_dimension=0, tiled=True).astype(
                    jnp.bfloat16
                ),
                "seq",
            ).astype(jnp.float32),
        )
        ffn_part = (totals[0], totals[1], totals[2])
        att_part = (totals[3], totals[4], totals[5])
        results[level] = (ffn_part, att_part)
    output = jnp.concatenate(outputs, axis=0)
    grad_tokens = jnp.concatenate(grad_parts, axis=0)
    grad_ffn_key = jnp.stack([r[0][0] for r in results])
    grad_ffn_recept = jnp.stack([r[0][1] for r in results])
    grad_ffn_value = jnp.stack([r[0][2] for r in results])
    grad_kvr = jnp.stack([r[1][0] for r in results])
    grad_att_out = jnp.stack([r[1][1] for r in results])
    vector_rows = jnp.stack([r[1][2] for r in results])
    grad_decay = vector_rows[:, :, 0]
    grad_first = vector_rows[:, :, 1]
    grad_mix = jnp.swapaxes(vector_rows[:, :, 2:7], 1, 2)
    grad_gain = jnp.swapaxes(vector_rows[:, :, 7:9], 1, 2)
    grad_bias = jnp.swapaxes(vector_rows[:, :, 9:11], 1, 2)
    return (
        output,
        grad_tokens,
        grad_decay,
        grad_first,
        grad_mix,
        grad_gain,
        grad_bias,
        grad_kvr,
        grad_att_out,
        grad_ffn_key,
        grad_ffn_recept,
        grad_ffn_value,
    )


def solution(mesh):
    in_specs = (
        P("dp", "seq", None),
        P("dp", None),
        P(),
        P(),
        P(),
        P(),
        P(),
        P(None, "dp", None),
        P(None, "dp", None),
        P(None, "dp", None),
        P(None, "dp", None),
        P(None, "dp", None),
        P("dp", "seq", None),
    )
    out_specs = (
        P("dp", "seq", None),
        P("dp", "seq", None),
        P(None, "dp"),
        P(None, "dp"),
        P(None, None, "dp"),
        P(None, None, "dp"),
        P(None, None, "dp"),
        P(None, "dp", None),
        P(None, "dp", None),
        P(None, "dp", None),
        P(None, "dp", None),
        P(None, "dp", None),
    )
    return jax.shard_map(body, mesh=mesh, in_specs=in_specs, out_specs=out_specs, check_vma=False)
```

```python
import functools
import math

import jax
import jax.numpy as jnp
from jax import lax
from jax.experimental import pallas as pl
from jax.experimental.pallas import tpu as pltpu
from jax.sharding import PartitionSpec as P

EPSILON = 1e-05
MESH = pl.DeviceIdType.MESH
F32, LOW = jnp.float32, jnp.bfloat16


class Place:
    def __init__(self, lines):
        self.lines = lines
        s, d = lax.axis_index("seq"), lax.axis_index("dp")
        self.s, self.d = s, d
        self.c, self.z = lax.rem(d, 2), d // 2
        x, y, c = lax.rem(s, 2), s // 2, self.c
        self.f = x * (1 - c) + y * c
        self.g = y * (1 - c) + x * c
        flip_x, flip_y = s + 1 - 2 * x, s + 2 - 4 * y
        self.first = (flip_x * (1 - c) + flip_y * c, d)
        self.second = (flip_y * (1 - c) + flip_x * c, d)
        self.across = (3 - s, d)
        self.partner = (s, d + 1 - 2 * c)

    def line(self, k):
        return lax.rem(self.z + k + self.lines, self.lines)

    def along(self, k):
        return (self.s, self.line(k) * 2 + self.c)

    def later(self, k):
        return (self.s + k, self.d)


def remote(src, dst, send, recv, device):
    return pltpu.make_async_remote_copy(
        src_ref=src, dst_ref=dst, send_sem=send, recv_sem=recv, device_id=device, device_id_type=MESH
    )


def signal(semaphore, device):
    pl.semaphore_signal(semaphore, inc=1, device_id=device, device_id_type=MESH)


def half(start, size, which, align):
    return pl.ds(pl.multiple_of(start + which * (size // 2), align), size // 2)


class Gather:
    def __init__(self, pos, units, send, recv, ahead):
        self.pos, self.units, self.ahead = pos, units, ahead
        self.turns = self.settled = 0
        lines = pos.lines
        self.stages = []
        self.plan, self.ready = {}, []
        for u in reversed(range(len(units))):
            at = u
            for stage, lag in enumerate((0, *GATHER_LAGS)):
                at += lag
                self.plan.setdefault(at, []).append((stage, u))
            self.ready.insert(0, at)
        for u, (w, (r0, rows, c0, cols), _) in enumerate(units):
            gh, fh = half(r0, rows, pos.g, 16), half(c0, cols, pos.f, 128)
            ar, ac = pl.ds(r0, rows), pl.ds(c0, cols)
            stages = [[], [], [], []]
            for k in range(1, lines):
                far = pos.line(-k)
                own = w.at[pos.z, pos.c, gh, fh]
                stages[0].append(remote(own, own, send.at[u, k - 1], recv.at[u, k - 1], pos.along(k)))
                j = lines - 1 + k - 1
                block = w.at[far, pos.c, gh, fh]
                stages[1].append(remote(block, block, send.at[u, j], recv.at[u, j], pos.second))
                j = 2 * (lines - 1) + k - 1
                block = w.at[far, pos.c, ar, fh]
                stages[2].append(remote(block, block, send.at[u, j], recv.at[u, j], pos.first))
            j = 3 * (lines - 1)
            block = w.at[:, pos.c, ar, ac]
            stages[3].append(remote(block, block, send.at[u, j], recv.at[u, j], pos.partner))
            self.stages.append(stages)

    def begin(self, u):
        if u < len(self.units):
            own = self.units[u][2]
            if own is not None:
                own.wait()
            for copy in self.stages[u][0]:
                copy.start()

    def turn(self):
        turn = self.turns
        self.turns += 1
        self.begin(turn + self.ahead)
        for stage, u in self.plan.get(turn, ()):
            for i, copy in enumerate(self.stages[u][stage]):
                copy.wait_recv()
                if stage < 2:
                    self.stages[u][stage + 1][i].start()
            if stage == 2:
                self.stages[u][3][0].start()
        self.settle(turn - sum(GATHER_LAGS) - 1)

    def need(self, u):
        while self.turns <= self.ready[u]:
            self.turn()

    def settle(self, count):
        while self.settled < min(count, len(self.units)):
            for stage in self.stages[self.settled]:
                for copy in stage:
                    copy.wait_send()
            self.settled += 1


class Reduce:
    def __init__(self, pos, units, shared, send, recv, free, credit, local):
        self.pos, self.units, self.shared = pos, units, shared
        self.send, self.recv, self.free, self.credit, self.local = send, recv, free, credit, local
        self.turns = self.emitted = self.cleared = self.paired = self.mark = self.settled = 0
        self.copies = {}
        self.steps = self.plan()
        self.site = 0

    def copy(self, u, j, src, dst, device):
        made = remote(src, dst, self.send.at[u, j], self.recv.at[u, j], device)
        self.copies[u, j] = made
        made.start()

    def views(self, u):
        w, landing, out, (r0, rows, c0, cols), _ = self.units[u]
        pos = self.pos
        v = {
            "ar": pl.ds(r0, rows),
            "ac": pl.ds(c0, cols),
            "gh": half(r0, rows, pos.g, 16),
            "go": half(r0, rows, 1 - pos.g, 16),
            "fh": half(c0, cols, pos.f, 128),
            "fo": half(c0, cols, 1 - pos.f, 128),
            "r0": pl.ds(r0, rows // 2),
            "r1": pl.ds(r0 + rows // 2, rows // 2),
            "c0": pl.ds(c0, cols // 2),
            "c1": pl.ds(c0 + cols // 2, cols // 2),
        }
        return w, landing, out, v

    def emit(self, u):
        w, landing, _, v = self.views(u)
        pos = self.pos
        assert u == self.emitted
        self.emitted += 1
        if u >= self.shared:
            pl.semaphore_wait(self.credit.at[u - self.shared], 1)
        self.copy(
            u, 0, w.at[:, 1 - pos.c, v["ar"], v["ac"]], landing.at[:, v["ar"], v["ac"]], pos.partner
        )

    def clear(self, u):
        pos = self.pos
        self.copies[u, 0].wait_send()
        signal(self.free.at[u, 0], pos.first)
        signal(self.free.at[u, 1], pos.second)
        for k in range(1, pos.lines):
            signal(self.free.at[u, 1 + k], pos.along(-k))

    def pair(self, u):
        w, landing, _, v = self.views(u)
        pos, c = self.pos, self.pos.c
        self.copies[u, 0].wait_recv()

        @pl.loop(0, pos.lines)
        def _(z):
            w[z, c, v["ar"], v["ac"]] += landing[z, v["ar"], v["ac"]]

        if u < self.shared:
            signal(self.credit.at[u], pos.partner)
        if self.units[u][4]:
            for k in range(1, pos.lines):
                pl.semaphore_wait(self.free.at[u, 1 + k], 1)
                self.copy(
                    u,
                    2 + k,
                    w.at[pos.line(k), c, v["ar"], v["ac"]],
                    w.at[k - 1, 1 - c, v["ar"], v["ac"]],
                    pos.along(k),
                )
            return
        pl.semaphore_wait(self.free.at[u, 0], 1)
        self.copy(u, 1, w.at[:, c, v["ar"], v["fo"]], w.at[:, 1 - c, v["ar"], v["c0"]], pos.first)

    def one(self, u):
        w, _, _, v = self.views(u)
        pos, c = self.pos, self.pos.c
        self.copies[u, 1].wait_recv()

        @pl.loop(0, pos.lines)
        def _(z):
            w[z, c, v["ar"], v["fh"]] += w[z, 1 - c, v["ar"], v["c0"]]

        pl.semaphore_wait(self.free.at[u, 1], 1)
        self.copy(u, 2, w.at[:, c, v["go"], v["fh"]], w.at[:, 1 - c, v["r0"], v["c1"]], pos.second)

    def two(self, u):
        w, _, _, v = self.views(u)
        pos, c = self.pos, self.pos.c
        self.copies[u, 2].wait_recv()

        @pl.loop(0, pos.lines)
        def _(z):
            w[z, c, v["gh"], v["fh"]] += w[z, 1 - c, v["r0"], v["c1"]]

        for k in range(1, pos.lines):
            pl.semaphore_wait(self.free.at[u, 1 + k], 1)
            self.copy(
                u,
                2 + k,
                w.at[pos.line(k), c, v["gh"], v["fh"]],
                w.at[k - 1, 1 - c, v["r1"], v["c1"]],
                pos.along(k),
            )

    def line(self, u):
        w, _, out, v = self.views(u)
        pos, c, lines = self.pos, self.pos.c, self.pos.lines
        for k in range(1, lines):
            self.copies[u, 2 + k].wait_recv()
        total = w[pos.z, c, v["gh"], v["fh"]].astype(F32)
        for k in range(1, lines):
            total = total + w[k - 1, 1 - c, v["r1"], v["c1"]].astype(F32)
        w[pos.z, c, v["gh"], v["fh"]] = total.astype(LOW)
        self.spread(u)

    def keep(self, u, j, src, there):
        made = pltpu.make_async_copy(src, there, self.local.at[u, j])
        self.copies[u, "local", j] = made
        made.start()

    def spread(self, u):
        w, _, out, v = self.views(u)
        pos, c, lines = self.pos, self.pos.c, self.pos.lines
        mine, there = w.at[pos.z, c, v["gh"], v["fh"]], out.at[v["gh"], v["fh"]]
        self.copy(u, 2 + lines, mine, w.at[lines - 1, 1 - c, v["r1"], v["c1"]], pos.second)
        self.copy(u, 3 + lines, mine, there, pos.first)
        self.keep(u, 0, mine, there)

    def relay(self, u):
        w, _, out, v = self.views(u)
        pos, c, lines = self.pos, self.pos.c, self.pos.lines
        self.copies[u, 2 + lines].wait_recv()
        came, there = w.at[lines - 1, 1 - c, v["r1"], v["c1"]], out.at[v["go"], v["fh"]]
        self.copy(u, 4 + lines, came, there, pos.first)
        self.keep(u, 1, came, there)

    def line_whole(self, u):
        w, _, _, v = self.views(u)
        pos, c, lines = self.pos, self.pos.c, self.pos.lines
        for k in range(1, lines):
            self.copies[u, 2 + k].wait_recv()
        total = w[pos.z, c, v["ar"], v["ac"]].astype(F32)
        for k in range(1, lines):
            total = total + w[k - 1, 1 - c, v["ar"], v["ac"]].astype(F32)
        w[pos.z, c, v["ar"], v["ac"]] = total.astype(LOW)
        pl.semaphore_wait(self.free.at[u, 0], 1)
        self.copy(
            u,
            1,
            w.at[pos.z, c, v["ar"], v["fo"]],
            w.at[lines - 1, 1 - c, v["ar"], v["c0"]],
            pos.first,
        )

    def one_share(self, u):
        w, _, _, v = self.views(u)
        pos, c, lines = self.pos, self.pos.c, self.pos.lines
        self.copies[u, 1].wait_recv()
        w[pos.z, c, v["ar"], v["fh"]] += w[lines - 1, 1 - c, v["ar"], v["c0"]]
        pl.semaphore_wait(self.free.at[u, 1], 1)
        self.copy(
            u,
            2,
            w.at[pos.z, c, v["go"], v["fh"]],
            w.at[lines - 1, 1 - c, v["r0"], v["c1"]],
            pos.second,
        )

    def two_share(self, u):
        w, _, _, v = self.views(u)
        pos, c, lines = self.pos, self.pos.c, self.pos.lines
        self.copies[u, 2].wait_recv()
        w[pos.z, c, v["gh"], v["fh"]] += w[lines - 1, 1 - c, v["r0"], v["c1"]]
        self.spread(u)

    def clears(self, count):
        while self.cleared < count:
            self.clear(self.cleared)
            self.cleared += 1

    def pairs(self, count):
        self.clears(count)
        while self.paired < count:
            self.pair(self.paired)
            self.paired += 1

    def serve(self, turns, eager=False):
        self.pairs(min(self.cleared, self.turns + LEAD))
        self.clears(self.emitted if eager else self.mark)
        self.mark = self.emitted
        for _ in range(turns):
            if all(u < self.paired for _, u in self.steps.get(self.turns, ())):
                self.turn()

    def plan(self):
        plan = {}
        for u in reversed(range(len(self.units))):
            whole = self.units[u][4]
            steps = (self.one, self.two, self.line)
            if whole:
                steps = (self.line_whole, self.one_share, self.two_share)
            steps = (*steps, self.relay)
            usual = LAGS if u < len(self.units) - LAST else LAST_LAGS
            lags = (WHOLE_LAG, *LAGS[:2], LAGS[3]) if whole else usual
            at = u
            for step, lag in zip(steps, lags):
                at += lag
                plan.setdefault(at, []).append((step, u))
        return plan

    def done(self):
        return self.turns > max(self.steps)

    def turn(self):
        if not self.done():
            steps = self.steps.get(self.turns, ())
            self.turns += 1
            self.pairs(max([u + 1 for _, u in steps] + [self.paired]))
            for step, u in steps:
                step(u)
            last = max(at for at, steps in self.steps.items() for _, u in steps if u == self.settled)
            if last <= self.turns - 4:
                self.settle(self.settled + 1)

    def settle(self, count):
        lines = self.pos.lines
        while self.settled < min(count, len(self.units)):
            u = self.settled
            for j in range(1, 5 + lines):
                self.copies[u, j].wait_send()
            for j in range(3 + lines, 5 + lines):
                self.copies[u, j].wait_recv()
            for j in range(2):
                self.copies[u, "local", j].wait()
            self.settled += 1


def dot(a, b):
    return jnp.dot(a, b, preferred_element_type=F32)


def dot_across(a, b):
    return lax.dot_general(a, b, (((1,), (1,)), ((), ())), preferred_element_type=F32)


SAVED = ("x", "x1", "key", "value", "logit", "numer", "denom", "value2", "recept")
SAVED_LOW = ("xk", "xv", "xr", "gated", "xk2", "xr2")
WIDE = 256
BLOCK = 32
LEAD = 12
GATHER_LAGS = (1, 1, 1)
VECTOR_TURNS = 4
AHEAD = 2
FIRST_PIECES = 1
LINE_FIRST = (1,7)
LAGS = (2,3,7,5)
LAST = 3
LAST_LAGS = (3,3,5,3)
WHOLE_LAG = 5
SITES = (1,0,1,1,1,0,0,0,0,0,1,1,0,0,1,1,0,1,0,2,0,1,1,0,0,1,1,1,1,0,1,1,1,2)
VMEM_BYTES = 63 * 2**20


def train_kernel(dims, *refs):
    layers, lines, rows, length, width, hidden = dims
    refs = list(refs)

    def take(count):
        got = refs[:count]
        del refs[:count]
        return got

    matrices = 5
    tokens, doc_starts, decay, first, mix, ln_gain, ln_bias = take(7)
    shards = take(matrices)
    (cotangent,) = take(1)
    output, grad_tokens, vector_out = take(3)
    grad_out = take(matrices)
    names = SAVED + SAVED_LOW + ("squared",)
    store = dict(zip(names, take(len(names))))
    weights = [take(matrices) for _ in range(layers)]
    landing = take(matrices)
    act = dict(zip(names, take(len(names))))
    (live, padded, grad, main, d_one, d_two, d_three, g_low, g_low2, g_low3, g_key2, turned) = take(12)
    vectors, small, vec, v_buf = take(4)
    (g_send, g_recv, own_sem, r_send, r_recv, r_free, r_credit, r_local, save_sem, load_sem, s_send, s_recv, v_send, v_recv) = take(14)
    tokens_total = rows * length
    blocks = length // BLOCK
    chunk = length // 8
    pos = Place(lines)
    s, last = pos.s, 3

    own = {}
    for l in range(layers):
        for m in range(matrices):
            own[l, m] = pltpu.make_async_copy(
                shards[m].at[l], weights[l][m].at[pos.z, pos.c], own_sem.at[l, m]
            )
            own[l, m].start()
    small[...] = jnp.zeros_like(small)
    vectors[...] = jnp.zeros_like(vectors)
    barrier = pltpu.get_barrier_semaphore()
    peers = [pos.along(k) for k in range(1, lines)]
    peers += [pos.first, pos.second, pos.across, pos.partner]
    for peer in peers:
        signal(barrier, peer)
    pl.semaphore_wait(barrier, len(peers))

    def pieces(m, count):
        _, _, r, c = weights[0][m].shape
        if m == 4:
            return [(m, (j * (r // count), r // count, 0, c)) for j in range(count)]
        return [(m, (0, r, j * (c // count), c // count)) for j in range(count)]

    def columns(m, count):
        _, _, r, c = weights[0][m].shape
        return [(m, (0, r, j * (c // count), c // count)) for j in range(count)]

    kvr = pieces(0, 3)
    start_units = [(0, (0, kvr[0][1][1], j * (width // FIRST_PIECES), width // FIRST_PIECES)) for j in range(FIRST_PIECES)]
    rest = kvr[1:] + pieces(1, 1) + pieces(2, 3) + pieces(3, 1) + columns(4, 3)
    layout = [start_units + rest, kvr[:1] + rest]
    base_of = [FIRST_PIECES - 1, FIRST_PIECES + len(rest)]
    gather = Gather(
        pos,
        [(weights[l][m], box, own.pop((l, m), None)) for l in range(layers) for m, box in layout[l]],
        g_send,
        g_recv,
        AHEAD,
    )
    for u in range(gather.ahead):
        gather.begin(u)

    back = pieces(3, 1) + pieces(4, 3) + pieces(2, 3) + pieces(1, 1) + [kvr[2], kvr[0], kvr[1]]
    line_first = LINE_FIRST
    reduce = Reduce(
        pos,
        [
            (weights[l][m], landing[m], grad_out[m].at[l], box, j in line_first)
            for l in reversed(range(layers))
            for j, (m, box) in enumerate(back)
        ],
        len(back),
        r_send,
        r_recv,
        r_free,
        r_credit,
        r_local,
    )

    sub = lax.broadcasted_iota(jnp.int32, (8, width), 0)
    place = lax.broadcasted_iota(jnp.int32, (length, 128), 0)
    at_token = (place % 8) * chunk + place // 8 + s * length
    for r in range(rows):
        start = jnp.zeros((length, 128), F32)
        for j in range(doc_starts.shape[1]):
            start = jnp.where(at_token == doc_starts[r, j], 1.0, start)
        live[r] = 1.0 - start
    p_row = lax.broadcasted_iota(jnp.int32, (length, length), 0)
    p_col = lax.broadcasted_iota(jnp.int32, (length, length), 1)
    order = jnp.where((p_row % 8) * chunk + p_row // 8 == p_col, 1.0, 0.0).astype(LOW)
    order_back = jnp.where((p_col % 8) * chunk + p_col // 8 == p_row, 1.0, 0.0).astype(LOW)

    def spread(tile):
        return jnp.concatenate([tile] * (width // 128), axis=-1)

    def span(i):
        return pl.ds(pl.multiple_of(i * BLOCK, BLOCK), BLOCK)

    def span_on(i):
        return pl.ds(pl.multiple_of(i * BLOCK + 8, 8), BLOCK)

    def tile(i):
        return pl.ds(pl.multiple_of(i * 8, 8), 8)

    def flat(ref):
        return ref[...].reshape(tokens_total, ref.shape[-1])

    def wide(j, base=0, size=WIDE):
        return pl.ds(pl.multiple_of(base + j * size, 128), size)

    def fold(block):
        return jnp.sum(block.reshape(rows * BLOCK // 8, 8, width), axis=0)

    def add_vector(level, row, block):
        vectors[level, row] += fold(block)

    def saving(name, level):
        if level == 0:
            pltpu.make_async_copy(act[name], store[name], save_sem.at[names.index(name)]).start()

    def saved(name, level):
        if level == 1:
            pltpu.make_async_copy(act[name], store[name], save_sem.at[names.index(name)]).wait()

    def loading(some):
        for name in some:
            pltpu.make_async_copy(store[name], act[name], load_sem.at[names.index(name)]).start()

    def loaded(name, level):
        if level == 0:
            pltpu.make_async_copy(store[name], act[name], load_sem.at[names.index(name)]).wait()

    def hop(index, device):
        return remote(small.at[0, index], small.at[1, index], s_send.at[index], s_recv.at[index], device)

    edge_count = 4 * layers

    def edge_start(index, step, there):
        @pl.when(there)
        def _():
            hop(index, pos.later(step)).start()

    def edge_wait(index, step, there):
        @pl.when(there)
        def _():
            hop(index, pos.later(step)).wait_recv()

    def edge_sent(index, step, there):
        @pl.when(there)
        def _():
            hop(index, pos.later(step)).wait_send()

    def chain_hop(level, direction, k):
        slot = edge_count + (level * 2 + direction) * 3
        return remote(
            small.at[0, slot],
            small.at[1, slot + k - 1],
            s_send.at[slot + k - 1],
            s_recv.at[slot + k - 1],
            pos.later(k if direction == 0 else -k),
        )

    def chain_do(level, direction, what):
        for k in range(1, 4):
            inside = s + k <= last if direction == 0 else s - k >= 0
            from_inside = s - k >= 0 if direction == 0 else s + k <= last

            @pl.when(from_inside if what == "wait_recv" else inside)
            def _():
                getattr(chain_hop(level, direction, k), what)()

    def chain_total(level, direction, r):
        slot = edge_count + (level * 2 + direction) * 3
        numer = jnp.zeros((1, width), F32)
        denom = jnp.zeros((1, width), F32)
        for k in (3, 2, 1):
            through = small[1, slot + k - 1, 3 * r : 3 * r + 1, :]
            numer = through * numer + small[1, slot + k - 1, 3 * r + 1 : 3 * r + 2, :]
            denom = through * denom + small[1, slot + k - 1, 3 * r + 2 : 3 * r + 3, :]
        return numer, denom

    def centred(x):
        center = x - jnp.mean(x, -1, keepdims=True)
        spread_ = jnp.mean(center * center, -1, keepdims=True)
        scale = lax.rsqrt(spread_ + EPSILON)
        return center * scale, scale

    def normalize_into(x_ref, level, which):
        gain, bias = ln_gain[level, which : which + 1, :], ln_bias[level, which : which + 1, :]

        @pl.loop(0, blocks)
        def _(i):
            n, _ = centred(x_ref[:, span(i), :])
            padded[:, span_on(i), :] = n * gain + bias

    def wrap_in(index):
        for r in range(rows):
            moved = pltpu.roll(padded[r, length : length + 8, :], 1, 0)
            padded[r, 0:8, :] = jnp.where(sub == 0, small[1, index, r : r + 1, :], moved)

    def normalize_shift(x_ref, level, which, outs, rates, unit):
        index = level * 2 + which
        normalize_into(x_ref, level, which)
        for r in range(rows):
            small[0, index, r : r + 1, :] = padded[r, length + 7 : length + 8, :]
        edge_start(index, 1, s < last)
        gather.need(unit)
        edge_wait(index, 1, s > 0)
        wrap_in(index)

        @pl.loop(0, blocks)
        def _(i):
            h = padded[:, span_on(i), :]
            before = padded[:, span(i), :] * spread(live[:, span(i), :])
            for out, j in zip(outs, rates):
                rate = mix[j, level : level + 1, :]
                out[:, span(i), :] = (h * rate + before * (1.0 - rate)).astype(LOW)

    def project(x_ref, w, base, count, put):
        @pl.loop(0, count // WIDE)
        def _(j):
            block = w[:, :, :, wide(j, base)].reshape(-1, WIDE)
            put(j, dot(flat(x_ref), block).reshape(rows, length, WIDE))

    def put_in(ref):
        def put(j, block):
            ref[:, :, wide(j)] = block

        return put

    def back_project(g_ref, w, base, count, out_ref):
        size = min(width, count)
        for j in range(count // size):
            block = w[:, :, :, base + j * size : base + (j + 1) * size].reshape(-1, size)
            got = dot_across(g_ref[:, :, j * size : (j + 1) * size].reshape(tokens_total, size), block)
            got = got.reshape(rows, length, width)
            if j == 0:
                out_ref[...] = got
            else:
                out_ref[...] += got

    def outer(x_ref, g_ref, w, base, count, g_base=0):
        turned[...] = flat(x_ref).T

        @pl.loop(0, count // WIDE)
        def _(j):
            g = g_ref[:, :, wide(j, g_base)].reshape(tokens_total, WIDE)
            got = dot(turned[...], g).astype(LOW)
            w[:, :, :, wide(j, base)] = got.reshape(lines, 2, width // (2 * lines), WIDE)

    def keep_rows(level):
        rate = jnp.exp(decay[level : level + 1, :])
        return jnp.broadcast_to(jnp.exp(-rate), (8, width)), rate

    def scan_local(level):
        keep, _ = keep_rows(level)

        def step(i, carry):
            out = []
            for r in range(rows):
                numer, denom, alive = carry[3 * r : 3 * r + 3]
                l128 = live[r, tile(i), :]
                l_now = spread(l128)
                lifted = jnp.exp(act["key"][r, tile(i), :])
                numer = keep * (numer * l_now) + lifted * act["value"][r, tile(i), :]
                denom = keep * (denom * l_now) + lifted
                out += [numer, denom, alive * l128]
            return tuple(out)

        zero = jnp.zeros((8, width), F32)
        carry = lax.fori_loop(0, chunk, step, (zero, zero, jnp.ones((8, 128), F32)) * rows, unroll=2)
        faded = keep
        for _ in range(chunk.bit_length() - 1):
            faded = faded * faded
        slot = edge_count + (level * 2) * 3
        before = []
        for r in range(rows):
            numer, denom, alive = carry[3 * r : 3 * r + 3]
            through = spread(alive) * faded
            vec[level, r] = through
            for shift in (1, 2, 4):
                inside = sub >= shift
                n_b, d_b, t_b = (pltpu.roll(a, shift, 0) for a in (numer, denom, through))
                numer = jnp.where(inside, through * n_b + numer, numer)
                denom = jnp.where(inside, through * d_b + denom, denom)
                through = jnp.where(inside, through * t_b, through)
            for j, a in enumerate((through, numer, denom)):
                small[0, slot, 3 * r + j : 3 * r + j + 1, :] = a[7:8, :]
            at_start = sub == 0
            n_b, d_b, t_b = (pltpu.roll(a, 1, 0) for a in (numer, denom, through))
            before.append(
                (jnp.where(at_start, 0.0, n_b), jnp.where(at_start, 0.0, d_b), jnp.where(at_start, 1.0, t_b))
            )
        chain_do(level, 0, "start")
        return before

    def scan_final(level, before):
        chain_do(level, 0, "wait_recv")
        keep, _ = keep_rows(level)
        bonus = jnp.broadcast_to(jnp.exp(first[level : level + 1, :]), (8, width))
        carry = []
        for r in range(rows):
            n_in, d_in = chain_total(level, 0, r)
            n_b, d_b, t_b = before[r]
            carry += [t_b * n_in + n_b, t_b * d_in + d_b]

        def step(i, carry):
            out = []
            for r in range(rows):
                numer, denom = carry[2 * r : 2 * r + 2]
                l_now = spread(live[r, tile(i), :])
                numer, denom = numer * l_now, denom * l_now
                act["numer"][r, tile(i), :] = numer
                act["denom"][r, tile(i), :] = denom
                value = act["value"][r, tile(i), :]
                lifted = jnp.exp(act["key"][r, tile(i), :])
                now = bonus * lifted
                main[r, tile(i), :] = (numer + now * value) / (denom + now)
                out += [keep * numer + lifted * value, keep * denom + lifted]
            return tuple(out)

        lax.fori_loop(0, chunk, step, tuple(carry), unroll=2)

    for r in range(rows):
        act["x"][r] = dot(order, tokens[r])
        grad[r] = dot(order, cotangent[r])

    def forward_layer(level):
        w_kvr, w_out, w_fkey, w_frec, w_fval = weights[level]
        base = base_of[level]
        for name in ("xk", "xv", "xr"):
            saved(name, level)
        normalize_shift(act["x"], level, 0, [act["xk"], act["xv"], act["xr"]], (0, 1, 2), base)
        saving("x", level)
        for j, (low, name) in enumerate((("xk", "key"), ("xv", "value"), ("xr", "logit"))):
            saving(low, level)
            saved(name, level)
            gather.need(base + j)
            project(act[low], w_kvr, j * width, width, put_in(act[name]))
            saving(name, level)
            if j == 1:
                before = scan_local(level)
        saved("numer", level)
        saved("denom", level)
        scan_final(level, before)
        saving("numer", level)
        saving("denom", level)
        saved("gated", level)

        @pl.loop(0, blocks)
        def _(i):
            act["gated"][:, span(i), :] = (
                jax.nn.sigmoid(act["logit"][:, span(i), :]) * main[:, span(i), :]
            ).astype(LOW)

        saving("gated", level)
        gather.need(base + 3)
        saved("x1", level)

        def put_x1(j, block):
            act["x1"][:, :, wide(j)] = act["x"][:, :, wide(j)] + block

        project(act["gated"], w_out, 0, width, put_x1)
        saving("x1", level)
        saved("xk2", level)
        saved("xr2", level)
        normalize_shift(act["x1"], level, 1, [act["xk2"], act["xr2"]], (3, 4), base + 4)
        saving("xk2", level)
        saving("xr2", level)
        saved("squared", level)
        third = hidden // 3
        for j in range(3):
            gather.need(base + 4 + j)

            def put_squared(i, block, j=j):
                up = jnp.maximum(block, 0.0)
                act["squared"][:, :, wide(i, j * third)] = (up * up).astype(LOW)

            project(act["xk2"], w_fkey, j * third, third, put_squared)
        saving("squared", level)
        gather.need(base + 7)
        saved("recept", level)
        project(act["xr2"], w_frec, 0, width, put_in(act["recept"]))
        saving("recept", level)
        saved("value2", level)
        share = hidden // lines
        for j in range(width // WIDE):
            gather.need(base + 8 + j)
            total = None
            for z in range(lines):
                got = dot(
                    act["squared"][:, :, z * share : (z + 1) * share].reshape(tokens_total, share),
                    w_fval[z, :, :, j * WIDE : (j + 1) * WIDE].reshape(share, WIDE),
                )
                total = got if total is None else total + got
            act["value2"][:, :, j * WIDE : (j + 1) * WIDE] = total.reshape(rows, length, WIDE)
        saving("value2", level)
        saved("x", level + 1)

        @pl.loop(0, blocks)
        def _(i):
            up = jax.nn.sigmoid(act["recept"][:, span(i), :]) * act["value2"][:, span(i), :]
            after = act["x1"][:, span(i), :] + up
            if level + 1 < layers:
                act["x"][:, span(i), :] = after
            else:
                g_low3[:, span(i), :] = after.astype(LOW)

    for level in range(layers):
        forward_layer(level)
    def blend_back(level, which, d_refs, rates):
        index = level * 2 + which
        wrap_in(index)

        @pl.loop(0, blocks)
        def _(i):
            l_now = spread(live[:, span(i), :])
            change = padded[:, span_on(i), :] - padded[:, span(i), :] * l_now
            direct, shifted = None, None
            for ref, j in zip(d_refs, rates):
                d = ref[:, span(i), :]
                rate = mix[j, level : level + 1, :]
                add_vector(level, 2 + j, d * change)
                direct = d * rate if direct is None else direct + d * rate
                shifted = d * (1.0 - rate) if shifted is None else shifted + d * (1.0 - rate)
            main[:, span(i), :] = direct
            d_refs[0][:, span(i), :] = shifted * l_now

        back_index = 2 * layers + index
        for r in range(rows):
            small[0, back_index, r : r + 1, :] = d_refs[0][r, 0:1, :]
        edge_start(back_index, -1, s > 0)

    def normalize_back(level, which, x_ref, q_ref, write):
        index = level * 2 + which
        back_index = 2 * layers + index
        edge_wait(back_index, -1, s < last)
        for r in range(rows):
            moved = pltpu.roll(q_ref[r, 0:8, :], 7, 0)
            padded[r, length : length + 8, :] = jnp.where(
                sub == 7, small[1, back_index, r : r + 1, :], moved
            )
            padded[r, 8:length, :] = q_ref[r, 8:length, :]
        gain = ln_gain[level, which : which + 1, :]

        @pl.loop(0, blocks)
        def _(i):
            d_h = main[:, span(i), :] + padded[:, span_on(i), :]
            n, scale = centred(x_ref[:, span(i), :])
            add_vector(level, 7 + which, d_h * n)
            add_vector(level, 9 + which, d_h)
            e = d_h * gain
            inner = e - jnp.mean(e, -1, keepdims=True) - n * jnp.mean(e * n, -1, keepdims=True)
            after = grad[:, span(i), :] + scale * inner
            grad[:, span(i), :] = after
            write(i, after)

    def wkv_terms(r, i, bonus):
        value = act["value"][r, tile(i), :]
        lifted = jnp.exp(act["key"][r, tile(i), :])
        now = bonus * lifted
        numer, denom = act["numer"][r, tile(i), :], act["denom"][r, tile(i), :]
        part = 1.0 / (denom + now)
        result = (numer + now * value) * part
        return value, lifted, now, numer, denom, part, result

    def scan_back_local(level):
        keep, _ = keep_rows(level)
        bonus = jnp.broadcast_to(jnp.exp(first[level : level + 1, :]), (8, width))

        def step(j, carry):
            i = chunk - 1 - j
            out = []
            for r in range(rows):
                h_n, h_d = carry[2 * r : 2 * r + 2]
                value, lifted, now, numer, denom, part, result = wkv_terms(r, i, bonus)
                gate = jax.nn.sigmoid(act["logit"][r, tile(i), :])
                d_gated = main[r, tile(i), :]
                d_wkv = d_gated * gate
                d_two[r, tile(i), :] = d_gated * result * gate * (1.0 - gate)
                main[r, tile(i), :] = d_wkv
                l_now = spread(live[r, tile(i), :])
                a = d_wkv * part
                out += [l_now * (a + keep * h_n), l_now * (keep * h_d - a * result)]
            return tuple(out)

        zero = jnp.zeros((8, width), F32)
        carry = lax.fori_loop(0, chunk, step, (zero, zero) * rows)
        slot = edge_count + (level * 2 + 1) * 3
        after = []
        for r in range(rows):
            h_n, h_d = carry[2 * r : 2 * r + 2]
            through = vec[level, r]
            for shift in (1, 2, 4):
                inside = sub < 8 - shift
                n_a, d_a, t_a = (pltpu.roll(a, 8 - shift, 0) for a in (h_n, h_d, through))
                h_n = jnp.where(inside, through * n_a + h_n, h_n)
                h_d = jnp.where(inside, through * d_a + h_d, h_d)
                through = jnp.where(inside, through * t_a, through)
            for j, a in enumerate((through, h_n, h_d)):
                small[0, slot, 3 * r + j : 3 * r + j + 1, :] = a[0:1, :]
            at_end = sub == 7
            n_a, d_a, t_a = (pltpu.roll(a, 7, 0) for a in (h_n, h_d, through))
            after.append(
                (jnp.where(at_end, 0.0, n_a), jnp.where(at_end, 0.0, d_a), jnp.where(at_end, 1.0, t_a))
            )
        chain_do(level, 1, "start")
        return after

    def scan_back_final(level, after):
        chain_do(level, 1, "wait_recv")
        keep, rate = keep_rows(level)
        bonus = jnp.broadcast_to(jnp.exp(first[level : level + 1, :]), (8, width))
        zero = jnp.zeros((8, width), F32)
        carry = [zero, zero]
        for r in range(rows):
            n_in, d_in = chain_total(level, 1, r)
            n_a, d_a, t_a = after[r]
            carry += [t_a * n_in + n_a, t_a * d_in + d_a]

        def step(j, carry):
            i = chunk - 1 - j
            d_keep, d_first = carry[:2]
            out = []
            for r in range(rows):
                h_n, h_d = carry[2 + 2 * r : 4 + 2 * r]
                value, lifted, now, numer, denom, part, result = wkv_terms(r, i, bonus)
                a = main[r, tile(i), :] * part
                d_now = a * (value - result) * now
                d_keep = d_keep + numer * h_n + denom * h_d
                d_first = d_first + d_now
                d_one[r, tile(i), :] = d_now + lifted * (value * h_n + h_d)
                d_two[r, tile(i), :] = a * now + lifted * h_n
                l_now = spread(live[r, tile(i), :])
                out += [l_now * (a + keep * h_n), l_now * (keep * h_d - a * result)]
            return (d_keep, d_first, *out)

        carry = lax.fori_loop(0, chunk, step, tuple(carry))
        vectors[level, 0] += carry[0] * (-rate * keep)
        vectors[level, 1] += carry[1]

    def to_low(src, dst):
        @pl.loop(0, blocks)
        def _(i):
            dst[:, span(i), :] = src[:, span(i), :].astype(LOW)

    ffn_names = ("value2", "recept", "squared", "xk2", "xr2", "x1")
    att_names = tuple(n for n in names if n not in ffn_names)

    def serve(eager=False):
        reduce.serve(SITES[reduce.site], eager)
        reduce.site += 1

    def backward_layer(level):
        w_kvr, w_out, w_fkey, w_frec, w_fval = weights[level]
        base = (layers - 1 - level) * len(back)
        third = hidden // 3
        share = hidden // lines
        loaded("value2", level)
        loaded("recept", level)

        @pl.loop(0, blocks)
        def _(i):
            gate = jax.nn.sigmoid(act["recept"][:, span(i), :])
            g = grad[:, span(i), :]
            g_low[:, span(i), :] = (g * gate).astype(LOW)
            g_low2[:, span(i), :] = (g * act["value2"][:, span(i), :] * gate * (1.0 - gate)).astype(LOW)

        loaded("xr2", level)
        back_project(g_low2, w_frec, 0, width, d_two)
        gather.settle(len(gather.units))
        outer(act["xr2"], g_low2, w_frec, 0, width)
        reduce.emit(base)
        if level == layers - 1:
            for r in range(rows):
                output[r] = dot(order_back, g_low3[r]).astype(LOW)
        loaded("squared", level)

        for half_way in range(2):

            @pl.loop(half_way * (lines // 2), (half_way + 1) * (lines // 2))
            def _(z):
                got = dot_across(flat(g_low), w_fval[z].reshape(share, width))
                got = got.reshape(rows, length, share)
                root = jnp.sqrt(act["squared"][:, :, wide(z, 0, share)].astype(F32))
                g_key2[:, :, wide(z, 0, share)] = (got * (2.0 * root)).astype(LOW)

            serve(True)

        @pl.loop(0, lines)
        def _(z):
            turned[...] = act["squared"][:, :, wide(z, 0, share)].reshape(tokens_total, share).T
            for j in range(width // WIDE):
                g = g_low[:, :, j * WIDE : (j + 1) * WIDE].reshape(tokens_total, WIDE)
                got = dot(turned[...], g).astype(LOW)
                w_fval[z, :, :, j * WIDE : (j + 1) * WIDE] = got.reshape(2, share // 2, WIDE)

        for j in range(3):
            reduce.emit(base + 1 + j)
        serve()
        back_project(g_key2, w_fkey, 0, hidden, d_one)
        serve()
        loaded("xk2", level)
        for j in range(3):
            outer(act["xk2"], g_key2, w_fkey, j * third, third, j * third)
            reduce.emit(base + 4 + j)
            serve()
        loaded("x1", level)
        normalize_into(act["x1"], level, 1)
        blend_back(level, 1, [d_one, d_two], (3, 4))
        serve()

        def write_att(i, after):
            g_low3[:, span(i), :] = after.astype(LOW)

        normalize_back(level, 1, act["x1"], d_one, write_att)
        serve()
        if level == 1:
            loading(ffn_names)
        back_project(g_low3, w_out, 0, width, main)
        loaded("gated", level)
        outer(act["gated"], g_low3, w_out, 0, width)
        reduce.emit(base + 7)
        serve()
        for name in ("logit", "key", "value", "numer", "denom"):
            loaded(name, level)
        after = scan_back_local(level)
        serve()
        to_low(d_two, g_low)
        loaded("xr", level)
        back_project(g_low, w_kvr, 2 * width, width, d_three)
        outer(act["xr"], g_low, w_kvr, 2 * width, width)
        reduce.emit(base + 8)
        serve()
        scan_back_final(level, after)
        serve()
        to_low(d_one, g_low2)
        to_low(d_two, g_low3)
        loaded("xk", level)
        loaded("xv", level)
        back_project(g_low2, w_kvr, 0, width, d_one)
        outer(act["xk"], g_low2, w_kvr, 0, width)
        reduce.emit(base + 9)
        serve()
        back_project(g_low3, w_kvr, width, width, d_two)
        outer(act["xv"], g_low3, w_kvr, width, width)
        reduce.emit(base + 10)
        serve()
        loaded("x", level)
        normalize_into(act["x"], level, 0)
        blend_back(level, 0, [d_one, d_two, d_three], (0, 1, 2))
        serve()

        def write_none(i, after):
            g_low[:, span(i), :] = after.astype(LOW)

        normalize_back(level, 0, act["x"], d_one, write_none)
        serve()
        if level == 1:
            loading(att_names)

    for level in reversed(range(layers)):
        backward_layer(level)
    for r in range(rows):
        grad_tokens[r] = dot(order_back, g_low[r]).astype(LOW)

    count = vectors.shape[1]

    def vector_hop(j, device):
        source = min(j, 3)
        return remote(v_buf.at[0, source], v_buf.at[1, j], v_send.at[j], v_recv.at[j], device)

    def vector_stage(stage):
        if stage == 0:
            for level in range(layers):
                for row in range(count):
                    j = level * count + row
                    v_buf[0, 0, j : j + 1, :] = jnp.sum(vectors[level, row], axis=0, keepdims=True)
        elif stage < 4:
            vector_hop(stage - 1, pos.partner).wait_recv()
            v_buf[0, stage] = v_buf[0, stage - 1] + v_buf[1, stage - 1]
        if stage < 3:
            vector_hop(stage, (pos.partner, pos.first, pos.second)[stage]).start()
        elif stage == 3:
            for k in range(1, lines):
                vector_hop(2 + k, pos.along(k)).start()
        else:
            total = v_buf[0, 3]
            for k in range(1, lines):
                vector_hop(2 + k, pos.along(k)).wait_recv()
                total = total + v_buf[1, 2 + k]
            vector_out[...] = total

    for stage in range(5):
        vector_stage(stage)
        for _ in range(VECTOR_TURNS):
            reduce.turn()
    while not reduce.done():
        reduce.turn()
    reduce.settle(len(reduce.units))
    for j, device in enumerate((pos.partner, pos.first, pos.second)):
        vector_hop(j, device).wait_send()
    for k in range(1, lines):
        vector_hop(2 + k, pos.along(k)).wait_send()
    for level in range(layers):
        for which in range(2):
            index = level * 2 + which
            edge_sent(index, 1, s < last)
            edge_sent(2 * layers + index, -1, s > 0)
        for direction in range(2):
            chain_do(level, direction, "wait_send")


def finish_kernel(dims, *refs):
    layers, share, moved = dims
    ins, sums = refs[:moved], refs[moved]
    outs = refs[moved + 1 : 2 * moved + 1]
    decay, first, mix, gain, bias = refs[2 * moved + 1 : 2 * moved + 6]
    came = refs[2 * moved + 6 : 3 * moved + 6]
    wide = came[:2] + refs[3 * moved + 6 : 4 * moved + 4]
    in_sem, out_sem = refs[4 * moved + 4 :]
    by_size = sorted(range(moved), key=lambda i: -ins[i].size)
    parts = [(i, j) for i in by_size for j in range(layers)]

    def arrive(i, j):
        return pltpu.make_async_copy(ins[i].at[j], came[i].at[j], in_sem.at[i, j])

    def leave(i, j):
        return pltpu.make_async_copy(wide[i].at[j], outs[i].at[j], out_sem.at[i, j])

    for part in parts:
        arrive(*part).start()
    offset = lax.axis_index("dp") * share
    width = sums.shape[1]
    own = pltpu.roll(sums[...], lax.rem(width - offset, width), 1)[:, :share]
    for level in range(layers):
        at = level * 11
        decay[level : level + 1, :] = own[at : at + 1]
        first[level : level + 1, :] = own[at + 1 : at + 2]
        for j in range(5):
            mix[j, level : level + 1, :] = own[at + 2 + j : at + 3 + j]
        for j in range(2):
            gain[level, j : j + 1, :] = own[at + 7 + j : at + 8 + j]
            bias[level, j : j + 1, :] = own[at + 9 + j : at + 10 + j]
    for i, j in parts:
        arrive(i, j).wait()
        if i >= 2:
            rows = ins[i].shape[1]

            @pl.loop(0, rows // 32)
            def _(k):
                at = pl.ds(pl.multiple_of(k * 32, 32), 32)
                wide[i][j, at, :] = came[i][j, at, :].astype(F32)

        leave(i, j).start()
    for part in parts:
        leave(*part).wait()


def fast_body(
    tokens, doc_starts, decay, first, mix, ln_gain, ln_bias,
    att_kvr, att_out, ffn_key, ffn_recept, ffn_value, cotangent,
):
    rows, length, width = tokens.shape
    layers, hidden = decay.shape[0], ffn_key.shape[2]
    lines = lax.axis_size("dp") // 2
    shards = (att_kvr, att_out, ffn_key, ffn_recept, ffn_value)
    plain, low = (rows, length, width), LOW
    saved = [jax.ShapeDtypeStruct(plain, F32)] * len(SAVED)
    saved += [jax.ShapeDtypeStruct(plain, low)] * len(SAVED_LOW)
    saved += [jax.ShapeDtypeStruct((rows, length, hidden), low)]
    vector_rows = -(-layers * 11 // 8) * 8
    outs = [
        jax.ShapeDtypeStruct(plain, low),
        jax.ShapeDtypeStruct(plain, low),
        jax.ShapeDtypeStruct((vector_rows, width), F32),
    ]
    outs += [jax.ShapeDtypeStruct(w.shape, low) for w in shards]
    outs += saved
    vmem, anywhere = pl.BlockSpec(memory_space=pltpu.VMEM), pl.BlockSpec(memory_space=pl.ANY)
    units = 11 * layers + FIRST_PIECES - 1
    hops = 4 * layers + 6 * layers
    dma, plain_f32, plain_low = pltpu.SemaphoreType.DMA, pltpu.VMEM(plain, F32), pltpu.VMEM(plain, low)
    scratch = [pltpu.VMEM((lines, 2) + w.shape[1:], low) for _ in range(layers) for w in shards]
    scratch += [pltpu.VMEM((lines,) + w.shape[1:], low) for w in shards]
    scratch += [pltpu.VMEM(a.shape, a.dtype) for a in saved]
    scratch += [
        pltpu.VMEM((rows, length, 128), F32),
        pltpu.VMEM((rows, length + 8, width), F32),
        plain_f32,
        plain_f32,
        plain_f32,
        plain_f32,
        plain_f32,
        plain_low,
        plain_low,
        plain_low,
        pltpu.VMEM((rows, length, hidden), low),
        pltpu.VMEM((width, rows * length), low),
        pltpu.VMEM((layers, 11, 8, width), F32),
        pltpu.VMEM((2, hops, 8, width), F32),
        pltpu.VMEM((layers, rows, 8, width), F32),
        pltpu.VMEM((2, 6, vector_rows, width), F32),
        dma((units, 3 * lines - 2)),
        dma((units, 3 * lines - 2)),
        dma((layers, len(shards))),
        dma((units, 5 + lines)),
        dma((units, 5 + lines)),
        pltpu.SemaphoreType.REGULAR((units, 1 + lines)),
        pltpu.SemaphoreType.REGULAR((11,)),
        dma((units, 2)),
        dma((len(saved),)),
        dma((len(saved),)),
        dma((hops,)),
        dma((hops,)),
        dma((6,)),
        dma((6,)),
    ]
    smem = pl.BlockSpec(memory_space=pltpu.SMEM)
    got = pl.pallas_call(
        functools.partial(train_kernel, (layers, lines, rows, length, width, hidden)),
        out_shape=outs,
        in_specs=[vmem, smem] + [vmem] * 5 + [anywhere] * len(shards) + [vmem],
        out_specs=[vmem] * 3 + [anywhere] * (len(outs) - 3),
        scratch_shapes=scratch,
        compiler_params=pltpu.CompilerParams(
            collective_id=0, has_side_effects=True, vmem_limit_bytes=VMEM_BYTES
        ),
    )(tokens, doc_starts, decay, first, jnp.swapaxes(mix, 0, 1), ln_gain, ln_bias, *shards, cotangent)
    share = width // lax.axis_size("dp")
    final = [jax.ShapeDtypeStruct(plain, low)] * 2
    final += [jax.ShapeDtypeStruct(w.shape, F32) for w in shards]
    final += [jax.ShapeDtypeStruct((layers, share), F32)] * 2
    final += [jax.ShapeDtypeStruct((5, layers, share), F32)]
    final += [jax.ShapeDtypeStruct((layers, 2, share), F32)] * 2
    moved = 2 + len(shards)
    done = pl.pallas_call(
        functools.partial(finish_kernel, (layers, share, moved)),
        out_shape=final,
        in_specs=[anywhere] * moved + [vmem],
        out_specs=[anywhere] * moved + [vmem] * 5,
        scratch_shapes=[pltpu.VMEM(a.shape, low) for a in final[:moved]]
        + [pltpu.VMEM(a.shape, F32) for a in final[2:moved]]
        + [dma((moved, layers)), dma((moved, layers))],
        compiler_params=pltpu.CompilerParams(vmem_limit_bytes=VMEM_BYTES),
    )(got[0], got[1], *got[3 : 3 + len(shards)], got[2])
    output, grad_tokens = done[:2]
    g_decay, g_first, g_mix, g_gain, g_bias = done[moved:]
    return (
        output,
        grad_tokens,
        g_decay,
        g_first,
        jnp.swapaxes(g_mix, 0, 1),
        g_gain,
        g_bias,
        *done[2:moved],
    )


def kernel_fits(tokens, decay, ffn_key, shards):
    rows, length, width = tokens.shape
    lines = lax.axis_size("dp") // 2
    return (
        lax.axis_size("seq") == 4
        and lax.axis_size("dp") == 2 * lines
        and lines > 1
        and decay.shape[0] == 2
        and rows == 2
        and length % BLOCK == 0
        and length & (length - 1) == 0
        and width % WIDE == 0
        and ffn_key.shape[2] == width * lines
        and all(w.shape[1] % 32 == 0 and w.shape[2] % WIDE == 0 for w in shards)
    )


def from_behind(block, axis, distance):
    devices = range(lax.axis_size(axis))
    route = [(i - distance, i) for i in devices if i - distance in devices]
    return lax.ppermute(block, axis, route)


def normalize(stream, gain_row, bias_row):
    center = stream - jnp.mean(stream, -1, keepdims=True)
    spread = jnp.mean(center * center, -1, keepdims=True)
    return center * lax.rsqrt(spread + EPSILON) * gain_row + bias_row


def blend(hidden, edge_row, rates, starts):
    earlier = (
        jnp.concatenate([edge_row[:, None, :], hidden[:, :-1, :]], axis=1)
        * (1.0 - starts)[:, :, None]
    )
    return tuple((hidden * rates[j] + earlier * (1.0 - rates[j]) for j in range(rates.shape[0])))


def product(inputs, matrix):
    return jnp.einsum("rcd,de->rce", inputs, matrix, preferred_element_type=jnp.float32)


def product_back(grads, matrix):
    return jnp.einsum("rce,de->rcd", grads, matrix, preferred_element_type=jnp.float32)


def outer_sum(inputs, grads):
    return jnp.einsum("rcd,rce->de", inputs, grads, preferred_element_type=jnp.float32)


def wkv_tokens(key_proj, value_proj, decay_row, foremost_line_entry, numer_in, denom_in, starts):
    rows, length, width = key_proj.shape
    block = math.gcd(length, 64)
    count = length // block
    rate = jnp.exp(decay_row)
    local = jnp.arange(block, dtype=jnp.float32)
    lower = (local[:, None] > local[None, :]).astype(jnp.float32)
    grow = jnp.exp(local[:, None] * rate[None, :])
    shrink = jnp.exp(-(local[:, None] - 1.0) * rate[None, :])
    fade = jnp.exp(-local[:, None] * rate[None, :])
    keep_rate = jnp.exp(-rate)

    def one_block(carry, inputs):
        accrued_dividend_total, accrued_divisor_total = carry
        present_lookup_entry, present_payload_entry, start_now = inputs
        counted = jnp.cumsum(start_now, axis=1)
        same = lower[None] * (counted[:, :, None] == counted[:, None, :]).astype(jnp.float32)
        alive = (counted == 0.0).astype(jnp.float32)[:, :, None]
        key_exp = jnp.exp(present_lookup_entry)
        lifted = grow[None] * key_exp
        numer_sum = jnp.einsum(
            "rji,ric->rjc", same, lifted * present_payload_entry, precision=lax.Precision.HIGHEST
        )
        denom_sum = jnp.einsum("rji,ric->rjc", same, lifted, precision=lax.Precision.HIGHEST)
        present_dividend_term = (
            shrink[None] * numer_sum + fade[None] * alive * accrued_dividend_total[:, None, :]
        )
        present_divisor_term = (
            shrink[None] * denom_sum + fade[None] * alive * accrued_divisor_total[:, None, :]
        )
        present_reward_term = jnp.exp(foremost_line_entry + present_lookup_entry)
        recurrence_result = (
            present_dividend_term + present_reward_term * present_payload_entry
        ) / (present_divisor_term + present_reward_term)
        numer_end = (
            keep_rate * present_dividend_term[:, -1] + key_exp[:, -1] * present_payload_entry[:, -1]
        )
        denom_end = keep_rate * present_divisor_term[:, -1] + key_exp[:, -1]
        return ((numer_end, denom_end), recurrence_result)

    def split(values):
        return jnp.swapaxes(values.reshape((rows, count, block) + values.shape[2:]), 0, 1)

    carry_end, results = lax.scan(
        one_block, (numer_in, denom_in), (split(key_proj), split(value_proj), split(starts))
    )
    return jnp.swapaxes(results, 0, 1).reshape(rows, length, width)


def span_transform(key_proj, value_proj, decay_row, starts):
    length = key_proj.shape[1]
    rate = jnp.exp(decay_row)
    steps = jnp.arange(length, dtype=jnp.float32)
    last_start = jnp.max(steps[None, :] * starts, axis=1)
    after = (steps[None, :] >= last_start[:, None]).astype(jnp.float32)
    weight = jnp.exp(key_proj - (length - 1.0 - steps)[None, :, None] * rate) * after[:, :, None]
    carry_numer = jnp.sum(weight * value_proj, axis=1)
    carry_denom = jnp.sum(weight, axis=1)
    through = jnp.prod(1.0 - starts, axis=1)[:, None] * jnp.exp(-length * rate)[None, :]
    return (through, carry_numer, carry_denom)


def body(
    tokens,
    doc_starts,
    decay,
    first,
    mix,
    ln_gain,
    ln_bias,
    att_kvr,
    att_out,
    ffn_key,
    ffn_recept,
    ffn_value,
    cotangent,
):
    shards = (att_kvr, att_out, ffn_key, ffn_recept, ffn_value)
    if kernel_fits(tokens, decay, ffn_key, shards):
        return fast_body(
            tokens, doc_starts, decay, first, mix, ln_gain, ln_bias, *shards, cotangent
        )
    row_total, token_total, width = tokens.shape
    layer_total = decay.shape[0]
    batches = 2
    per_batch = row_total // batches
    positions = lax.axis_index("seq") * token_total + jnp.arange(token_total, dtype=jnp.int32)
    starts_all = jnp.any(doc_starts[:, :, None] == positions[None, None, :], axis=1).astype(
        jnp.float32
    )
    empty = jnp.zeros((per_batch, width), jnp.float32)

    def edge_of(hidden):
        return from_behind(hidden[:, -1, :], "seq", 1)

    def edge_back(grad_edge):
        return from_behind(grad_edge, "seq", -1)

    def chain_forward(through, carry_numer, carry_denom):
        incoming = (empty, empty)
        sent_numer, sent_denom = (carry_numer, carry_denom)
        for relay_turn in range(lax.axis_size("seq") - 1):
            incoming = from_behind((sent_numer, sent_denom), "seq", 1)
            sent_numer = through * incoming[0] + carry_numer
            sent_denom = through * incoming[1] + carry_denom
        return incoming

    def forward_layer(stream, level, matrices, starts):
        w_kvr, w_out, w_fkey, w_frec, w_fval = matrices
        hidden, norm_one = jax.vjp(normalize, stream, ln_gain[level, 0], ln_bias[level, 0])
        edge_row = edge_of(hidden)
        blends, blend_one = jax.vjp(
            lambda h_in, e_in, r_in: blend(h_in, e_in, r_in, starts),
            hidden,
            edge_row,
            mix[level, :3],
        )
        xk_low, xv_low, xr_low = [b.astype(jnp.bfloat16) for b in blends]
        key_proj = product(xk_low, w_kvr[:, :width])
        value_proj = product(xv_low, w_kvr[:, width : 2 * width])
        logit = product(xr_low, w_kvr[:, 2 * width :])
        transform, transform_one = jax.vjp(
            lambda k_in, v_in, d_in: span_transform(k_in, v_in, d_in, starts),
            key_proj,
            value_proj,
            decay[level],
        )
        numer_in, denom_in = chain_forward(transform[0], transform[1], transform[2])
        mixed, tokens_one = jax.vjp(
            lambda k_in, v_in, d_in, f_in, n_in, z_in: wkv_tokens(
                k_in, v_in, d_in, f_in, n_in, z_in, starts
            ),
            key_proj,
            value_proj,
            decay[level],
            first[level],
            numer_in,
            denom_in,
        )
        gated, gate_one = jax.vjp(lambda g_in, m_in: jax.nn.sigmoid(g_in) * m_in, logit, mixed)
        gated_low = gated.astype(jnp.bfloat16)
        middle = stream + product(gated_low, w_out)
        hidden_two, norm_two = jax.vjp(normalize, middle, ln_gain[level, 1], ln_bias[level, 1])
        edge_two = edge_of(hidden_two)
        blends_two, blend_two = jax.vjp(
            lambda h_in, e_in, r_in: blend(h_in, e_in, r_in, starts),
            hidden_two,
            edge_two,
            mix[level, 3:],
        )
        xk2_low, xr2_low = [b.astype(jnp.bfloat16) for b in blends_two]
        key_two = product(xk2_low, w_fkey)
        squared, square_one = jax.vjp(lambda k_in: jnp.square(jax.nn.relu(k_in)), key_two)
        squared_low = squared.astype(jnp.bfloat16)
        value_two = product(squared_low, w_fval)
        recept = product(xr2_low, w_frec)
        branch, branch_one = jax.vjp(
            lambda r_in, v_in: jax.nn.sigmoid(r_in) * v_in, recept, value_two
        )
        record = (
            norm_one,
            blend_one,
            xk_low,
            xv_low,
            xr_low,
            transform[0],
            numer_in,
            denom_in,
            transform_one,
            tokens_one,
            gate_one,
            gated_low,
            norm_two,
            blend_two,
            xk2_low,
            xr2_low,
            square_one,
            squared_low,
            branch_one,
        )
        return (middle + branch, record)

    gathered = []
    for level in range(layer_total):
        gathered.append(
            (
                lax.all_gather(att_kvr[level], "dp", axis=0, tiled=True),
                lax.all_gather(att_out[level], "dp", axis=0, tiled=True),
                lax.all_gather(ffn_key[level], "dp", axis=0, tiled=True),
                lax.all_gather(ffn_recept[level], "dp", axis=0, tiled=True),
                lax.all_gather(ffn_value[level], "dp", axis=0, tiled=True),
            )
        )
    pair_lists = [[] for level in range(layer_total)]
    vector_sums = [None] * layer_total
    outputs = []
    grad_parts = []
    for batch in range(batches):
        low_row = batch * per_batch
        starts = starts_all[low_row : low_row + per_batch]
        stream = tokens[low_row : low_row + per_batch].astype(jnp.float32)
        records = []
        for level in range(layer_total):
            stream, record = forward_layer(stream, level, gathered[level], starts)
            records.append(record)
        outputs.append(stream.astype(jnp.bfloat16))
        gradient = cotangent[low_row : low_row + per_batch].astype(jnp.float32)
        for level in reversed(range(layer_total)):
            backward_w_kvr, backward_w_out, backward_w_fkey, backward_w_frec, backward_w_fval = (
                gathered[level]
            )
            (
                backward_norm_one,
                backward_blend_one,
                backward_xk_low,
                backward_xv_low,
                backward_xr_low,
                backward_through,
                backward_numer_in,
                backward_denom_in,
                backward_transform_one,
                backward_tokens_one,
                backward_gate_one,
                backward_gated_low,
                backward_norm_two,
                backward_blend_two,
                backward_xk2_low,
                backward_xr2_low,
                backward_square_one,
                backward_squared_low,
                backward_branch_one,
            ) = records[level]
            d_recept, d_value_two = backward_branch_one(gradient)
            g_value_two = d_value_two.astype(jnp.bfloat16)
            g_recept = d_recept.astype(jnp.bfloat16)
            (d_key_two,) = backward_square_one(product_back(g_value_two, backward_w_fval))
            g_key_two = d_key_two.astype(jnp.bfloat16)
            d_hidden_two, d_edge_two, d_rates_two = backward_blend_two(
                (product_back(g_key_two, backward_w_fkey), product_back(g_recept, backward_w_frec))
            )
            d_hidden_two = d_hidden_two.at[:, -1, :].add(edge_back(d_edge_two))
            d_middle_norm, d_gain_two, d_bias_two = backward_norm_two(d_hidden_two)
            d_middle = gradient + d_middle_norm
            g_att = d_middle.astype(jnp.bfloat16)
            d_logit, d_mixed = backward_gate_one(product_back(g_att, backward_w_out))
            g_logit = d_logit.astype(jnp.bfloat16)
            (
                d_key_one,
                d_value_one,
                d_decay_one,
                d_first,
                backward_direct_numer,
                backward_direct_denom,
            ) = backward_tokens_one(d_mixed)
            chain_incoming = (empty, empty)
            chain_sent_numer = backward_direct_numer
            chain_sent_denom = backward_direct_denom
            for chain_relay_turn in range(lax.axis_size("seq") - 1):
                chain_incoming = from_behind((chain_sent_numer, chain_sent_denom), "seq", -1)
                chain_sent_numer = backward_through * chain_incoming[0] + backward_direct_numer
                chain_sent_denom = backward_through * chain_incoming[1] + backward_direct_denom
            g_numer_out, g_denom_out = chain_incoming
            d_key_two_part, d_value_two_part, d_decay_two = backward_transform_one(
                (
                    g_numer_out * backward_numer_in + g_denom_out * backward_denom_in,
                    g_numer_out,
                    g_denom_out,
                )
            )
            g_key = (d_key_one + d_key_two_part).astype(jnp.bfloat16)
            g_value = (d_value_one + d_value_two_part).astype(jnp.bfloat16)
            d_blends = (
                product_back(g_key, backward_w_kvr[:, :width]),
                product_back(g_value, backward_w_kvr[:, width : 2 * width]),
                product_back(g_logit, backward_w_kvr[:, 2 * width :]),
            )
            d_hidden, d_edge, d_rates = backward_blend_one(d_blends)
            d_hidden = d_hidden.at[:, -1, :].add(edge_back(d_edge))
            d_stream_norm, d_gain_one, d_bias_one = backward_norm_one(d_hidden)
            pairs = (
                (backward_xk2_low, g_key_two),
                (backward_xr2_low, g_recept),
                (backward_squared_low, g_value_two),
                (backward_xk_low, g_key),
                (backward_xv_low, g_value),
                (backward_xr_low, g_logit),
                (backward_gated_low, g_att),
            )
            columns = (
                [d_decay_one + d_decay_two, d_first]
                + [d_rates[j] for j in range(3)]
                + [d_rates_two[j] for j in range(2)]
                + [d_gain_one, d_gain_two, d_bias_one, d_bias_two]
            )
            backward_vectors = jnp.stack(columns, axis=1)
            gradient, pairs, vectors = (d_middle + d_stream_norm, pairs, backward_vectors)
            pair_lists[level].append(pairs)
            vector_sums[level] = (
                vectors if vector_sums[level] is None else vector_sums[level] + vectors
            )
        grad_parts.append(gradient.astype(jnp.bfloat16))
    results = [None] * layer_total
    for level in reversed(range(layer_total)):
        pair_list = pair_lists[level]

        def summed(index):
            inputs = jnp.concatenate([p[index][0] for p in pair_list], axis=0)
            grads = jnp.concatenate([p[index][1] for p in pair_list], axis=0)
            return outer_sum(inputs, grads)

        ffn_part = (summed(0), summed(1), summed(2))
        finish_grad_kvr = jnp.concatenate([summed(3), summed(4), summed(5)], axis=1)
        totals = (
            lax.psum(
                lax.psum_scatter(ffn_part[0], "dp", scatter_dimension=0, tiled=True).astype(
                    jnp.bfloat16
                ),
                "seq",
            ).astype(jnp.float32),
            lax.psum(
                lax.psum_scatter(ffn_part[1], "dp", scatter_dimension=0, tiled=True).astype(
                    jnp.bfloat16
                ),
                "seq",
            ).astype(jnp.float32),
            lax.psum(
                lax.psum_scatter(ffn_part[2], "dp", scatter_dimension=0, tiled=True).astype(
                    jnp.bfloat16
                ),
                "seq",
            ).astype(jnp.float32),
            lax.psum(
                lax.psum_scatter(finish_grad_kvr, "dp", scatter_dimension=0, tiled=True).astype(
                    jnp.bfloat16
                ),
                "seq",
            ).astype(jnp.float32),
            lax.psum(
                lax.psum_scatter(summed(6), "dp", scatter_dimension=0, tiled=True).astype(
                    jnp.bfloat16
                ),
                "seq",
            ).astype(jnp.float32),
            lax.psum(
                lax.psum_scatter(vector_sums[level], "dp", scatter_dimension=0, tiled=True).astype(
                    jnp.bfloat16
                ),
                "seq",
            ).astype(jnp.float32),
        )
        ffn_part = (totals[0], totals[1], totals[2])
        att_part = (totals[3], totals[4], totals[5])
        results[level] = (ffn_part, att_part)
    output = jnp.concatenate(outputs, axis=0)
    grad_tokens = jnp.concatenate(grad_parts, axis=0)
    grad_ffn_key = jnp.stack([r[0][0] for r in results])
    grad_ffn_recept = jnp.stack([r[0][1] for r in results])
    grad_ffn_value = jnp.stack([r[0][2] for r in results])
    grad_kvr = jnp.stack([r[1][0] for r in results])
    grad_att_out = jnp.stack([r[1][1] for r in results])
    vector_rows = jnp.stack([r[1][2] for r in results])
    grad_decay = vector_rows[:, :, 0]
    grad_first = vector_rows[:, :, 1]
    grad_mix = jnp.swapaxes(vector_rows[:, :, 2:7], 1, 2)
    grad_gain = jnp.swapaxes(vector_rows[:, :, 7:9], 1, 2)
    grad_bias = jnp.swapaxes(vector_rows[:, :, 9:11], 1, 2)
    return (
        output,
        grad_tokens,
        grad_decay,
        grad_first,
        grad_mix,
        grad_gain,
        grad_bias,
        grad_kvr,
        grad_att_out,
        grad_ffn_key,
        grad_ffn_recept,
        grad_ffn_value,
    )


def solution(mesh):
    in_specs = (
        P("dp", "seq", None),
        P("dp", None),
        P(),
        P(),
        P(),
        P(),
        P(),
        P(None, "dp", None),
        P(None, "dp", None),
        P(None, "dp", None),
        P(None, "dp", None),
        P(None, "dp", None),
        P("dp", "seq", None),
    )
    out_specs = (
        P("dp", "seq", None),
        P("dp", "seq", None),
        P(None, "dp"),
        P(None, "dp"),
        P(None, None, "dp"),
        P(None, None, "dp"),
        P(None, None, "dp"),
        P(None, "dp", None),
        P(None, "dp", None),
        P(None, "dp", None),
        P(None, "dp", None),
        P(None, "dp", None),
    )
    return jax.shard_map(body, mesh=mesh, in_specs=in_specs, out_specs=out_specs, check_vma=False)
```
